128 devices in a mesh: colat: 16 (over x_lo, y, core), depth: 8 (over x_hi, z).
Axes of the slice: x: 4 (x_hi: 2, x_lo: 2; x = x_hi * 2 + x_lo), y: 4, z: 4, core: 2. Of those that a mesh axis runs over, the one named last changes fastest.
Arguments:
- displacement: float32 [3, 64, 32, 2048], P(None, 'colat', 'depth'), may hold values from -6 to 6
- previous: float32 [3, 64, 32, 2048], P(None, 'colat', 'depth'), may hold values from -6 to 6
- node_blocks: int32 [64, 32], P('colat', 'depth'), may hold values from 1 to 8
- inverse_mass: float32 [64, 32], P('colat', 'depth'), may hold values from 0.0008 to 0.003
- jacobian_diag: float32 [2, 16, 5, 8, 5], P(None, 'colat', None, 'depth'), may hold values from 0.6 to 1.5
- jacobian_off: float32 [2, 16, 5, 8, 5], P(None, 'colat', None, 'depth'), may hold values from -0.25 to 0.25
- inverse_radius: float32 [16, 5, 8, 5], P('colat', None, 'depth'), may hold values from 2 to 6
- lame_lambda: float32 [16, 5, 8, 5, 2048], P('colat', None, 'depth'), may hold values from 0.3 to 1
- lame_mu: float32 [16, 5, 8, 5, 2048], P('colat', None, 'depth'), may hold values from 0.3 to 1
Outputs:
- displacement_mid: float32 [3, 64, 32, 2048], P(None, 'colat', 'depth')
- displacement_final: float32 [3, 64, 32, 2048], P(None, 'colat', 'depth')
The draws below stay inside these ranges and needn't reach their ends.
All inputs are finite; a program needn't handle non-finite values.
Results may differ from the reference program's by a relative error of at most 0.0014.
Values may be sent and summed in bfloat16 or wider, within the bound.
No kernel may reach another device: no remote copies, remote signals or barrier semaphores. Data moves between devices by JAX's collectives and lax.ppermute only.
A program may use at most 64 MiB of HBM per device.

```python
import math
import jax
import jax.numpy as jnp
import numpy as np
from jax import lax

ORDERS = 1024
BLOCK = 128
STEPS = 2
NB = 8
SAMPLES = 2048
ECOL = 16
EDEP = 8
NCOL = 64
NDEP = 32


def draw_node_blocks(key, part):
    key_band = jax.random.fold_in(key, 11)
    key_layer = jax.random.fold_in(key, 12)
    key_jitter = jax.random.fold_in(key, 13)
    key_slot = jax.random.fold_in(key, 14)
    band_level = jax.random.randint(key_band, (ECOL,), 0, NB // 2 + 1)
    layer_level = jax.random.randint(key_layer, (EDEP,), 0, (NB + 1) // 2)
    jitter = jax.random.randint(key_jitter, (ECOL, EDEP), 0, 2)
    element_blocks = jnp.clip(band_level[:, None] + layer_level[None, :] + jitter, 1, NB)
    total = ECOL * EDEP
    high_slot = jax.random.randint(key_slot, (), 0, total)
    low_slot = (high_slot + total // 2) % total
    flattened = element_blocks.reshape(-1).at[high_slot].set(NB).at[low_slot].set(1)
    element_blocks = flattened.reshape(ECOL, EDEP)
    node_rows = jnp.arange(NCOL, dtype=jnp.int32)
    node_cols = jnp.arange(NDEP, dtype=jnp.int32)
    upper_row = node_rows // 4
    lower_row = jnp.maximum(node_rows - 1, 0) // 4
    upper_col = node_cols // 4
    lower_col = jnp.maximum(node_cols - 1, 0) // 4
    upper_part = jnp.take(element_blocks, upper_row, axis=0)
    lower_part = jnp.take(element_blocks, lower_row, axis=0)
    first_max = jnp.maximum(jnp.take(upper_part, upper_col, axis=1), jnp.take(upper_part, lower_col, axis=1))
    second_max = jnp.maximum(jnp.take(lower_part, upper_col, axis=1), jnp.take(lower_part, lower_col, axis=1))
    return jnp.maximum(first_max, second_max).astype(jnp.int32)


def levels(own_key, dims, pieces, low, top_value):
    factor_of, own = 1.0, jax.random.fold_in(own_key, 6)
    for dim, blocks in pieces:
        steps = jnp.exp(jax.random.uniform(jax.random.fold_in(own, dim), (blocks,), jnp.float32, low / len(pieces), top_value / len(pieces)))
        factor_of = factor_of * jnp.repeat(steps, dims[dim] // blocks).reshape([-1 if axis == dim else 1 for axis in range(len(dims))])
    return factor_of


def gaussian(own_key, shape, width, bound, shards=(), held_as=jnp.bfloat16):
    drawn = width * jax.random.normal(own_key, shape, jnp.float32)
    if shards:
        drawn = drawn * levels(own_key, shape, shards, -0.22, 0.18)
    return jnp.clip(drawn, -bound, bound).astype(held_as)


def setup_inputs(seed: int = 0) -> dict:
    key_of = jax.random.split(jax.random.key(seed), 10)
    displacement = gaussian(key_of[0], (3, NCOL, NDEP, 2 * ORDERS), 1.0, 6.0, ((1, 16), (2, 8)), jnp.float32)
    previous = gaussian(key_of[1], (3, NCOL, NDEP, 2 * ORDERS), 1.0, 6.0, ((1, 16), (2, 8)), jnp.float32)
    node_blocks = draw_node_blocks(jax.random.fold_in(key_of[9], 71), 0)
    inverse_mass = jnp.clip(jnp.exp(math.log(0.003) - 1.3217559 * jax.random.uniform(key_of[3], (NCOL, NDEP), jnp.float32) ** levels(key_of[3], (NCOL, NDEP), ((0, 16), (1, 8)), -0.2, 0.2)), 0.0008, 0.003)
    jacobian_diag = jnp.clip(jnp.exp(math.log(1.5) - 0.9162907 * jax.random.uniform(key_of[4], (2, ECOL, 5, EDEP, 5), jnp.float32) ** levels(key_of[4], (2, ECOL, 5, EDEP, 5), ((1, 16), (3, 8)), -0.2, 0.2)), 0.6, 1.5)
    jacobian_off = jnp.clip(jax.random.uniform(key_of[5], (2, ECOL, 5, EDEP, 5), jnp.float32, -0.25, 0.25) * levels(key_of[5], (2, ECOL, 5, EDEP, 5), ((1, 16), (3, 8)), -0.4, 0.0), -0.25, 0.25)
    inverse_radius = jnp.clip(jnp.exp(math.log(6.0) - 1.0986123 * jax.random.uniform(key_of[6], (ECOL, 5, EDEP, 5), jnp.float32) ** levels(key_of[6], (ECOL, 5, EDEP, 5), ((0, 16), (2, 8)), -0.2, 0.2)), 2.0, 6.0)
    lame_lambda = jnp.clip(jnp.exp(math.log(1.0) - 1.2039728 * jax.random.uniform(key_of[7], (ECOL, 5, EDEP, 5, SAMPLES), jnp.float32) ** levels(key_of[7], (ECOL, 5, EDEP, 5, SAMPLES), ((0, 16), (2, 8)), -0.2, 0.2)), 0.3, 1.0)
    lame_mu = jnp.clip(jnp.exp(math.log(1.0) - 1.2039728 * jax.random.uniform(key_of[8], (ECOL, 5, EDEP, 5, SAMPLES), jnp.float32) ** levels(key_of[8], (ECOL, 5, EDEP, 5, SAMPLES), ((0, 16), (2, 8)), -0.2, 0.2)), 0.3, 1.0)
    return dict(displacement=displacement, previous=previous, node_blocks=node_blocks, inverse_mass=inverse_mass, jacobian_diag=jacobian_diag, jacobian_off=jacobian_off, inverse_radius=inverse_radius, lame_lambda=lame_lambda, lame_mu=lame_mu)


def gll_derivative():
    points = np.array([-1.0, -math.sqrt(3.0 / 7.0), 0.0, math.sqrt(3.0 / 7.0), 1.0])
    weights = np.ones(5)
    for row_index in range(5):
        for col_index in range(5):
            if row_index != col_index:
                weights[row_index] = weights[row_index] / (points[row_index] - points[col_index])
    deriv_matrix = np.zeros((5, 5))
    for row_index in range(5):
        for col_index in range(5):
            if row_index != col_index:
                deriv_matrix[row_index, col_index] = weights[col_index] / weights[row_index] / (points[row_index] - points[col_index])
        deriv_matrix[row_index, row_index] = -np.sum(deriv_matrix[row_index])
    return jnp.asarray(deriv_matrix, dtype=jnp.float32)

def basis_table(coef_width, sample_count):
    coef_index = np.arange(coef_width, dtype=np.int64)
    block_index = coef_index // (2 * BLOCK)
    order_index = block_index * BLOCK + coef_index % BLOCK
    real_rows = (coef_index // BLOCK % 2 == 0)[:, None]
    sample_index = np.arange(sample_count, dtype=np.int64)
    phase_index = order_index[:, None] * sample_index[None, :] % sample_count
    angles = phase_index.astype(np.float32) * np.float32(2.0 * math.pi / sample_count)
    cosine = np.cos(angles).astype(np.float32)
    sine = np.sin(angles).astype(np.float32)
    order_float = order_index.astype(np.float32)[:, None]
    value_cols = np.where(real_rows, cosine, -sine)
    deriv_cols = np.where(real_rows, -order_float * sine, -order_float * cosine)
    table_np = np.concatenate([value_cols, deriv_cols], axis=1).astype(np.float32)
    return jnp.asarray(table_np, dtype=jnp.bfloat16)

def unfold_nodes(source, which_axis):
    elements = (source.shape[which_axis] - 1) // 4
    strided = [lax.slice_in_dim(source, offset, offset + 4 * (elements - 1) + 1, 4, which_axis) for offset in range(5)]
    return jnp.stack(strided, axis=which_axis + 1)

def fold_nodes(source, which_axis):
    moved = jnp.moveaxis(source, (which_axis, which_axis + 1), (0, 1))
    elements = moved.shape[0]
    trailing = moved.shape[2:]
    main_rows = moved[:, 0:4].reshape((4 * elements,) + trailing)
    carried = jnp.concatenate([moved[:, 4:5], jnp.zeros((elements, 3) + trailing, moved.dtype)], axis=1).reshape((4 * elements,) + trailing)
    shifted = jnp.concatenate([jnp.zeros((4,) + trailing, moved.dtype), carried], axis=0)[:4 * elements + 1]
    summed = jnp.concatenate([main_rows, jnp.zeros((1,) + trailing, moved.dtype)], axis=0) + shifted
    return jnp.moveaxis(summed, 0, which_axis)

def element_load(element_view, jac_diag, jac_off, inverse_radius, lame_lambda, lame_mu):
    half_width = element_view.shape[-1] // 2
    field_vals = element_view[..., :half_width]
    field_dphi = element_view[..., half_width:]
    deriv_matrix = gll_derivative()
    diag_one = jac_diag[0][..., None]
    diag_two = jac_diag[1][..., None]
    off_one = jac_off[0][..., None]
    off_two = jac_off[1][..., None]
    radius_inv = inverse_radius[..., None] * jnp.float32(2.0 / half_width)

    def strains(values, dphi):
        grad_xi = jnp.einsum('ia,cpaqbk->cpiqbk', deriv_matrix, values, precision=lax.Precision.HIGHEST)
        grad_eta = jnp.einsum('jb,cpaqbk->cpaqjk', deriv_matrix, values, precision=lax.Precision.HIGHEST)
        grad_s = diag_one * grad_xi + off_one * grad_eta
        grad_z = off_two * grad_xi + diag_two * grad_eta
        strain_ss = grad_s[0]
        strain_zz = grad_z[2]
        strain_pp = radius_inv * (dphi[1] + values[0])
        strain_sz = 0.5 * (grad_z[0] + grad_s[2])
        strain_sp = 0.5 * (radius_inv * (dphi[0] - values[1]) + grad_s[1])
        strain_zp = 0.5 * (radius_inv * dphi[2] + grad_z[1])
        return jnp.stack([strain_ss, strain_zz, strain_pp, strain_sz, strain_sp, strain_zp])
    strain, pullback = jax.vjp(strains, field_vals, field_dphi)
    trace_sum = strain[0] + strain[1] + strain[2]
    cotangent = jnp.stack([lame_lambda * trace_sum + 2.0 * lame_mu * strain[0], lame_lambda * trace_sum + 2.0 * lame_mu * strain[1], lame_lambda * trace_sum + 2.0 * lame_mu * strain[2], 4.0 * lame_mu * strain[3], 4.0 * lame_mu * strain[4], 4.0 * lame_mu * strain[5]])
    load_vals, load_dphi = pullback(cotangent)
    return jnp.concatenate([load_vals, load_dphi], axis=-1)

def from_samples(node_load, table_bf):
    flattened = node_load.reshape(-1, node_load.shape[-1])
    result = lax.dot_general(flattened, table_bf, (((1,), (1,)), ((), ())), preferred_element_type=jnp.float32)
    return result.reshape(node_load.shape[:-1] + (table_bf.shape[0],))

def reference(displacement, previous, node_blocks, inverse_mass, jacobian_diag, jacobian_off, inverse_radius, lame_lambda, lame_mu):
    coef_width = 2 * ORDERS
    table_bf = basis_table(coef_width, SAMPLES)
    block_of = jnp.arange(coef_width, dtype=jnp.int32) // (2 * BLOCK)
    live_mask = block_of[None, None, :] < node_blocks[:, :, None]
    diag_bands = jnp.moveaxis(jacobian_diag, 1, 0)
    off_bands = jnp.moveaxis(jacobian_off, 1, 0)

    def forces(current):
        live = jnp.where(live_mask, current, 0.0).astype(jnp.bfloat16)
        widened = jnp.pad(live, ((0, 0), (0, 1), (0, 1), (0, 0)))

        def band_force(band_items):
            band_index, diag_band, off_band, radius_band, lambda_band, mu_band = band_items
            node_rows = lax.dynamic_slice_in_dim(widened, band_index * 4, 5, axis=1)
            samples = jnp.dot(node_rows.reshape(-1, coef_width), table_bf, preferred_element_type=jnp.float32)
            samples = samples.reshape((3, 5, NDEP + 1, 2 * SAMPLES))
            element_view = unfold_nodes(samples, 2)[:, None]
            node_load = element_load(element_view, diag_band[:, None], off_band[:, None], radius_band[None], lambda_band[None], mu_band[None])
            element_force = from_samples(node_load.astype(jnp.bfloat16), table_bf) * jnp.float32(-1.0 / SAMPLES)
            return fold_nodes(element_force[:, 0], 2)
        band_items = (jnp.arange(ECOL, dtype=jnp.int32), diag_bands, off_bands, inverse_radius, lame_lambda, lame_mu)
        bands = lax.map(band_force, band_items)
        bands = jnp.moveaxis(bands, 0, 1)
        assembled = fold_nodes(bands, 1)
        return assembled[:, :NCOL, :NDEP]
    current = displacement
    before = previous
    results = []
    for step_index in range(STEPS):
        assembled = forces(current)
        advanced = jnp.where(live_mask, 2.0 * current - before + inverse_mass[None, :, :, None] * assembled, 0.0)
        before = current
        current = advanced
        results.append(current)
    return (results[0], current)
```

```python
import functools
import math

import jax
import jax.numpy as jnp
import ml_dtypes
import numpy as np
from jax import lax
from jax.experimental import pallas as pl
from jax.experimental.pallas import tpu as pltpu
from jax.sharding import PartitionSpec as P

BF16 = jnp.bfloat16
F32 = jnp.float32
WIDTH = 2048
LANES = 128
RADIX = 16
OWN = 48
NODES = 80
STRAINS = 152
VMEM_LIMIT = 40 * 1024 * 1024


def gll_derivative():
    points = np.array([-1.0, -math.sqrt(3.0 / 7.0), 0.0, math.sqrt(3.0 / 7.0), 1.0])
    weights = np.ones(5)
    for row in range(5):
        for col in range(5):
            if row != col:
                weights[row] /= points[row] - points[col]
    matrix = np.zeros((5, 5))
    for row in range(5):
        for col in range(5):
            if row != col:
                matrix[row, col] = weights[col] / weights[row] / (points[row] - points[col])
        matrix[row, row] = -np.sum(matrix[row])
    return matrix


def node_row(comp, i, j):
    if i == 4:
        return OWN + (12 + comp if j == 4 else 4 * comp + j)
    if j == 4:
        return OWN + 16 + 4 * comp + i
    return 16 * comp + 4 * i + j


def strain_row(strain, node):
    return 24 * strain + node if node < 24 else 144 + strain


def strain_terms():
    deriv = gll_derivative()
    parts = np.zeros((5, STRAINS, 2 * NODES))
    node_of = np.zeros((STRAINS, 25))
    half = math.sqrt(0.5)
    for i in range(5):
        for j in range(5):
            node = 5 * i + j

            def grad(strain, along_z, comp, scale):
                row = strain_row(strain, node)
                for other in range(5):
                    xi, eta = (2, 3) if along_z else (0, 1)
                    parts[xi, row, node_row(comp, other, j)] += scale * deriv[i, other]
                    parts[eta, row, node_row(comp, i, other)] += scale * deriv[j, other]

            def radial(strain, comp, azimuthal, scale):
                row = strain_row(strain, node)
                parts[4, row, NODES * azimuthal + node_row(comp, i, j)] += scale / 1024.0

            grad(0, False, 0, 1.0)
            grad(1, True, 2, 1.0)
            radial(2, 1, 1, 1.0)
            radial(2, 0, 0, 1.0)
            grad(3, True, 0, half)
            grad(3, False, 2, half)
            radial(4, 0, 1, half)
            radial(4, 1, 0, -half)
            grad(4, False, 1, half)
            radial(5, 2, 1, half)
            grad(5, True, 1, half)
            for strain in range(6):
                node_of[strain_row(strain, node), node] = 1.0
    parts[:, 150] = parts[:, 144] + parts[:, 145] + parts[:, 146]
    node_of[150, 24] = 1.0
    return parts.astype(np.float32), node_of.astype(np.float32)


def sample_tables():
    order = np.arange(LANES)[:, None]
    table = np.zeros((RADIX, 2 * LANES, LANES))
    for k0 in range(RADIX):
        angle = 2.0 * math.pi * (order * (16 * np.arange(LANES)[None, :] + k0) % WIDTH) / WIDTH
        table[k0, :LANES] = np.cos(angle)
        table[k0, LANES:] = -np.sin(angle)
    return (
        table.astype(ml_dtypes.bfloat16),
        np.ascontiguousarray(table.transpose(0, 2, 1)).astype(ml_dtypes.bfloat16),
    )


def lane_shuffle():
    shuffle = np.zeros((LANES, LANES))
    for t in range(8):
        for k0 in range(16):
            shuffle[16 * t + k0, 8 * k0 + t] = 1.0
    return shuffle.astype(ml_dtypes.bfloat16)


def face(fixed_i, fixed_j):
    return [(fixed_i, n) if fixed_j is None else (n, fixed_j) for n in range(5)]


def message_row(comp, n):
    return 12 + comp if n == 4 else 4 * comp + n


def first_halo_select():
    select = np.zeros((48, OWN))
    for comp in range(3):
        for n in range(4):
            select[4 * comp + n, node_row(comp, 0, n)] = 1.0
            select[16 + 4 * comp + n, node_row(comp, n, 0)] = 1.0
        select[32 + 12 + comp, node_row(comp, 0, 0)] = 1.0
    return select.astype(ml_dtypes.bfloat16)


def pick(faces):
    select = np.zeros((16 * len(faces), NODES))
    for index, nodes in enumerate(faces):
        for comp in range(3):
            for n, (i, j) in enumerate(nodes):
                select[16 * index + message_row(comp, n), node_row(comp, i, j)] = 1.0
    return select


ROW_LOW, ROW_HIGH = face(0, None), face(4, None)
COL_LOW, COL_HIGH = face(None, 0), face(None, 4)


def outgoing_select():
    even = pick([ROW_HIGH, ROW_LOW, COL_HIGH, COL_LOW])
    odd = pick([ROW_LOW, ROW_HIGH, COL_HIGH, COL_LOW])
    return np.stack([even, odd]).astype(ml_dtypes.bfloat16)


def column_select():
    out = np.zeros((4, 32, 64))
    for par_c in range(2):
        faces = [ROW_HIGH, ROW_LOW] if par_c == 0 else [ROW_LOW, ROW_HIGH]
        arrive = pick(faces).T
        full = np.concatenate([pick([COL_HIGH]), pick([COL_LOW])], axis=0)
        whole = np.concatenate([np.eye(32), full @ arrive], axis=1)
        for par_d in range(2):
            out[2 * par_c + par_d] = whole if par_d == 0 else np.roll(whole, 16, axis=0)
    return out.astype(ml_dtypes.bfloat16)


def arrival_select():
    out = np.zeros((4, NODES, 64))
    for par_c in range(2):
        rows = [ROW_HIGH, ROW_LOW] if par_c == 0 else [ROW_LOW, ROW_HIGH]
        for par_d in range(2):
            cols = [COL_HIGH, COL_LOW] if par_d == 0 else [COL_LOW, COL_HIGH]
            out[2 * par_c + par_d] = pick(rows + cols).T
    return out.astype(ml_dtypes.bfloat16)


def last_select():
    select = np.zeros((OWN, 48))
    for comp in range(3):
        for n in range(4):
            select[node_row(comp, 0, n), 4 * comp + n] = 1.0
            select[node_row(comp, n, 0), 16 + 4 * comp + n] = 1.0
        select[node_row(comp, 0, 0), 32 + 12 + comp] = 1.0
    return select.astype(ml_dtypes.bfloat16)


def turned(value, eighths, scale_sign):
    re, im = value
    eighths = (scale_sign * eighths) % 16
    if eighths == 0:
        return re, im
    if eighths == 4:
        return -im, re
    if eighths == 8:
        return -re, -im
    if eighths == 12:
        return im, -re
    root = math.sqrt(0.5)
    if eighths == 2:
        return (re - im) * root, (im + re) * root
    if eighths == 14:
        return (re + im) * root, (im - re) * root
    cosine = math.cos(2.0 * math.pi * eighths / 16)
    sine = math.sin(2.0 * math.pi * eighths / 16)
    return re * cosine - im * sine, im * cosine + re * sine


def add(left, right):
    return left[0] + right[0], left[1] + right[1]


def sub(left, right):
    return left[0] - right[0], left[1] - right[1]


def transform(values, sign):
    count = len(values)
    if count == 1:
        return values
    even = transform(values[0::2], sign)
    odd = transform(values[1::2], sign)
    odd = [turned(value, q * (16 // count), sign) for q, value in enumerate(odd)]
    return [add(a, b) for a, b in zip(even, odd)] + [sub(a, b) for a, b in zip(even, odd)]


def spread(blocks):
    even = transform(blocks, 1)
    odd = transform([turned(value, b, 1) for b, value in enumerate(blocks)], 1)
    return [value for pair in zip(even, odd) for value in pair]


def gathered(values):
    even = transform(values[0::2], -1)
    odd = transform(values[1::2], -1)
    return [add(a, turned(b, index, -1)) for index, (a, b) in enumerate(zip(even, odd))]


def block(index, part):
    return slice(2 * LANES * index + LANES * part, 2 * LANES * index + LANES * (part + 1))


def orders(index):
    lane = lax.broadcasted_iota(jnp.int32, (1, LANES), 1)
    return (lane + LANES * index).astype(F32)


def dot(left, right):
    return jnp.dot(left, right, preferred_element_type=F32)


def first_kernel(disp_ref, meta_ref, select_ref, out_ref):
    live = meta_ref[:, 1:2]
    for index in range(8):
        lanes = slice(256 * index, 256 * (index + 1))
        value = jnp.where(live > index, disp_ref[:, lanes], 0.0).astype(BF16)
        out_ref[:, lanes] = dot(select_ref[...], value).astype(BF16)
    mass = meta_ref[:, 0:1]
    high = mass.astype(BF16).astype(F32)
    lane = lax.broadcasted_iota(jnp.int32, (OWN, LANES), 1)
    info = jnp.where(lane == 0, high, jnp.where(lane == 1, mass - high, jnp.where(lane == 2, live, 0.0)))
    out_ref[:, WIDTH:] = dot(select_ref[...], info.astype(BF16)).astype(BF16)


def material_kernel(lambda_ref, mu_ref, shuffle_ref, out_ref, work):
    for index in range(16):
        lanes = slice(LANES * index, LANES * (index + 1))
        lam, mu = lambda_ref[:, lanes], mu_ref[:, lanes] * 2.0
        row = lax.broadcasted_iota(jnp.int32, (8, LANES), 0)
        last = jnp.where(row < 6, mu[24:25], jnp.where(row == 6, lam[24:25], 0.0))
        stacked = jnp.concatenate([lam[:24], mu[:24], last], axis=0)
        high = stacked.astype(BF16)
        low = (stacked - high.astype(F32)).astype(BF16)
        shuffled = dot(high, shuffle_ref[...]) + dot(low, shuffle_ref[...])
        work[index] = shuffled if index == 0 else pltpu.roll(shuffled, 8 * index, 1)
    group = lax.broadcasted_iota(jnp.int32, (8, LANES), 1) // 8
    for rows in range(7):
        part = slice(8 * rows, 8 * rows + 8)
        held = [work[(16 - index) % 16, part] for index in range(16)]
        for bit in range(4):
            chosen = (group >> bit) % 2 == 1
            held = [jnp.where(chosen, held[(index - (1 << bit)) % 16], held[index]) for index in range(16)]
        for index in range(16):
            out_ref[index, part] = held[index] if index == 0 else pltpu.roll(held[index], LANES - 8 * index, 1)


def forces(nodes, operator_ref, back_ref, table_ref, tback_ref, material_ref, both, strain, spectrum, emit):
    for index in range(8):
        order = orders(index)
        re = nodes(block(index, 0))
        im = nodes(block(index, 1))
        both[:NODES, block(index, 0)] = re.astype(BF16)
        both[:NODES, block(index, 1)] = im.astype(BF16)
        both[NODES:, block(index, 0)] = (im * (-order)).astype(BF16)
        both[NODES:, block(index, 1)] = (re * order).astype(BF16)
        lanes = slice(256 * index, 256 * (index + 1))
        strain[:, lanes] = dot(operator_ref[...], both[:, lanes])

    @pl.loop(0, STRAINS // 8)
    def _(group):
        rows = pl.ds(pl.multiple_of(group * 8, 8), 8)
        values = [(strain[rows, block(b, 0)], strain[rows, block(b, 1)]) for b in range(8)]
        for k0, (re, im) in enumerate(spread(values)):
            spectrum[k0, rows, :LANES] = re
            spectrum[k0, rows, LANES:] = im

    for k0 in range(RADIX):
        sample = dot(spectrum[k0].astype(BF16), table_ref[k0])
        lam, mu, last = material_ref[k0, :24], material_ref[k0, 24:48], material_ref[k0, 48:]
        parts = [sample[24 * s : 24 * s + 24] for s in range(6)]
        volume = lam * (parts[0] + parts[1] + parts[2])
        stress = [volume + mu * part for part in parts[:3]] + [mu * part for part in parts[3:]]
        stress.append(last * sample[144:])
        stress = jnp.concatenate(stress, axis=0).astype(BF16)
        spectrum[k0] = dot(stress, tback_ref[k0])

    @pl.loop(0, STRAINS // 8)
    def _(group):
        rows = pl.ds(pl.multiple_of(group * 8, 8), 8)
        values = [(spectrum[k0, rows, :LANES], spectrum[k0, rows, LANES:]) for k0 in range(RADIX)]
        for b, (re, im) in enumerate(gathered(values)):
            strain[rows, block(b, 0)] = re
            strain[rows, block(b, 1)] = im

    for index in range(8):
        lanes = slice(256 * index, 256 * (index + 1))
        order = orders(index)
        pulled = dot(back_ref[...], strain[:, lanes].astype(BF16))
        re = pulled[:NODES, :LANES] + order * pulled[NODES:, LANES:]
        im = pulled[:NODES, LANES:] - order * pulled[NODES:, :LANES]
        emit(index, re, im)


def step_one_kernel(
    place, disp_ref, prev_ref, meta_ref, row_ref, col_ref, corner_ref,
    operator_ref, back_ref, table_ref, tback_ref, material_ref, select_ref,
    sum_ref, pair_ref, side_ref, faces_ref,
    tiles, both, strain, spectrum,
):
    rest_c, rest_d = place[2].astype(F32), place[3].astype(F32)
    tiles[:16] = row_ref[...].astype(F32) * rest_c + corner_ref[...].astype(F32) * (rest_c * rest_d)
    tiles[16:] = col_ref[...].astype(F32) * rest_d
    info = tiles[:, WIDTH:]
    lane = lax.broadcasted_iota(jnp.int32, (32, LANES), 1)
    halo_info = jnp.where(lane == 0, info[:, 0:1] + info[:, 1:2], jnp.where(lane == 1, info[:, 2:3], 0.0))
    sum_ref[:OWN, WIDTH:] = meta_ref[...]
    sum_ref[OWN:, WIDTH:] = halo_info
    live = meta_ref[:, 1:2]

    def nodes(lanes):
        own = jnp.where(live > lanes.start // 256, disp_ref[:, lanes], 0.0)
        return jnp.concatenate([own, tiles[:, lanes]], axis=0)

    mass = sum_ref[:, WIDTH : WIDTH + 1] * (-1.0 / WIDTH)

    def emit(index, re, im):
        for part, value in ((0, re), (1, im)):
            lanes = block(index, part)
            value = mass * value
            total = 2.0 * disp_ref[:, lanes] - prev_ref[:, lanes] + value[:OWN]
            total = jnp.concatenate([total, value[OWN:]], axis=0)
            sum_ref[:, lanes] = total
            sent = dot(select_ref[place[0]], total.astype(BF16)).astype(BF16)
            pair_ref[:, lanes] = sent[:16]
            side_ref[:, lanes] = sent[16:32]
            faces_ref[:, lanes] = sent[32:]

    forces(nodes, operator_ref, back_ref, table_ref, tback_ref, material_ref, both, strain, spectrum, emit)


def column_kernel(place, faces_ref, pair_ref, side_ref, select_ref, pair_out, side_out):
    select = select_ref[2 * place[0] + place[1]]
    for index in range(8):
        lanes = slice(256 * index, 256 * (index + 1))
        stacked = jnp.concatenate([faces_ref[:, lanes], pair_ref[:, lanes], side_ref[:, lanes]], axis=0)
        sent = dot(select, stacked).astype(BF16)
        pair_out[:, lanes] = sent[:16]
        side_out[:, lanes] = sent[16:]


def step_two_kernel(
    place, disp_ref, sum_ref, cpair_ref, cside_ref, dpair_ref, dside_ref,
    operator_ref, back_ref, table_ref, tback_ref, material_ref, select_ref,
    mid_ref, sum_out, row_out, col_out,
    current, both, strain, spectrum,
):
    select = select_ref[2 * place[0] + place[1]]
    live = sum_ref[:, WIDTH + 1 : WIDTH + 2]
    for index in range(8):
        lanes = slice(256 * index, 256 * (index + 1))
        arrived = jnp.concatenate([ref[:, lanes] for ref in (cpair_ref, cside_ref, dpair_ref, dside_ref)], axis=0)
        value = jnp.where(live > index, sum_ref[:, lanes] + dot(select, arrived), 0.0)
        current[:, lanes] = value
        mid_ref[:, lanes] = value[:OWN]
    mass = sum_ref[:, WIDTH : WIDTH + 1] * (-1.0 / WIDTH)

    def emit(index, re, im):
        for part, value in ((0, re), (1, im)):
            lanes = block(index, part)
            value = mass * value
            sum_out[:, lanes] = 2.0 * current[:OWN, lanes] - disp_ref[:, lanes] + value[:OWN]
            row_out[:, lanes] = value[OWN : OWN + 16].astype(BF16)
            col_out[:, lanes] = value[OWN + 16 :].astype(BF16)

    forces(
        lambda lanes: current[:, lanes],
        operator_ref, back_ref, table_ref, tback_ref, material_ref, both, strain, spectrum, emit,
    )


def last_kernel(sum_ref, meta_ref, row_ref, col_ref, corner_ref, select_ref, out_ref):
    live = meta_ref[:, 1:2]
    for index in range(8):
        lanes = slice(256 * index, 256 * (index + 1))
        arrived = jnp.concatenate([row_ref[:, lanes], col_ref[:, lanes], corner_ref[:, lanes]], axis=0)
        value = sum_ref[:, lanes] + dot(select_ref[...], arrived)
        out_ref[:, lanes] = jnp.where(live > index, value, 0.0)


def call(kernel, outs, scratch=(), scalars=False, inputs=0, flops=0):
    vmem = pl.BlockSpec(memory_space=pltpu.VMEM)
    specs = [vmem] * inputs
    if scalars:
        specs = [pl.BlockSpec(memory_space=pltpu.SMEM)] + specs
    return pl.pallas_call(
        kernel,
        out_shape=outs,
        in_specs=specs,
        out_specs=jax.tree.map(lambda _: vmem, outs),
        scratch_shapes=list(scratch),
        compiler_params=pltpu.CompilerParams(vmem_limit_bytes=VMEM_LIMIT),
        cost_estimate=pl.CostEstimate(flops=flops, bytes_accessed=1 << 20, transcendentals=0),
    )


def shape(*dims, dtype=F32):
    return jax.ShapeDtypeStruct(dims, dtype)


def solution(mesh):
    bands, layers = mesh.shape["colat"], mesh.shape["depth"]
    parts, node_of = strain_terms()
    table, tback = sample_tables()

    def shifted(array, by_c, by_d):
        pairs = [
            (c * layers + d, (c + by_c) % bands * layers + (d + by_d) % layers)
            for c in range(bands)
            for d in range(layers)
        ]
        return lax.ppermute(array, ("colat", "depth"), pairs)

    def swapped(array, axis, odd):
        count = mesh.shape[axis]
        pairs = [(n, (n + 1) % count if n % 2 == odd else (n - 1) % count) for n in range(count)]
        return lax.ppermute(array, axis, pairs)

    def per_device(displacement, previous, node_blocks, inverse_mass, jac_diag, jac_off, inv_radius, lame_l, lame_m):
        at_c, at_d = lax.axis_index("colat"), lax.axis_index("depth")
        place = jnp.stack([at_c % 2, at_d % 2, at_c < bands - 1, at_d < layers - 1]).astype(jnp.int32)
        disp = displacement.reshape(OWN, WIDTH)
        prev = previous.reshape(OWN, WIDTH)
        lane = lax.broadcasted_iota(jnp.int32, (3, 4, 4, LANES), 3)
        meta = jnp.where(
            lane == 0,
            inverse_mass[None, :, :, None],
            jnp.where(lane == 1, node_blocks.astype(F32)[None, :, :, None], 0.0),
        ).reshape(OWN, LANES)

        halo = call(first_kernel, shape(OWN, WIDTH + LANES, dtype=BF16), inputs=3)(
            disp, meta, jnp.asarray(first_halo_select())
        )
        row = shifted(halo[:16], -1, 0)
        col = shifted(halo[16:32], 0, -1)
        corner = shifted(halo[32:], -1, -1)

        factors = jnp.stack(
            [item.reshape(25) for item in (jac_diag[0], jac_off[0], jac_off[1], jac_diag[1], inv_radius)]
        )
        spread_factors = jnp.dot(factors, jnp.asarray(node_of.T), precision=lax.Precision.HIGHEST)
        operator = jnp.sum(spread_factors[:, :, None] * jnp.asarray(parts), axis=0).astype(BF16)
        back = jnp.sum(spread_factors[:, None, :] * jnp.asarray(parts.transpose(0, 2, 1)), axis=0).astype(BF16)
        material = call(
            material_kernel, shape(RADIX, 56, LANES), [pltpu.VMEM((16, 56, LANES), F32)], inputs=3
        )(lame_l.reshape(25, WIDTH), lame_m.reshape(25, WIDTH), jnp.asarray(lane_shuffle()))

        work = [
            pltpu.VMEM((2 * NODES, WIDTH), BF16),
            pltpu.VMEM((STRAINS, WIDTH), F32),
            pltpu.VMEM((RADIX, STRAINS, 2 * LANES), F32),
        ]
        tile = shape(16, WIDTH, dtype=BF16)
        shared = (operator, back, jnp.asarray(table), jnp.asarray(tback), material)
        total, pair, side, faces = call(
            step_one_kernel,
            (shape(NODES, WIDTH + LANES), tile, tile, shape(32, WIDTH, dtype=BF16)),
            [pltpu.VMEM((32, WIDTH + LANES), F32)] + work,
            scalars=True, inputs=12, flops=10**9,
        )(place, disp, prev, meta, row, col, corner, *shared, jnp.asarray(outgoing_select()))
        cpair = swapped(pair, "colat", 0)
        cside = swapped(side, "colat", 1)
        pair, side = call(column_kernel, (tile, tile), scalars=True, inputs=4)(
            place, faces, cpair, cside, jnp.asarray(column_select())
        )
        dpair = swapped(pair, "depth", 0)
        dside = swapped(side, "depth", 1)
        middle, final, row, col = call(
            step_two_kernel,
            (shape(OWN, WIDTH), shape(OWN, WIDTH), tile, tile),
            [pltpu.VMEM((NODES, WIDTH), F32)] + work,
            scalars=True, inputs=12, flops=10**9,
        )(place, disp, total, cpair, cside, dpair, dside, *shared, jnp.asarray(arrival_select()))
        corner = shifted(row, 1, 1)
        col = shifted(col, 0, 1)
        row = shifted(row, 1, 0)
        final = call(last_kernel, shape(OWN, WIDTH), inputs=6)(
            final, meta, row, col, corner, jnp.asarray(last_select())
        )
        return middle.reshape(displacement.shape), final.reshape(displacement.shape)

    return jax.shard_map(
        per_device,
        mesh=mesh,
        in_specs=(
            P(None, "colat", "depth", None),
            P(None, "colat", "depth", None),
            P("colat", "depth"),
            P("colat", "depth"),
            P(None, "colat", None, "depth", None),
            P(None, "colat", None, "depth", None),
            P("colat", None, "depth", None),
            P("colat", None, "depth", None, None),
            P("colat", None, "depth", None, None),
        ),
        out_specs=(P(None, "colat", "depth", None), P(None, "colat", "depth", None)),
        check_vma=False,
    )
```

```python
import functools
import math

import jax
import jax.numpy as jnp
import ml_dtypes
import numpy as np
from jax import lax
from jax.experimental import pallas as pl
from jax.experimental.pallas import tpu as pltpu
from jax.sharding import PartitionSpec as P

BF16 = jnp.bfloat16
F32 = jnp.float32
WIDTH = 2048
LANES = 128
RADIX = 16
OWN = 48
NODES = 80
STRAINS = 152
VMEM_LIMIT = 40 * 1024 * 1024


def gll_derivative():
    points = np.array([-1.0, -math.sqrt(3.0 / 7.0), 0.0, math.sqrt(3.0 / 7.0), 1.0])
    weights = np.ones(5)
    for row in range(5):
        for col in range(5):
            if row != col:
                weights[row] /= points[row] - points[col]
    matrix = np.zeros((5, 5))
    for row in range(5):
        for col in range(5):
            if row != col:
                matrix[row, col] = weights[col] / weights[row] / (points[row] - points[col])
        matrix[row, row] = -np.sum(matrix[row])
    return matrix


def node_row(comp, i, j):
    if i == 4:
        return OWN + (12 + comp if j == 4 else 4 * comp + j)
    if j == 4:
        return OWN + 16 + 4 * comp + i
    return 16 * comp + 4 * i + j


def strain_row(strain, node):
    return 24 * strain + node if node < 24 else 144 + strain


def strain_terms():
    deriv = gll_derivative()
    parts = np.zeros((5, STRAINS, 2 * NODES))
    node_of = np.zeros((STRAINS, 25))
    half = math.sqrt(0.5)
    for i in range(5):
        for j in range(5):
            node = 5 * i + j

            def grad(strain, along_z, comp, scale):
                row = strain_row(strain, node)
                for other in range(5):
                    xi, eta = (2, 3) if along_z else (0, 1)
                    parts[xi, row, node_row(comp, other, j)] += scale * deriv[i, other]
                    parts[eta, row, node_row(comp, i, other)] += scale * deriv[j, other]

            def radial(strain, comp, azimuthal, scale):
                row = strain_row(strain, node)
                parts[4, row, NODES * azimuthal + node_row(comp, i, j)] += scale / 1024.0

            grad(0, False, 0, 1.0)
            grad(1, True, 2, 1.0)
            radial(2, 1, 1, 1.0)
            radial(2, 0, 0, 1.0)
            grad(3, True, 0, half)
            grad(3, False, 2, half)
            radial(4, 0, 1, half)
            radial(4, 1, 0, -half)
            grad(4, False, 1, half)
            radial(5, 2, 1, half)
            grad(5, True, 1, half)
            for strain in range(6):
                node_of[strain_row(strain, node), node] = 1.0
    parts[:, 150] = parts[:, 144] + parts[:, 145] + parts[:, 146]
    node_of[150, 24] = 1.0
    return parts.astype(np.float32), node_of.astype(np.float32)


def sample_tables():
    order = np.arange(LANES)[:, None]
    table = np.zeros((RADIX, 2 * LANES, LANES))
    for k0 in range(RADIX):
        angle = 2.0 * math.pi * (order * (16 * np.arange(LANES)[None, :] + k0) % WIDTH) / WIDTH
        table[k0, :LANES] = np.cos(angle)
        table[k0, LANES:] = -np.sin(angle)
    return (
        table.astype(ml_dtypes.bfloat16),
        np.ascontiguousarray(table.transpose(0, 2, 1)).astype(ml_dtypes.bfloat16),
    )


def lane_shuffle():
    shuffle = np.zeros((LANES, LANES))
    for t in range(8):
        for k0 in range(16):
            shuffle[16 * t + k0, 8 * k0 + t] = 1.0
    return shuffle.astype(ml_dtypes.bfloat16)


def face(fixed_i, fixed_j):
    return [(fixed_i, n) if fixed_j is None else (n, fixed_j) for n in range(5)]


def message_row(comp, n):
    return 12 + comp if n == 4 else 4 * comp + n


def pick(faces):
    select = np.zeros((16 * len(faces), NODES))
    for index, nodes in enumerate(faces):
        for comp in range(3):
            for n, (i, j) in enumerate(nodes):
                select[16 * index + message_row(comp, n), node_row(comp, i, j)] = 1.0
    return select


ROW_LOW, ROW_HIGH = face(0, None), face(4, None)
COL_LOW, COL_HIGH = face(None, 0), face(None, 4)


def outgoing_select():
    even = pick([ROW_HIGH, ROW_LOW, COL_HIGH, COL_LOW])
    odd = pick([ROW_LOW, ROW_HIGH, COL_HIGH, COL_LOW])
    return np.stack([even, odd]).astype(ml_dtypes.bfloat16)


def column_select():
    out = np.zeros((4, 32, 64))
    for par_c in range(2):
        faces = [ROW_HIGH, ROW_LOW] if par_c == 0 else [ROW_LOW, ROW_HIGH]
        arrive = pick(faces).T
        full = np.concatenate([pick([COL_HIGH]), pick([COL_LOW])], axis=0)
        whole = np.concatenate([np.eye(32), full @ arrive], axis=1)
        for par_d in range(2):
            out[2 * par_c + par_d] = whole if par_d == 0 else np.roll(whole, 16, axis=0)
    return out.astype(ml_dtypes.bfloat16)


def arrival_select():
    out = np.zeros((4, NODES, 64))
    for par_c in range(2):
        rows = [ROW_HIGH, ROW_LOW] if par_c == 0 else [ROW_LOW, ROW_HIGH]
        for par_d in range(2):
            cols = [COL_HIGH, COL_LOW] if par_d == 0 else [COL_LOW, COL_HIGH]
            out[2 * par_c + par_d] = pick(rows + cols).T
    return out.astype(ml_dtypes.bfloat16)


def turned(value, eighths, scale_sign):
    re, im = value
    eighths = (scale_sign * eighths) % 16
    if eighths == 0:
        return re, im
    if eighths == 4:
        return -im, re
    if eighths == 8:
        return -re, -im
    if eighths == 12:
        return im, -re
    root = math.sqrt(0.5)
    if eighths == 2:
        return (re - im) * root, (im + re) * root
    if eighths == 14:
        return (re + im) * root, (im - re) * root
    cosine = math.cos(2.0 * math.pi * eighths / 16)
    sine = math.sin(2.0 * math.pi * eighths / 16)
    return re * cosine - im * sine, im * cosine + re * sine


def add(left, right):
    return left[0] + right[0], left[1] + right[1]


def sub(left, right):
    return left[0] - right[0], left[1] - right[1]


def transform(values, sign):
    count = len(values)
    if count == 1:
        return values
    even = transform(values[0::2], sign)
    odd = transform(values[1::2], sign)
    odd = [turned(value, q * (16 // count), sign) for q, value in enumerate(odd)]
    return [add(a, b) for a, b in zip(even, odd)] + [sub(a, b) for a, b in zip(even, odd)]


def spread(blocks):
    even = transform(blocks, 1)
    odd = transform([turned(value, b, 1) for b, value in enumerate(blocks)], 1)
    return [value for pair in zip(even, odd) for value in pair]


def gathered(values):
    even = transform(values[0::2], -1)
    odd = transform(values[1::2], -1)
    return [add(a, turned(b, index, -1)) for index, (a, b) in enumerate(zip(even, odd))]


def block(index, part):
    return slice(2 * LANES * index + LANES * part, 2 * LANES * index + LANES * (part + 1))


def orders(index):
    lane = lax.broadcasted_iota(jnp.int32, (1, LANES), 1)
    return (lane + LANES * index).astype(F32)


def dot(left, right):
    return jnp.dot(left, right, preferred_element_type=F32)


def node_column(scalar, rows):
    row = lax.broadcasted_iota(jnp.int32, (len(rows), 1), 0)
    column = jnp.zeros((len(rows), 1), F32)
    for value in sorted(set(rows)):
        chosen = functools.reduce(jnp.logical_or, [row == at for at, held in enumerate(rows) if held == value])
        column = jnp.where(chosen, scalar(value), column)
    return column


def own_rows(ref, lanes):
    return jnp.concatenate([ref[c, i, :, lanes] for c in range(3) for i in range(4)], axis=0)


def own_columns(blocks_ref, mass_ref):
    rows = [(i, j) for i in range(4) for j in range(4)]
    live = node_column(lambda at: blocks_ref[at[0], at[1]].astype(F32), rows)
    mass = node_column(lambda at: mass_ref[at[0], at[1]], rows)
    return jnp.concatenate([live] * 3, axis=0), jnp.concatenate([mass] * 3, axis=0)


def first_kernel(blocks_ref, mass_ref, disp_ref, row_out, col_out, corner_out):
    faces = (
        (row_out, [(0, n) for n in range(4)]),
        (col_out, [(n, 0) for n in range(4)]),
        (corner_out, [(0, 0)]),
    )
    for out, rows in faces:
        live = node_column(lambda at: blocks_ref[at[0], at[1]].astype(F32), rows)
        mass = node_column(lambda at: mass_ref[at[0], at[1]], rows)
        high = mass.astype(BF16).astype(F32)
        lane = lax.broadcasted_iota(jnp.int32, (len(rows), LANES), 1)
        info = jnp.where(lane == 0, high, jnp.where(lane == 1, mass - high, jnp.where(lane == 2, live, 0.0)))
        for c in range(3):
            for index in range(8):
                lanes = slice(256 * index, 256 * (index + 1))
                if out is row_out:
                    value = disp_ref[c, 0, :, lanes]
                elif out is col_out:
                    value = jnp.concatenate([disp_ref[c, n, 0:1, lanes] for n in range(4)], axis=0)
                else:
                    value = disp_ref[c, 0, 0:1, lanes]
                out[c, :, lanes] = jnp.where(live > index, value, 0.0).astype(BF16)
            out[c, :, WIDTH:] = info.astype(BF16)


def material_kernel(lambda_ref, mu_ref, shuffle_ref, out_ref, work):
    for index in range(16):
        lanes = slice(LANES * index, LANES * (index + 1))
        lam = jnp.concatenate([lambda_ref[i, :, lanes] for i in range(5)], axis=0)
        mu = jnp.concatenate([mu_ref[i, :, lanes] for i in range(5)], axis=0) * 2.0
        row = lax.broadcasted_iota(jnp.int32, (8, LANES), 0)
        last = jnp.where(row < 6, mu[24:25], jnp.where(row == 6, lam[24:25], 0.0))
        stacked = jnp.concatenate([lam[:24], mu[:24], last], axis=0)
        high = stacked.astype(BF16)
        low = (stacked - high.astype(F32)).astype(BF16)
        shuffled = dot(high, shuffle_ref[...]) + dot(low, shuffle_ref[...])
        work[index] = shuffled if index == 0 else pltpu.roll(shuffled, 8 * index, 1)
    group = lax.broadcasted_iota(jnp.int32, (8, LANES), 1) // 8
    for rows in range(7):
        part = slice(8 * rows, 8 * rows + 8)
        held = [work[(16 - index) % 16, part] for index in range(16)]
        for bit in range(4):
            chosen = (group >> bit) % 2 == 1
            held = [jnp.where(chosen, held[(index - (1 << bit)) % 16], held[index]) for index in range(16)]
        for index in range(16):
            out_ref[index, part] = held[index] if index == 0 else pltpu.roll(held[index], LANES - 8 * index, 1)


def forces(nodes, operator_ref, back_ref, table_ref, tback_ref, material_ref, both, strain, spectrum, emit):
    for index in range(8):
        order = orders(index)
        re = nodes(block(index, 0))
        im = nodes(block(index, 1))
        both[:NODES, block(index, 0)] = re.astype(BF16)
        both[:NODES, block(index, 1)] = im.astype(BF16)
        both[NODES:, block(index, 0)] = (im * (-order)).astype(BF16)
        both[NODES:, block(index, 1)] = (re * order).astype(BF16)
        lanes = slice(256 * index, 256 * (index + 1))
        strain[:, lanes] = dot(operator_ref[...], both[:, lanes])

    @pl.loop(0, STRAINS // 8)
    def _(group):
        rows = pl.ds(pl.multiple_of(group * 8, 8), 8)
        values = [(strain[rows, block(b, 0)], strain[rows, block(b, 1)]) for b in range(8)]
        for k0, (re, im) in enumerate(spread(values)):
            spectrum[k0, rows, :LANES] = re
            spectrum[k0, rows, LANES:] = im

    for k0 in range(RADIX):
        sample = dot(spectrum[k0].astype(BF16), table_ref[k0])
        lam, mu, last = material_ref[k0, :24], material_ref[k0, 24:48], material_ref[k0, 48:]
        parts = [sample[24 * s : 24 * s + 24] for s in range(6)]
        volume = lam * (parts[0] + parts[1] + parts[2])
        stress = [volume + mu * part for part in parts[:3]] + [mu * part for part in parts[3:]]
        stress.append(last * sample[144:])
        stress = jnp.concatenate(stress, axis=0).astype(BF16)
        spectrum[k0] = dot(stress, tback_ref[k0])

    @pl.loop(0, STRAINS // 8)
    def _(group):
        rows = pl.ds(pl.multiple_of(group * 8, 8), 8)
        values = [(spectrum[k0, rows, :LANES], spectrum[k0, rows, LANES:]) for k0 in range(RADIX)]
        for b, (re, im) in enumerate(gathered(values)):
            strain[rows, block(b, 0)] = re
            strain[rows, block(b, 1)] = im

    for index in range(8):
        lanes = slice(256 * index, 256 * (index + 1))
        order = orders(index)
        pulled = dot(back_ref[...], strain[:, lanes].astype(BF16))
        re = pulled[:NODES, :LANES] + order * pulled[NODES:, LANES:]
        im = pulled[:NODES, LANES:] - order * pulled[NODES:, :LANES]
        emit(index, re, im)


def step_one_kernel(
    place, blocks_ref, mass_ref, disp_ref, prev_ref, row_ref, col_ref, corner_ref,
    operator_ref, back_ref, table_ref, tback_ref, material_ref, select_ref,
    sum_ref, pair_ref, side_ref, faces_ref,
    own, tiles, both, strain, spectrum,
):
    rest_c, rest_d = place[2].astype(F32), place[3].astype(F32)
    for lanes in [slice(256 * n, 256 * (n + 1)) for n in range(8)] + [slice(WIDTH, WIDTH + LANES)]:
        rows = [row_ref[c, :, lanes].astype(F32) * rest_c for c in range(3)]
        corner = [corner_ref[c, :, lanes].astype(F32) * (rest_c * rest_d) for c in range(3)]
        cols = [col_ref[c, :, lanes].astype(F32) * rest_d for c in range(3)]
        width = lanes.stop - lanes.start
        pieces = rows + corner + [jnp.zeros((1, width), F32)] + cols + [jnp.zeros((4, width), F32)]
        tiles[:, lanes] = jnp.concatenate(pieces, axis=0)
    info = tiles[:, WIDTH:]
    lane = lax.broadcasted_iota(jnp.int32, (32, LANES), 1)
    halo_info = jnp.where(lane == 0, info[:, 0:1] + info[:, 1:2], jnp.where(lane == 1, info[:, 2:3], 0.0))
    live, mass = own_columns(blocks_ref, mass_ref)
    lane = lax.broadcasted_iota(jnp.int32, (OWN, LANES), 1)
    sum_ref[:OWN, WIDTH:] = jnp.where(lane == 0, mass, jnp.where(lane == 1, live, 0.0))
    sum_ref[OWN:, WIDTH:] = halo_info

    def nodes(lanes):
        value = own_rows(disp_ref, lanes)
        own[:, lanes] = 2.0 * value - own_rows(prev_ref, lanes)
        value = jnp.where(live > lanes.start // 256, value, 0.0)
        return jnp.concatenate([value, tiles[:, lanes]], axis=0)

    mass = sum_ref[:, WIDTH : WIDTH + 1] * (-1.0 / WIDTH)

    def emit(index, re, im):
        for part, value in ((0, re), (1, im)):
            lanes = block(index, part)
            value = mass * value
            total = jnp.concatenate([own[:, lanes] + value[:OWN], value[OWN:]], axis=0)
            sum_ref[:, lanes] = total
            sent = dot(select_ref[place[0]], total.astype(BF16)).astype(BF16)
            pair_ref[:, lanes] = sent[:16]
            side_ref[:, lanes] = sent[16:32]
            faces_ref[:, lanes] = sent[32:]

    forces(nodes, operator_ref, back_ref, table_ref, tback_ref, material_ref, both, strain, spectrum, emit)


def column_kernel(place, faces_ref, pair_ref, side_ref, select_ref, pair_out, side_out):
    select = select_ref[2 * place[0] + place[1]]
    for index in range(8):
        lanes = slice(256 * index, 256 * (index + 1))
        stacked = jnp.concatenate([faces_ref[:, lanes], pair_ref[:, lanes], side_ref[:, lanes]], axis=0)
        sent = dot(select, stacked).astype(BF16)
        pair_out[:, lanes] = sent[:16]
        side_out[:, lanes] = sent[16:]


def step_two_kernel(
    place, disp_ref, sum_ref, cpair_ref, cside_ref, dpair_ref, dside_ref,
    operator_ref, back_ref, table_ref, tback_ref, material_ref, select_ref,
    mid_ref, sum_out, row_out, col_out, corner_out,
    current, both, strain, spectrum,
):
    select = select_ref[2 * place[0] + place[1]]
    live = sum_ref[:, WIDTH + 1 : WIDTH + 2]
    for index in range(8):
        lanes = slice(256 * index, 256 * (index + 1))
        arrived = jnp.concatenate([ref[:, lanes] for ref in (cpair_ref, cside_ref, dpair_ref, dside_ref)], axis=0)
        value = jnp.where(live > index, sum_ref[:, lanes] + dot(select, arrived), 0.0)
        current[:, lanes] = value
        mid_ref[:, lanes] = value[:OWN]
    mass = sum_ref[:, WIDTH : WIDTH + 1] * (-1.0 / WIDTH)

    def emit(index, re, im):
        for part, value in ((0, re), (1, im)):
            lanes = block(index, part)
            value = mass * value
            total = 2.0 * current[:OWN, lanes] - own_rows(disp_ref, lanes) + value[:OWN]
            value = value.astype(BF16)
            for c in range(3):
                for i in range(4):
                    at = 16 * c + 4 * i
                    sum_out[c, i, :, lanes] = total[at : at + 4]
                at = OWN + 4 * c
                row_out[c, :, lanes] = value[at : at + 4]
                corner_out[c, :, lanes] = value[OWN + 12 + c : OWN + 13 + c]
                col_out[c, :, lanes] = value[at + 16 : at + 20]

    forces(
        lambda lanes: current[:, lanes],
        operator_ref, back_ref, table_ref, tback_ref, material_ref, both, strain, spectrum, emit,
    )


def last_kernel(blocks_ref, sum_ref, row_ref, col_ref, corner_ref, out_ref):
    for i in range(4):
        live = node_column(lambda at: blocks_ref[at[0], at[1]].astype(F32), [(i, n) for n in range(4)])
        first = lax.broadcasted_iota(jnp.int32, (4, 1), 0) == 0
        for c in range(3):
            for index in range(8):
                lanes = slice(256 * index, 256 * (index + 1))
                arrived = col_ref[c, i : i + 1, lanes].astype(F32)
                if i == 0:
                    arrived = arrived + corner_ref[c, :, lanes].astype(F32)
                value = sum_ref[c, i, :, lanes] + jnp.where(first, arrived, 0.0)
                if i == 0:
                    value = value + row_ref[c, :, lanes].astype(F32)
                out_ref[c, i, :, lanes] = jnp.where(live > index, value, 0.0)


def call(kernel, outs, scratch=(), scalars=0, inputs=0, flops=0):
    vmem = pl.BlockSpec(memory_space=pltpu.VMEM)
    return pl.pallas_call(
        kernel,
        out_shape=outs,
        in_specs=[pl.BlockSpec(memory_space=pltpu.SMEM)] * scalars + [vmem] * inputs,
        out_specs=jax.tree.map(lambda _: vmem, outs),
        scratch_shapes=list(scratch),
        compiler_params=pltpu.CompilerParams(vmem_limit_bytes=VMEM_LIMIT),
        cost_estimate=pl.CostEstimate(flops=flops, bytes_accessed=1 << 20, transcendentals=0),
    )


def shape(*dims, dtype=F32):
    return jax.ShapeDtypeStruct(dims, dtype)


def solution(mesh):
    bands, layers = mesh.shape["colat"], mesh.shape["depth"]
    parts, node_of = strain_terms()
    table, tback = sample_tables()

    def shifted(array, by_c, by_d):
        pairs = [
            (c * layers + d, (c + by_c) % bands * layers + (d + by_d) % layers)
            for c in range(bands)
            for d in range(layers)
        ]
        return lax.ppermute(array, ("colat", "depth"), pairs)

    def swapped(array, axis, odd):
        count = mesh.shape[axis]
        pairs = [(n, (n + 1) % count if n % 2 == odd else (n - 1) % count) for n in range(count)]
        return lax.ppermute(array, axis, pairs)

    def per_device(displacement, previous, node_blocks, inverse_mass, jac_diag, jac_off, inv_radius, lame_l, lame_m):
        at_c, at_d = lax.axis_index("colat"), lax.axis_index("depth")
        place = jnp.stack([at_c % 2, at_d % 2, at_c < bands - 1, at_d < layers - 1]).astype(jnp.int32)
        row_face = shape(3, 4, WIDTH + LANES, dtype=BF16)
        point = shape(3, 1, WIDTH + LANES, dtype=BF16)
        row, col, corner = call(first_kernel, (row_face, row_face, point), scalars=2, inputs=1)(
            node_blocks, inverse_mass, displacement
        )
        corner = shifted(corner, -1, -1)
        col = shifted(col, 0, -1)
        row = shifted(row, -1, 0)

        factors = jnp.stack(
            [item.reshape(25) for item in (jac_diag[0], jac_off[0], jac_off[1], jac_diag[1], inv_radius)]
        )
        spread_factors = jnp.dot(factors, jnp.asarray(node_of.T), precision=lax.Precision.HIGHEST)
        operator = jnp.sum(spread_factors[:, :, None] * jnp.asarray(parts), axis=0).astype(BF16)
        back = jnp.sum(spread_factors[:, None, :] * jnp.asarray(parts.transpose(0, 2, 1)), axis=0).astype(BF16)
        material = call(
            material_kernel, shape(RADIX, 56, LANES), [pltpu.VMEM((16, 56, LANES), F32)], inputs=3
        )(lame_l.reshape(5, 5, WIDTH), lame_m.reshape(5, 5, WIDTH), jnp.asarray(lane_shuffle()))

        work = [
            pltpu.VMEM((2 * NODES, WIDTH), BF16),
            pltpu.VMEM((STRAINS, WIDTH), F32),
            pltpu.VMEM((RADIX, STRAINS, 2 * LANES), F32),
        ]
        tile = shape(16, WIDTH, dtype=BF16)
        shared = (operator, back, jnp.asarray(table), jnp.asarray(tback), material)
        total, pair, side, faces = call(
            step_one_kernel,
            (shape(NODES, WIDTH + LANES), tile, tile, shape(32, WIDTH, dtype=BF16)),
            [pltpu.VMEM((OWN, WIDTH), F32), pltpu.VMEM((32, WIDTH + LANES), F32)] + work,
            scalars=3, inputs=11, flops=10**9,
        )(
            place, node_blocks, inverse_mass, displacement, previous, row, col, corner,
            *shared, jnp.asarray(outgoing_select()),
        )
        cpair = swapped(pair, "colat", 0)
        cside = swapped(side, "colat", 1)
        pair, side = call(column_kernel, (tile, tile), scalars=1, inputs=4)(
            place, faces, cpair, cside, jnp.asarray(column_select())
        )
        dpair = swapped(pair, "depth", 0)
        dside = swapped(side, "depth", 1)
        row_face = shape(3, 4, WIDTH, dtype=BF16)
        middle, final, row, col, corner = call(
            step_two_kernel,
            (
                shape(OWN, WIDTH), shape(3, 4, 4, WIDTH), row_face, row_face,
                shape(3, 1, WIDTH, dtype=BF16),
            ),
            [pltpu.VMEM((NODES, WIDTH), F32)] + work,
            scalars=1, inputs=12, flops=10**9,
        )(place, displacement, total, cpair, cside, dpair, dside, *shared, jnp.asarray(arrival_select()))
        corner = shifted(corner, 1, 1)
        col = shifted(col, 0, 1)
        row = shifted(row, 1, 0)
        final = call(last_kernel, shape(3, 4, 4, WIDTH), scalars=1, inputs=4)(
            node_blocks, final, row, col, corner
        )
        return middle.reshape(displacement.shape), final

    return jax.shard_map(
        per_device,
        mesh=mesh,
        in_specs=(
            P(None, "colat", "depth", None),
            P(None, "colat", "depth", None),
            P("colat", "depth"),
            P("colat", "depth"),
            P(None, "colat", None, "depth", None),
            P(None, "colat", None, "depth", None),
            P("colat", None, "depth", None),
            P("colat", None, "depth", None, None),
            P("colat", None, "depth", None, None),
        ),
        out_specs=(P(None, "colat", "depth", None), P(None, "colat", "depth", None)),
        check_vma=False,
    )
```

```python
import functools
import math

import jax
import jax.numpy as jnp
import ml_dtypes
import numpy as np
from jax import lax
from jax.experimental import pallas as pl
from jax.experimental.pallas import tpu as pltpu
from jax.sharding import PartitionSpec as P

BF16 = jnp.bfloat16
F32 = jnp.float32
WIDTH = 2048
LANES = 128
RADIX = 16
OWN = 48
NODES = 80
STRAINS = 152
VMEM_LIMIT = 40 * 1024 * 1024


def gll_derivative():
    points = np.array([-1.0, -math.sqrt(3.0 / 7.0), 0.0, math.sqrt(3.0 / 7.0), 1.0])
    weights = np.ones(5)
    for row in range(5):
        for col in range(5):
            if row != col:
                weights[row] /= points[row] - points[col]
    matrix = np.zeros((5, 5))
    for row in range(5):
        for col in range(5):
            if row != col:
                matrix[row, col] = weights[col] / weights[row] / (points[row] - points[col])
        matrix[row, row] = -np.sum(matrix[row])
    return matrix


def node_row(comp, i, j):
    if i == 4:
        return OWN + (12 + comp if j == 4 else 4 * comp + j)
    if j == 4:
        return OWN + 16 + 4 * comp + i
    return 16 * comp + 4 * i + j


def strain_row(strain, node):
    return 24 * strain + node if node < 24 else 144 + strain


def strain_terms():
    deriv = gll_derivative()
    parts = np.zeros((5, STRAINS, 2 * NODES))
    place_of = np.zeros((2, STRAINS, 5))
    half = math.sqrt(0.5)
    for i in range(5):
        for j in range(5):
            node = 5 * i + j

            def grad(strain, along_z, comp, scale):
                row = strain_row(strain, node)
                for other in range(5):
                    xi, eta = (2, 3) if along_z else (0, 1)
                    parts[xi, row, node_row(comp, other, j)] += scale * deriv[i, other]
                    parts[eta, row, node_row(comp, i, other)] += scale * deriv[j, other]

            def radial(strain, comp, azimuthal, scale):
                row = strain_row(strain, node)
                parts[4, row, NODES * azimuthal + node_row(comp, i, j)] += scale / 1024.0

            grad(0, False, 0, 1.0)
            grad(1, True, 2, 1.0)
            radial(2, 1, 1, 1.0)
            radial(2, 0, 0, 1.0)
            grad(3, True, 0, half)
            grad(3, False, 2, half)
            radial(4, 0, 1, half)
            radial(4, 1, 0, -half)
            grad(4, False, 1, half)
            radial(5, 2, 1, half)
            grad(5, True, 1, half)
            for strain in range(6):
                place_of[0, strain_row(strain, node), i] = 1.0
                place_of[1, strain_row(strain, node), j] = 1.0
    parts[:, 150] = parts[:, 144] + parts[:, 145] + parts[:, 146]
    place_of[:, 150, 4] = 1.0
    return parts.astype(np.float32), place_of.astype(np.float32)


def sample_tables():
    order = np.arange(LANES)[:, None]
    table = np.zeros((RADIX, 2 * LANES, LANES))
    for k0 in range(RADIX):
        angle = 2.0 * math.pi * (order * (16 * np.arange(LANES)[None, :] + k0) % WIDTH) / WIDTH
        table[k0, :LANES] = np.cos(angle)
        table[k0, LANES:] = -np.sin(angle)
    return (
        table.astype(ml_dtypes.bfloat16),
        np.ascontiguousarray(table.transpose(0, 2, 1)).astype(ml_dtypes.bfloat16),
    )


def lane_shuffle():
    shuffle = np.zeros((LANES, LANES))
    for t in range(8):
        for k0 in range(16):
            shuffle[16 * t + k0, 8 * k0 + t] = 1.0
    return shuffle.astype(ml_dtypes.bfloat16)


def face(fixed_i, fixed_j):
    return [(fixed_i, n) if fixed_j is None else (n, fixed_j) for n in range(5)]


def message_row(comp, n):
    return 12 + comp if n == 4 else 4 * comp + n


def pick(faces):
    select = np.zeros((16 * len(faces), NODES))
    for index, nodes in enumerate(faces):
        for comp in range(3):
            for n, (i, j) in enumerate(nodes):
                select[16 * index + message_row(comp, n), node_row(comp, i, j)] = 1.0
    return select


ROW_LOW, ROW_HIGH = face(0, None), face(4, None)
COL_LOW, COL_HIGH = face(None, 0), face(None, 4)


def outgoing_select():
    even = pick([ROW_HIGH, ROW_LOW, COL_HIGH, COL_LOW])
    odd = pick([ROW_LOW, ROW_HIGH, COL_HIGH, COL_LOW])
    return np.stack([even, odd]).astype(ml_dtypes.bfloat16)


def column_select():
    out = np.zeros((4, 32, 64))
    for par_c in range(2):
        faces = [ROW_HIGH, ROW_LOW] if par_c == 0 else [ROW_LOW, ROW_HIGH]
        arrive = pick(faces).T
        full = np.concatenate([pick([COL_HIGH]), pick([COL_LOW])], axis=0)
        whole = np.concatenate([np.eye(32), full @ arrive], axis=1)
        for par_d in range(2):
            out[2 * par_c + par_d] = whole if par_d == 0 else np.roll(whole, 16, axis=0)
    return out.astype(ml_dtypes.bfloat16)


def arrival_select():
    out = np.zeros((4, NODES, 64))
    for par_c in range(2):
        rows = [ROW_HIGH, ROW_LOW] if par_c == 0 else [ROW_LOW, ROW_HIGH]
        for par_d in range(2):
            cols = [COL_HIGH, COL_LOW] if par_d == 0 else [COL_LOW, COL_HIGH]
            out[2 * par_c + par_d] = pick(rows + cols).T
    return out.astype(ml_dtypes.bfloat16)


def turned(value, eighths, scale_sign):
    re, im = value
    eighths = (scale_sign * eighths) % 16
    if eighths == 0:
        return re, im
    if eighths == 4:
        return -im, re
    if eighths == 8:
        return -re, -im
    if eighths == 12:
        return im, -re
    root = math.sqrt(0.5)
    if eighths == 2:
        return (re - im) * root, (im + re) * root
    if eighths == 14:
        return (re + im) * root, (im - re) * root
    cosine = math.cos(2.0 * math.pi * eighths / 16)
    sine = math.sin(2.0 * math.pi * eighths / 16)
    return re * cosine - im * sine, im * cosine + re * sine


def add(left, right):
    return left[0] + right[0], left[1] + right[1]


def sub(left, right):
    return left[0] - right[0], left[1] - right[1]


def transform(values, sign):
    count = len(values)
    if count == 1:
        return values
    even = transform(values[0::2], sign)
    odd = transform(values[1::2], sign)
    odd = [turned(value, q * (16 // count), sign) for q, value in enumerate(odd)]
    return [add(a, b) for a, b in zip(even, odd)] + [sub(a, b) for a, b in zip(even, odd)]


def spread(blocks):
    even = transform(blocks, 1)
    odd = transform([turned(value, b, 1) for b, value in enumerate(blocks)], 1)
    return [value for pair in zip(even, odd) for value in pair]


def gathered(values):
    even = transform(values[0::2], -1)
    odd = transform(values[1::2], -1)
    return [add(a, turned(b, index, -1)) for index, (a, b) in enumerate(zip(even, odd))]


def block(index, part):
    return slice(2 * LANES * index + LANES * part, 2 * LANES * index + LANES * (part + 1))


def orders(index):
    lane = lax.broadcasted_iota(jnp.int32, (1, LANES), 1)
    return (lane + LANES * index).astype(F32)


def dot(left, right):
    return jnp.dot(left, right, preferred_element_type=F32)


def node_column(scalar, rows):
    row = lax.broadcasted_iota(jnp.int32, (len(rows), 1), 0)
    column = jnp.zeros((len(rows), 1), F32)
    for value in sorted(set(rows)):
        chosen = functools.reduce(jnp.logical_or, [row == at for at, held in enumerate(rows) if held == value])
        column = jnp.where(chosen, scalar(value), column)
    return column


def own_rows(ref, lanes):
    return jnp.concatenate([ref[c, i, :, lanes] for c in range(3) for i in range(4)], axis=0)


def first_kernel(blocks_hbm, mass_hbm, disp_hbm, row_out, col_out, corner_out, blocks_ref, mass_ref, disp_ref, sems):
    loads = [
        pltpu.make_async_copy(source, target, sems.at[n])
        for n, (source, target) in enumerate(
            ((blocks_hbm, blocks_ref), (mass_hbm, mass_ref), (disp_hbm, disp_ref))
        )
    ]
    for load in loads:
        load.start()
    for load in loads:
        load.wait()
    faces = (
        (row_out, [(0, n) for n in range(4)]),
        (col_out, [(n, 0) for n in range(4)]),
        (corner_out, [(0, 0)]),
    )
    for out, rows in faces:
        live = node_column(lambda at: blocks_ref[at[0], at[1]].astype(F32), rows)
        mass = node_column(lambda at: mass_ref[at[0], at[1]], rows)
        high = mass.astype(BF16).astype(F32)
        lane = lax.broadcasted_iota(jnp.int32, (len(rows), LANES), 1)
        info = jnp.where(lane == 0, high, jnp.where(lane == 1, mass - high, jnp.where(lane == 2, live, 0.0)))
        for c in range(3):
            for index in range(8):
                lanes = slice(256 * index, 256 * (index + 1))
                if out is row_out:
                    value = disp_ref[c, 0, :, lanes]
                elif out is col_out:
                    value = jnp.concatenate([disp_ref[c, n, 0:1, lanes] for n in range(4)], axis=0)
                else:
                    value = disp_ref[c, 0, 0:1, lanes]
                out[c, :, lanes] = jnp.where(live > index, value, 0.0).astype(BF16)
            out[c, :, WIDTH:] = info.astype(BF16)


def exact_dot(left, right):
    return jnp.dot(left, right, preferred_element_type=F32, precision=lax.Precision.HIGHEST)


def prepare_kernel(
    place, blocks_ref, mass_ref, disp_ref, prev_ref, diag_ref, off_ref, radius_ref, lambda_ref, mu_ref,
    parts_ref, place_of_ref, shuffle_ref, outgoing_ref, column_ref, arrival_ref,
    operator_out, back_out, material_out, own_out, free_out, info_out, outgoing_out, column_out, arrival_out,
    shuffled,
):
    operator = jnp.zeros((STRAINS, 2 * NODES), F32)
    for term, factor in enumerate((diag_ref[0], off_ref[0], off_ref[1], diag_ref[1], radius_ref[...])):
        spread_i = exact_dot(place_of_ref[0], factor) * place_of_ref[1]
        operator = operator + parts_ref[term] * exact_dot(spread_i, jnp.ones((5, 2 * NODES), F32))
    operator_out[...] = operator.astype(BF16)
    back_out[...] = operator.T.astype(BF16)

    nodes = [(i, j) for i in range(4) for j in range(4)]
    live = jnp.concatenate([node_column(lambda at: blocks_ref[at[0], at[1]].astype(F32), nodes)] * 3, axis=0)
    mass = jnp.concatenate([node_column(lambda at: mass_ref[at[0], at[1]], nodes)] * 3, axis=0)
    lane = lax.broadcasted_iota(jnp.int32, (OWN, LANES), 1)
    info_out[:OWN] = jnp.where(lane == 0, mass, jnp.where(lane == 1, live, 0.0))
    lane = lax.broadcasted_iota(jnp.int32, (8, LANES), 1)
    rests = jnp.where(lane == 0, place[2].astype(F32), jnp.where(lane == 1, place[3].astype(F32), 0.0))
    info_out[OWN:] = rests
    for index in range(8):
        lanes = slice(256 * index, 256 * (index + 1))
        value = jnp.where(live > index, own_rows(disp_ref, lanes), 0.0)
        own_out[:, lanes] = value
        free_out[:, lanes] = jnp.where(live > index, 2.0 * value - own_rows(prev_ref, lanes), 0.0)

    outgoing_out[...] = outgoing_ref[place[0]]
    column_out[...] = column_ref[2 * place[0] + place[1]]
    arrival_out[...] = arrival_ref[2 * place[0] + place[1]]

    for which, (ref, factor) in enumerate(((lambda_ref, 1.0), (mu_ref, 2.0))):
        value = ref[...] * factor
        high = value.astype(BF16)
        low = (value - high.astype(F32)).astype(BF16)
        shuffled[which] = dot(high, shuffle_ref[...]) + dot(low, shuffle_ref[...])
    group = lax.broadcasted_iota(jnp.int32, (8, LANES), 1) // 8
    row = lax.broadcasted_iota(jnp.int32, (8, LANES), 0)
    for rows in range(7):
        held = []
        for s in range(16):
            if rows < 6:
                value = shuffled[rows // 3, pl.ds(128 * (rows % 3) + s, 8, stride=16), :]
            else:
                at = slice(384 + s, 385 + s)
                value = jnp.where(row < 6, shuffled[1, at], jnp.where(row == 6, shuffled[0, at], 0.0))
            held.append(value if s == 0 else pltpu.roll(value, 8 * s, 1))
        held = [held[(16 - index) % 16] for index in range(16)]
        for bit in range(4):
            chosen = (group >> bit) % 2 == 1
            held = [jnp.where(chosen, held[(index - (1 << bit)) % 16], held[index]) for index in range(16)]
        for index in range(16):
            value = held[index] if index == 0 else pltpu.roll(held[index], LANES - 8 * index, 1)
            material_out[index, 8 * rows : 8 * rows + 8] = value


def forces(nodes, operator_ref, back_ref, table_ref, tback_ref, material_ref, both, strain, spectrum, emit):
    for index in range(8):
        order = orders(index)
        re = nodes(block(index, 0))
        im = nodes(block(index, 1))
        both[:NODES, block(index, 0)] = re.astype(BF16)
        both[:NODES, block(index, 1)] = im.astype(BF16)
        both[NODES:, block(index, 0)] = (im * (-order)).astype(BF16)
        both[NODES:, block(index, 1)] = (re * order).astype(BF16)
        lanes = slice(256 * index, 256 * (index + 1))
        strain[:, lanes] = dot(operator_ref[...], both[:, lanes])

    for group in range(STRAINS // 8):
        rows = slice(8 * group, 8 * group + 8)
        values = [(strain[rows, block(b, 0)], strain[rows, block(b, 1)]) for b in range(8)]
        for k0, (re, im) in enumerate(spread(values)):
            spectrum[k0, rows, :LANES] = re
            spectrum[k0, rows, LANES:] = im

    for k0 in range(RADIX):
        sample = dot(spectrum[k0].astype(BF16), table_ref[k0])
        lam, mu, last = material_ref[k0, :24], material_ref[k0, 24:48], material_ref[k0, 48:]
        parts = [sample[24 * s : 24 * s + 24] for s in range(6)]
        volume = lam * (parts[0] + parts[1] + parts[2])
        stress = [volume + mu * part for part in parts[:3]] + [mu * part for part in parts[3:]]
        stress.append(last * sample[144:])
        stress = jnp.concatenate(stress, axis=0).astype(BF16)
        spectrum[k0] = dot(stress, tback_ref[k0])

    for group in range(STRAINS // 8):
        rows = slice(8 * group, 8 * group + 8)
        values = [(spectrum[k0, rows, :LANES], spectrum[k0, rows, LANES:]) for k0 in range(RADIX)]
        for b, (re, im) in enumerate(gathered(values)):
            strain[rows, block(b, 0)] = re
            strain[rows, block(b, 1)] = im

    for index in range(8):
        lanes = slice(256 * index, 256 * (index + 1))
        order = orders(index)
        pulled = dot(back_ref[...], strain[:, lanes].astype(BF16))
        re = pulled[:NODES, :LANES] + order * pulled[NODES:, LANES:]
        im = pulled[:NODES, LANES:] - order * pulled[NODES:, :LANES]
        emit(index, re, im)


def step_one_kernel(
    own_ref, free_ref, info_ref, row_ref, col_ref, corner_ref,
    operator_ref, back_ref, table_ref, tback_ref, material_ref, select_ref,
    sum_ref, pair_ref, side_ref, faces_ref,
    tiles, both, strain, spectrum,
):
    rest_c, rest_d = info_ref[OWN : OWN + 1, 0:1], info_ref[OWN : OWN + 1, 1:2]
    for lanes in [slice(256 * n, 256 * (n + 1)) for n in range(8)] + [slice(WIDTH, WIDTH + LANES)]:
        rows = [row_ref[c, :, lanes].astype(F32) * rest_c for c in range(3)]
        corner = [corner_ref[c, :, lanes].astype(F32) * (rest_c * rest_d) for c in range(3)]
        cols = [col_ref[c, :, lanes].astype(F32) * rest_d for c in range(3)]
        width = lanes.stop - lanes.start
        pieces = rows + corner + [jnp.zeros((1, width), F32)] + cols + [jnp.zeros((4, width), F32)]
        tiles[:, lanes] = jnp.concatenate(pieces, axis=0)
    info = tiles[:, WIDTH:]
    lane = lax.broadcasted_iota(jnp.int32, (32, LANES), 1)
    sum_ref[:OWN, WIDTH:] = info_ref[:OWN]
    sum_ref[OWN:, WIDTH:] = jnp.where(
        lane == 0, info[:, 0:1] + info[:, 1:2], jnp.where(lane == 1, info[:, 2:3], 0.0)
    )
    mass = sum_ref[:, WIDTH : WIDTH + 1] * (-1.0 / WIDTH)

    def nodes(lanes):
        return jnp.concatenate([own_ref[:, lanes], tiles[:, lanes]], axis=0)

    def emit(index, re, im):
        for part, value in ((0, re), (1, im)):
            lanes = block(index, part)
            value = mass * value
            sum_ref[:OWN, lanes] = free_ref[:, lanes] + value[:OWN]
            sum_ref[OWN:, lanes] = value[OWN:]
        lanes = slice(256 * index, 256 * (index + 1))
        sent = dot(select_ref[...], sum_ref[:, lanes].astype(BF16)).astype(BF16)
        pair_ref[:, lanes] = sent[:16]
        side_ref[:, lanes] = sent[16:32]
        faces_ref[:, lanes] = sent[32:]

    forces(nodes, operator_ref, back_ref, table_ref, tback_ref, material_ref, both, strain, spectrum, emit)


def column_kernel(faces_ref, pair_ref, side_ref, select_ref, pair_out, side_out):
    for index in range(8):
        lanes = slice(256 * index, 256 * (index + 1))
        stacked = jnp.concatenate([faces_ref[:, lanes], pair_ref[:, lanes], side_ref[:, lanes]], axis=0)
        sent = dot(select_ref[...], stacked).astype(BF16)
        pair_out[:, lanes] = sent[:16]
        side_out[:, lanes] = sent[16:]


def step_two_kernel(
    own_ref, sum_ref, cpair_ref, cside_ref, dpair_ref, dside_ref,
    operator_ref, back_ref, table_ref, tback_ref, material_ref, select_ref,
    mid_ref, sum_out, row_out, col_out, corner_out,
    current, both, strain, spectrum,
):
    live = sum_ref[:, WIDTH + 1 : WIDTH + 2]
    for index in range(8):
        lanes = slice(256 * index, 256 * (index + 1))
        arrived = jnp.concatenate([ref[:, lanes] for ref in (cpair_ref, cside_ref, dpair_ref, dside_ref)], axis=0)
        value = jnp.where(live > index, sum_ref[:, lanes] + dot(select_ref[...], arrived), 0.0)
        current[:, lanes] = value
        mid_ref[:, lanes] = value[:OWN]
    mass = sum_ref[:, WIDTH : WIDTH + 1] * (-1.0 / WIDTH)

    def emit(index, re, im):
        masked = jnp.where(live > index, mass, 0.0)
        for part, value in ((0, re), (1, im)):
            lanes = block(index, part)
            value = masked * value
            total = 2.0 * current[:OWN, lanes] - own_ref[:, lanes] + value[:OWN]
            value = value.astype(BF16)
            for c in range(3):
                for i in range(4):
                    at = 16 * c + 4 * i
                    sum_out[c, i, :, lanes] = total[at : at + 4]
                at = OWN + 4 * c
                row_out[c, :, lanes] = value[at : at + 4]
                corner_out[c, :, lanes] = value[OWN + 12 + c : OWN + 13 + c]
                col_out[c, :, lanes] = value[at + 16 : at + 20]

    forces(
        lambda lanes: current[:, lanes],
        operator_ref, back_ref, table_ref, tback_ref, material_ref, both, strain, spectrum, emit,
    )


def last_kernel(sum_ref, row_ref, col_ref, corner_ref, out_ref):
    first = lax.broadcasted_iota(jnp.int32, (4, 1), 0) == 0
    for c in range(3):
        for i in range(4):
            arrived = col_ref[c, i : i + 1].astype(F32)
            if i == 0:
                arrived = arrived + corner_ref[c].astype(F32)
            value = sum_ref[c, i] + jnp.where(first, arrived, 0.0)
            if i == 0:
                value = value + row_ref[c].astype(F32)
            out_ref[c, i] = value


def call(kernel, outs, scratch=(), scalars=0, inputs=0, flops=0, far=0):
    vmem = pl.BlockSpec(memory_space=pltpu.VMEM)
    return pl.pallas_call(
        kernel,
        out_shape=outs,
        in_specs=[pl.BlockSpec(memory_space=pltpu.HBM)] * far
        + [pl.BlockSpec(memory_space=pltpu.SMEM)] * scalars
        + [vmem] * inputs,
        out_specs=jax.tree.map(lambda _: vmem, outs),
        scratch_shapes=list(scratch),
        compiler_params=pltpu.CompilerParams(vmem_limit_bytes=VMEM_LIMIT),
        cost_estimate=pl.CostEstimate(flops=flops, bytes_accessed=1 << 20, transcendentals=0),
    )


def shape(*dims, dtype=F32):
    return jax.ShapeDtypeStruct(dims, dtype)


def solution(mesh):
    bands, layers = mesh.shape["colat"], mesh.shape["depth"]
    parts, place_of = strain_terms()
    table, tback = sample_tables()

    def shifted(array, by_c, by_d):
        pairs = [
            (c * layers + d, (c + by_c) % bands * layers + (d + by_d) % layers)
            for c in range(bands)
            for d in range(layers)
        ]
        return lax.ppermute(array, ("colat", "depth"), pairs)

    def swapped(array, axis, odd):
        count = mesh.shape[axis]
        pairs = [(n, (n + 1) % count if n % 2 == odd else (n - 1) % count) for n in range(count)]
        return lax.ppermute(array, axis, pairs)

    def per_device(displacement, previous, node_blocks, inverse_mass, jac_diag, jac_off, inv_radius, lame_l, lame_m):
        at_c, at_d = lax.axis_index("colat"), lax.axis_index("depth")
        place = jnp.stack([at_c % 2, at_d % 2, at_c < bands - 1, at_d < layers - 1]).astype(jnp.int32)
        row_face = shape(3, 4, WIDTH + LANES, dtype=BF16)
        point = shape(3, 1, WIDTH + LANES, dtype=BF16)
        row, col, corner = call(
            first_kernel,
            (row_face, row_face, point),
            [
                pltpu.SMEM((4, 4), jnp.int32),
                pltpu.SMEM((4, 4), F32),
                pltpu.VMEM((3, 4, 4, WIDTH), F32),
                pltpu.SemaphoreType.DMA((3,)),
            ],
            far=3,
        )(node_blocks, inverse_mass, displacement)
        corner = shifted(corner, -1, -1)
        col = shifted(col, 0, -1)
        row = shifted(row, -1, 0)

        operator, back, material, own, free, info, outgoing, column, arrival = call(
            prepare_kernel,
            (
                shape(STRAINS, 2 * NODES, dtype=BF16),
                shape(2 * NODES, STRAINS, dtype=BF16),
                shape(RADIX, 56, LANES),
                shape(OWN, WIDTH),
                shape(OWN, WIDTH),
                shape(OWN + 8, LANES),
                shape(64, NODES, dtype=BF16),
                shape(32, 64, dtype=BF16),
                shape(NODES, 64, dtype=BF16),
            ),
            [pltpu.VMEM((2, 400, LANES), F32)],
            scalars=3, inputs=13, flops=10**9,
        )(
            place, node_blocks, inverse_mass, displacement, previous,
            jac_diag.reshape(2, 5, 5), jac_off.reshape(2, 5, 5), inv_radius.reshape(5, 5),
            lame_l.reshape(400, LANES), lame_m.reshape(400, LANES),
            jnp.asarray(parts), jnp.asarray(place_of), jnp.asarray(lane_shuffle()),
            jnp.asarray(outgoing_select()), jnp.asarray(column_select()), jnp.asarray(arrival_select()),
        )

        work = [
            pltpu.VMEM((2 * NODES, WIDTH), BF16),
            pltpu.VMEM((STRAINS, WIDTH), F32),
            pltpu.VMEM((RADIX, STRAINS, 2 * LANES), F32),
        ]
        tile = shape(16, WIDTH, dtype=BF16)
        shared = (operator, back, jnp.asarray(table), jnp.asarray(tback), material)
        total, pair, side, faces = call(
            step_one_kernel,
            (shape(NODES, WIDTH + LANES), tile, tile, shape(32, WIDTH, dtype=BF16)),
            [pltpu.VMEM((32, WIDTH + LANES), F32)] + work,
            inputs=12, flops=10**9,
        )(own, free, info, row, col, corner, *shared, outgoing)
        cpair = swapped(pair, "colat", 0)
        cside = swapped(side, "colat", 1)
        pair, side = call(column_kernel, (tile, tile), inputs=4)(faces, cpair, cside, column)
        dpair = swapped(pair, "depth", 0)
        dside = swapped(side, "depth", 1)
        row_face = shape(3, 4, WIDTH, dtype=BF16)
        middle, final, row, col, corner = call(
            step_two_kernel,
            (
                shape(OWN, WIDTH), shape(3, 4, 4, WIDTH), row_face, row_face,
                shape(3, 1, WIDTH, dtype=BF16),
            ),
            [pltpu.VMEM((NODES, WIDTH), F32)] + work,
            inputs=12, flops=10**9,
        )(own, total, cpair, cside, dpair, dside, *shared, arrival)
        corner = shifted(corner, 1, 1)
        col = shifted(col, 0, 1)
        row = shifted(row, 1, 0)
        final = call(last_kernel, shape(3, 4, 4, WIDTH), inputs=4)(final, row, col, corner)
        return middle.reshape(displacement.shape), final

    return jax.shard_map(
        per_device,
        mesh=mesh,
        in_specs=(
            P(None, "colat", "depth", None),
            P(None, "colat", "depth", None),
            P("colat", "depth"),
            P("colat", "depth"),
            P(None, "colat", None, "depth", None),
            P(None, "colat", None, "depth", None),
            P("colat", None, "depth", None),
            P("colat", None, "depth", None, None),
            P("colat", None, "depth", None, None),
        ),
        out_specs=(P(None, "colat", "depth", None), P(None, "colat", "depth", None)),
        check_vma=False,
    )
```

```python
import functools
import math

import jax
import jax.numpy as jnp
import ml_dtypes
import numpy as np
from jax import lax
from jax.experimental import pallas as pl
from jax.experimental.pallas import tpu as pltpu
from jax.sharding import PartitionSpec as P

BF16 = jnp.bfloat16
F32 = jnp.float32
WIDTH = 2048
LANES = 128
RADIX = 16
OWN = 48
NODES = 80
STRAINS = 152
VMEM_LIMIT = 40 * 1024 * 1024


def gll_derivative():
    points = np.array([-1.0, -math.sqrt(3.0 / 7.0), 0.0, math.sqrt(3.0 / 7.0), 1.0])
    weights = np.ones(5)
    for row in range(5):
        for col in range(5):
            if row != col:
                weights[row] /= points[row] - points[col]
    matrix = np.zeros((5, 5))
    for row in range(5):
        for col in range(5):
            if row != col:
                matrix[row, col] = weights[col] / weights[row] / (points[row] - points[col])
        matrix[row, row] = -np.sum(matrix[row])
    return matrix


def node_row(comp, i, j):
    if i == 4:
        return OWN + (12 + comp if j == 4 else 4 * comp + j)
    if j == 4:
        return OWN + 16 + 4 * comp + i
    return 16 * comp + 4 * i + j


def strain_row(strain, node):
    return 24 * strain + node if node < 24 else 144 + strain


def strain_terms():
    deriv = gll_derivative()
    parts = np.zeros((5, STRAINS, 2 * NODES))
    place_of = np.zeros((2, STRAINS, 5))
    half = math.sqrt(0.5)
    for i in range(5):
        for j in range(5):
            node = 5 * i + j

            def grad(strain, along_z, comp, scale):
                row = strain_row(strain, node)
                for other in range(5):
                    xi, eta = (2, 3) if along_z else (0, 1)
                    parts[xi, row, node_row(comp, other, j)] += scale * deriv[i, other]
                    parts[eta, row, node_row(comp, i, other)] += scale * deriv[j, other]

            def radial(strain, comp, azimuthal, scale):
                row = strain_row(strain, node)
                parts[4, row, NODES * azimuthal + node_row(comp, i, j)] += scale / 1024.0

            grad(0, False, 0, 1.0)
            grad(1, True, 2, 1.0)
            radial(2, 1, 1, 1.0)
            radial(2, 0, 0, 1.0)
            grad(3, True, 0, half)
            grad(3, False, 2, half)
            radial(4, 0, 1, half)
            radial(4, 1, 0, -half)
            grad(4, False, 1, half)
            radial(5, 2, 1, half)
            grad(5, True, 1, half)
            for strain in range(6):
                place_of[0, strain_row(strain, node), i] = 1.0
                place_of[1, strain_row(strain, node), j] = 1.0
    parts[:, 150] = parts[:, 144] + parts[:, 145] + parts[:, 146]
    place_of[:, 150, 4] = 1.0
    return parts.astype(np.float32), place_of.astype(np.float32)


def sample_tables():
    order = np.arange(LANES)[:, None]
    table = np.zeros((RADIX, 2 * LANES, LANES))
    for k0 in range(RADIX):
        angle = 2.0 * math.pi * (order * (16 * np.arange(LANES)[None, :] + k0) % WIDTH) / WIDTH
        table[k0, :LANES] = np.cos(angle)
        table[k0, LANES:] = -np.sin(angle)
    return (
        table.astype(ml_dtypes.bfloat16),
        np.ascontiguousarray(table.transpose(0, 2, 1)).astype(ml_dtypes.bfloat16),
    )


def lane_shuffle():
    shuffle = np.zeros((LANES, LANES))
    for t in range(8):
        for k0 in range(16):
            shuffle[16 * t + k0, 8 * k0 + t] = 1.0
    return shuffle.astype(ml_dtypes.bfloat16)


def face(fixed_i, fixed_j):
    return [(fixed_i, n) if fixed_j is None else (n, fixed_j) for n in range(5)]


def message_row(comp, n):
    return 12 + comp if n == 4 else 4 * comp + n


def pick(faces):
    select = np.zeros((16 * len(faces), NODES))
    for index, nodes in enumerate(faces):
        for comp in range(3):
            for n, (i, j) in enumerate(nodes):
                select[16 * index + message_row(comp, n), node_row(comp, i, j)] = 1.0
    return select


ROW_LOW, ROW_HIGH = face(0, None), face(4, None)
COL_LOW, COL_HIGH = face(None, 0), face(None, 4)


def outgoing_select():
    even = pick([ROW_HIGH, ROW_LOW, COL_HIGH, COL_LOW])
    odd = pick([ROW_LOW, ROW_HIGH, COL_HIGH, COL_LOW])
    return np.stack([even, odd]).astype(ml_dtypes.bfloat16)


def column_select():
    out = np.zeros((4, 32, 64))
    for par_c in range(2):
        faces = [ROW_HIGH, ROW_LOW] if par_c == 0 else [ROW_LOW, ROW_HIGH]
        arrive = pick(faces).T
        full = np.concatenate([pick([COL_HIGH]), pick([COL_LOW])], axis=0)
        whole = np.concatenate([np.eye(32), full @ arrive], axis=1)
        for par_d in range(2):
            out[2 * par_c + par_d] = whole if par_d == 0 else np.roll(whole, 16, axis=0)
    return out.astype(ml_dtypes.bfloat16)


def arrival_select():
    out = np.zeros((4, NODES, 64))
    for par_c in range(2):
        rows = [ROW_HIGH, ROW_LOW] if par_c == 0 else [ROW_LOW, ROW_HIGH]
        for par_d in range(2):
            cols = [COL_HIGH, COL_LOW] if par_d == 0 else [COL_LOW, COL_HIGH]
            out[2 * par_c + par_d] = pick(rows + cols).T
    return out.astype(ml_dtypes.bfloat16)


def turned(value, eighths, scale_sign):
    re, im = value
    eighths = (scale_sign * eighths) % 16
    if eighths == 0:
        return re, im
    if eighths == 4:
        return -im, re
    if eighths == 8:
        return -re, -im
    if eighths == 12:
        return im, -re
    root = math.sqrt(0.5)
    if eighths == 2:
        return (re - im) * root, (im + re) * root
    if eighths == 14:
        return (re + im) * root, (im - re) * root
    cosine = math.cos(2.0 * math.pi * eighths / 16)
    sine = math.sin(2.0 * math.pi * eighths / 16)
    return re * cosine - im * sine, im * cosine + re * sine


def add(left, right):
    return left[0] + right[0], left[1] + right[1]


def sub(left, right):
    return left[0] - right[0], left[1] - right[1]


def transform(values, sign):
    count = len(values)
    if count == 1:
        return values
    even = transform(values[0::2], sign)
    odd = transform(values[1::2], sign)
    odd = [turned(value, q * (16 // count), sign) for q, value in enumerate(odd)]
    return [add(a, b) for a, b in zip(even, odd)] + [sub(a, b) for a, b in zip(even, odd)]


def spread(blocks):
    even = transform(blocks, 1)
    odd = transform([turned(value, b, 1) for b, value in enumerate(blocks)], 1)
    return [value for pair in zip(even, odd) for value in pair]


def gathered(values):
    even = transform(values[0::2], -1)
    odd = transform(values[1::2], -1)
    return [add(a, turned(b, index, -1)) for index, (a, b) in enumerate(zip(even, odd))]


def block(index, part):
    return slice(2 * LANES * index + LANES * part, 2 * LANES * index + LANES * (part + 1))


def orders(index):
    lane = lax.broadcasted_iota(jnp.int32, (1, LANES), 1)
    return (lane + LANES * index).astype(F32)


def dot(left, right):
    return jnp.dot(left, right, preferred_element_type=F32)


def node_column(scalar, rows):
    row = lax.broadcasted_iota(jnp.int32, (len(rows), 1), 0)
    column = jnp.zeros((len(rows), 1), F32)
    for value in sorted(set(rows)):
        chosen = functools.reduce(jnp.logical_or, [row == at for at, held in enumerate(rows) if held == value])
        column = jnp.where(chosen, scalar(value), column)
    return column


def own_rows(ref, lanes):
    return jnp.concatenate([ref[c, i, :, lanes] for c in range(3) for i in range(4)], axis=0)


def first_kernel(blocks_hbm, mass_hbm, disp_hbm, row_out, col_out, corner_out, blocks_ref, mass_ref, disp_ref, sems):
    loads = [
        pltpu.make_async_copy(source, target, sems.at[n])
        for n, (source, target) in enumerate(
            ((blocks_hbm, blocks_ref), (mass_hbm, mass_ref), (disp_hbm, disp_ref))
        )
    ]
    for load in loads:
        load.start()
    for load in loads:
        load.wait()
    faces = (
        (row_out, [(0, n) for n in range(4)]),
        (col_out, [(n, 0) for n in range(4)]),
        (corner_out, [(0, 0)]),
    )
    for out, rows in faces:
        live = node_column(lambda at: blocks_ref[at[0], at[1]].astype(F32), rows)
        mass = node_column(lambda at: mass_ref[at[0], at[1]], rows)
        high = mass.astype(BF16).astype(F32)
        lane = lax.broadcasted_iota(jnp.int32, (len(rows), LANES), 1)
        info = jnp.where(lane == 0, high, jnp.where(lane == 1, mass - high, jnp.where(lane == 2, live, 0.0)))
        for c in range(3):
            for index in range(8):
                lanes = slice(256 * index, 256 * (index + 1))
                if out is row_out:
                    value = disp_ref[c, 0, :, lanes]
                elif out is col_out:
                    value = jnp.concatenate([disp_ref[c, n, 0:1, lanes] for n in range(4)], axis=0)
                else:
                    value = disp_ref[c, 0, 0:1, lanes]
                out[c, :, lanes] = jnp.where(live > index, value, 0.0).astype(BF16)
            out[c, :, WIDTH:] = info.astype(BF16)


def exact_dot(left, right):
    return jnp.dot(left, right, preferred_element_type=F32, precision=lax.Precision.HIGHEST)


def prepare_kernel(
    place, blocks_ref, mass_ref, disp_ref, prev_ref, diag_ref, off_ref, radius_ref, lambda_ref, mu_ref,
    parts_ref, place_of_ref, shuffle_ref, outgoing_ref, column_ref, arrival_ref,
    operator_out, back_out, material_out, own_out, free_out, info_out, outgoing_out, column_out, arrival_out,
    shuffled,
):
    operator = jnp.zeros((STRAINS, 2 * NODES), F32)
    for term, factor in enumerate((diag_ref[0], off_ref[0], off_ref[1], diag_ref[1], radius_ref[...])):
        spread_i = exact_dot(place_of_ref[0], factor) * place_of_ref[1]
        operator = operator + parts_ref[term] * exact_dot(spread_i, jnp.ones((5, 2 * NODES), F32))
    operator_out[...] = operator.astype(BF16)
    back_out[...] = operator.T.astype(BF16)

    nodes = [(i, j) for i in range(4) for j in range(4)]
    live = jnp.concatenate([node_column(lambda at: blocks_ref[at[0], at[1]].astype(F32), nodes)] * 3, axis=0)
    mass = jnp.concatenate([node_column(lambda at: mass_ref[at[0], at[1]], nodes)] * 3, axis=0)
    lane = lax.broadcasted_iota(jnp.int32, (OWN, LANES), 1)
    info_out[:OWN] = jnp.where(lane == 0, mass, jnp.where(lane == 1, live, 0.0))
    lane = lax.broadcasted_iota(jnp.int32, (8, LANES), 1)
    rests = jnp.where(lane == 0, place[2].astype(F32), jnp.where(lane == 1, place[3].astype(F32), 0.0))
    info_out[OWN:] = rests
    for index in range(8):
        lanes = slice(256 * index, 256 * (index + 1))
        value = jnp.where(live > index, own_rows(disp_ref, lanes), 0.0)
        own_out[:, lanes] = value
        free_out[:, lanes] = jnp.where(live > index, 2.0 * value - own_rows(prev_ref, lanes), 0.0)

    outgoing_out[...] = outgoing_ref[place[0]]
    column_out[...] = column_ref[2 * place[0] + place[1]]
    arrival_out[...] = arrival_ref[2 * place[0] + place[1]]

    for which, (ref, factor) in enumerate(((lambda_ref, 1.0), (mu_ref, 2.0))):
        value = ref[...] * factor
        high = value.astype(BF16)
        low = (value - high.astype(F32)).astype(BF16)
        shuffled[which] = dot(high, shuffle_ref[...]) + dot(low, shuffle_ref[...])
    group = lax.broadcasted_iota(jnp.int32, (8, LANES), 1) // 8
    row = lax.broadcasted_iota(jnp.int32, (8, LANES), 0)
    for rows in range(7):
        held = []
        for s in range(16):
            if rows < 6:
                value = shuffled[rows // 3, pl.ds(128 * (rows % 3) + s, 8, stride=16), :]
            else:
                at = slice(384 + s, 385 + s)
                value = jnp.where(row < 6, shuffled[1, at], jnp.where(row == 6, shuffled[0, at], 0.0))
            held.append(value if s == 0 else pltpu.roll(value, 8 * s, 1))
        held = [held[(16 - index) % 16] for index in range(16)]
        for bit in range(4):
            chosen = (group >> bit) % 2 == 1
            held = [jnp.where(chosen, held[(index - (1 << bit)) % 16], held[index]) for index in range(16)]
        for index in range(16):
            value = held[index] if index == 0 else pltpu.roll(held[index], LANES - 8 * index, 1)
            material_out[index, 8 * rows : 8 * rows + 8] = value


def forces(nodes, operator_ref, back_ref, table_ref, tback_ref, material_ref, both, strain, spectrum, emit):
    for index in range(8):
        order = orders(index)
        re = nodes(block(index, 0))
        im = nodes(block(index, 1))
        both[:NODES, block(index, 0)] = re.astype(BF16)
        both[:NODES, block(index, 1)] = im.astype(BF16)
        both[NODES:, block(index, 0)] = (im * (-order)).astype(BF16)
        both[NODES:, block(index, 1)] = (re * order).astype(BF16)
        lanes = slice(256 * index, 256 * (index + 1))
        strain[:, lanes] = dot(operator_ref[...], both[:, lanes])

    for group in range(STRAINS // 8):
        rows = slice(8 * group, 8 * group + 8)
        values = [(strain[rows, block(b, 0)], strain[rows, block(b, 1)]) for b in range(8)]
        for k0, (re, im) in enumerate(spread(values)):
            spectrum[k0, rows, :LANES] = re
            spectrum[k0, rows, LANES:] = im

    for k0 in range(RADIX):
        sample = dot(spectrum[k0].astype(BF16), table_ref[k0])
        lam, mu, last = material_ref[k0, :24], material_ref[k0, 24:48], material_ref[k0, 48:]
        parts = [sample[24 * s : 24 * s + 24] for s in range(6)]
        volume = lam * (parts[0] + parts[1] + parts[2])
        stress = [volume + mu * part for part in parts[:3]] + [mu * part for part in parts[3:]]
        stress.append(last * sample[144:])
        stress = jnp.concatenate(stress, axis=0).astype(BF16)
        spectrum[k0] = dot(stress, tback_ref[k0])

    for group in range(STRAINS // 8):
        rows = slice(8 * group, 8 * group + 8)
        values = [(spectrum[k0, rows, :LANES], spectrum[k0, rows, LANES:]) for k0 in range(RADIX)]
        for b, (re, im) in enumerate(gathered(values)):
            strain[rows, block(b, 0)] = re
            strain[rows, block(b, 1)] = im

    for index in range(8):
        lanes = slice(256 * index, 256 * (index + 1))
        order = orders(index)
        pulled = dot(back_ref[...], strain[:, lanes].astype(BF16))
        re = pulled[:NODES, :LANES] + order * pulled[NODES:, LANES:]
        im = pulled[:NODES, LANES:] - order * pulled[NODES:, :LANES]
        emit(index, re, im)


def step_one_kernel(
    own_ref, free_ref, info_ref, row_ref, col_ref, corner_ref,
    operator_ref, back_ref, table_ref, tback_ref, material_ref, select_ref,
    sum_ref, pair_ref, side_ref, faces_ref,
    tiles, both, strain, spectrum,
):
    rest_c, rest_d = info_ref[OWN : OWN + 1, 0:1], info_ref[OWN : OWN + 1, 1:2]
    for lanes in [slice(256 * n, 256 * (n + 1)) for n in range(8)] + [slice(WIDTH, WIDTH + LANES)]:
        rows = [row_ref[c, :, lanes].astype(F32) * rest_c for c in range(3)]
        corner = [corner_ref[c, :, lanes].astype(F32) * (rest_c * rest_d) for c in range(3)]
        cols = [col_ref[c, :, lanes].astype(F32) * rest_d for c in range(3)]
        width = lanes.stop - lanes.start
        pieces = rows + corner + [jnp.zeros((1, width), F32)] + cols + [jnp.zeros((4, width), F32)]
        tiles[:, lanes] = jnp.concatenate(pieces, axis=0)
    info = tiles[:, WIDTH:]
    lane = lax.broadcasted_iota(jnp.int32, (32, LANES), 1)
    sum_ref[:OWN, WIDTH:] = info_ref[:OWN]
    sum_ref[OWN:, WIDTH:] = jnp.where(
        lane == 0, info[:, 0:1] + info[:, 1:2], jnp.where(lane == 1, info[:, 2:3], 0.0)
    )
    mass = sum_ref[:, WIDTH : WIDTH + 1] * (-1.0 / WIDTH)

    def nodes(lanes):
        return jnp.concatenate([own_ref[:, lanes], tiles[:, lanes]], axis=0)

    def emit(index, re, im):
        for part, value in ((0, re), (1, im)):
            lanes = block(index, part)
            value = mass * value
            sum_ref[:OWN, lanes] = free_ref[:, lanes] + value[:OWN]
            sum_ref[OWN:, lanes] = value[OWN:]
        lanes = slice(256 * index, 256 * (index + 1))
        sent = dot(select_ref[...], sum_ref[:, lanes].astype(BF16)).astype(BF16)
        pair_ref[:, lanes] = sent[:16]
        side_ref[:, lanes] = sent[16:32]
        faces_ref[:, lanes] = sent[32:]

    forces(nodes, operator_ref, back_ref, table_ref, tback_ref, material_ref, both, strain, spectrum, emit)


def column_kernel(faces_ref, pair_ref, side_ref, select_ref, pair_out, side_out):
    for index in range(8):
        lanes = slice(256 * index, 256 * (index + 1))
        stacked = jnp.concatenate([faces_ref[:, lanes], pair_ref[:, lanes], side_ref[:, lanes]], axis=0)
        sent = dot(select_ref[...], stacked).astype(BF16)
        pair_out[:, lanes] = sent[:16]
        side_out[:, lanes] = sent[16:]


def step_two_kernel(
    own_ref, sum_ref, cpair_ref, cside_ref, dpair_ref, dside_ref,
    operator_ref, back_ref, table_ref, tback_ref, material_ref, select_ref,
    mid_ref, sum_out, row_out, col_out, corner_out,
    current, both, strain, spectrum,
):
    live = sum_ref[:, WIDTH + 1 : WIDTH + 2]
    for index in range(8):
        lanes = slice(256 * index, 256 * (index + 1))
        arrived = jnp.concatenate([ref[:, lanes] for ref in (cpair_ref, cside_ref, dpair_ref, dside_ref)], axis=0)
        value = jnp.where(live > index, sum_ref[:, lanes] + dot(select_ref[...], arrived), 0.0)
        current[:, lanes] = value
        mid_ref[:, lanes] = value[:OWN]
    mass = sum_ref[:, WIDTH : WIDTH + 1] * (-1.0 / WIDTH)

    def emit(index, re, im):
        masked = jnp.where(live > index, mass, 0.0)
        for part, value in ((0, re), (1, im)):
            lanes = block(index, part)
            value = masked * value
            total = 2.0 * current[:OWN, lanes] - own_ref[:, lanes] + value[:OWN]
            value = value.astype(BF16)
            for c in range(3):
                for i in range(4):
                    at = 16 * c + 4 * i
                    sum_out[c, i, :, lanes] = total[at : at + 4]
                at = OWN + 4 * c
                row_out[c, :, lanes] = value[at : at + 4]
                corner_out[c, :, lanes] = value[OWN + 12 + c : OWN + 13 + c]
                col_out[c, :, lanes] = value[at + 16 : at + 20]

    forces(
        lambda lanes: current[:, lanes],
        operator_ref, back_ref, table_ref, tback_ref, material_ref, both, strain, spectrum, emit,
    )


def last_kernel(sum_ref, row_ref, col_ref, corner_ref, out_ref):
    first = lax.broadcasted_iota(jnp.int32, (4, 1), 0) == 0
    for c in range(3):
        for i in range(4):
            arrived = col_ref[c, i : i + 1].astype(F32)
            if i == 0:
                arrived = arrived + corner_ref[c].astype(F32)
            value = sum_ref[c, i] + jnp.where(first, arrived, 0.0)
            if i == 0:
                value = value + row_ref[c].astype(F32)
            out_ref[c, i] = value


def call(kernel, outs, scratch=(), scalars=0, inputs=0, flops=0, far=0, vmem=VMEM_LIMIT):
    near = pl.BlockSpec(memory_space=pltpu.VMEM)
    return pl.pallas_call(
        kernel,
        out_shape=outs,
        in_specs=[pl.BlockSpec(memory_space=pltpu.HBM)] * far
        + [pl.BlockSpec(memory_space=pltpu.SMEM)] * scalars
        + [near] * inputs,
        out_specs=jax.tree.map(lambda _: near, outs),
        scratch_shapes=list(scratch),
        compiler_params=pltpu.CompilerParams(vmem_limit_bytes=vmem),
        cost_estimate=pl.CostEstimate(flops=flops, bytes_accessed=1 << 20, transcendentals=0),
    )


def shape(*dims, dtype=F32):
    return jax.ShapeDtypeStruct(dims, dtype)


def solution(mesh):
    bands, layers = mesh.shape["colat"], mesh.shape["depth"]
    parts, place_of = strain_terms()
    table, tback = sample_tables()

    def shifted(array, by_c, by_d):
        pairs = [
            (c * layers + d, (c + by_c) % bands * layers + (d + by_d) % layers)
            for c in range(bands)
            for d in range(layers)
        ]
        return lax.ppermute(array, ("colat", "depth"), pairs)

    def swapped(array, axis, odd):
        count = mesh.shape[axis]
        pairs = [(n, (n + 1) % count if n % 2 == odd else (n - 1) % count) for n in range(count)]
        return lax.ppermute(array, axis, pairs)

    def per_device(displacement, previous, node_blocks, inverse_mass, jac_diag, jac_off, inv_radius, lame_l, lame_m):
        at_c, at_d = lax.axis_index("colat"), lax.axis_index("depth")
        place = jnp.stack([at_c % 2, at_d % 2, at_c < bands - 1, at_d < layers - 1]).astype(jnp.int32)
        row_face = shape(3, 4, WIDTH + LANES, dtype=BF16)
        point = shape(3, 1, WIDTH + LANES, dtype=BF16)
        row, col, corner = call(
            first_kernel,
            (row_face, row_face, point),
            [
                pltpu.SMEM((4, 4), jnp.int32),
                pltpu.SMEM((4, 4), F32),
                pltpu.VMEM((3, 4, 4, WIDTH), F32),
                pltpu.SemaphoreType.DMA((3,)),
            ],
            far=3, flops=2 * 10**11, vmem=62 * 1024 * 1024,
        )(node_blocks, inverse_mass, displacement)
        corner = shifted(corner, -1, -1)
        col = shifted(col, 0, -1)
        row = shifted(row, -1, 0)

        operator, back, material, own, free, info, outgoing, column, arrival = call(
            prepare_kernel,
            (
                shape(STRAINS, 2 * NODES, dtype=BF16),
                shape(2 * NODES, STRAINS, dtype=BF16),
                shape(RADIX, 56, LANES),
                shape(OWN, WIDTH),
                shape(OWN, WIDTH),
                shape(OWN + 8, LANES),
                shape(64, NODES, dtype=BF16),
                shape(32, 64, dtype=BF16),
                shape(NODES, 64, dtype=BF16),
            ),
            [pltpu.VMEM((2, 400, LANES), F32)],
            scalars=3, inputs=13, flops=10**9,
        )(
            place, node_blocks, inverse_mass, displacement, previous,
            jac_diag.reshape(2, 5, 5), jac_off.reshape(2, 5, 5), inv_radius.reshape(5, 5),
            lame_l.reshape(400, LANES), lame_m.reshape(400, LANES),
            jnp.asarray(parts), jnp.asarray(place_of), jnp.asarray(lane_shuffle()),
            jnp.asarray(outgoing_select()), jnp.asarray(column_select()), jnp.asarray(arrival_select()),
        )

        work = [
            pltpu.VMEM((2 * NODES, WIDTH), BF16),
            pltpu.VMEM((STRAINS, WIDTH), F32),
            pltpu.VMEM((RADIX, STRAINS, 2 * LANES), F32),
        ]
        tile = shape(16, WIDTH, dtype=BF16)
        shared = (operator, back, jnp.asarray(table), jnp.asarray(tback), material)
        total, pair, side, faces = call(
            step_one_kernel,
            (shape(NODES, WIDTH + LANES), tile, tile, shape(32, WIDTH, dtype=BF16)),
            [pltpu.VMEM((32, WIDTH + LANES), F32)] + work,
            inputs=12, flops=10**9,
        )(own, free, info, row, col, corner, *shared, outgoing)
        cpair = swapped(pair, "colat", 0)
        cside = swapped(side, "colat", 1)
        pair, side = call(column_kernel, (tile, tile), inputs=4)(faces, cpair, cside, column)
        dpair = swapped(pair, "depth", 0)
        dside = swapped(side, "depth", 1)
        row_face = shape(3, 4, WIDTH, dtype=BF16)
        middle, final, row, col, corner = call(
            step_two_kernel,
            (
                shape(OWN, WIDTH), shape(3, 4, 4, WIDTH), row_face, row_face,
                shape(3, 1, WIDTH, dtype=BF16),
            ),
            [pltpu.VMEM((NODES, WIDTH), F32)] + work,
            inputs=12, flops=10**9,
        )(own, total, cpair, cside, dpair, dside, *shared, arrival)
        corner = shifted(corner, 1, 1)
        col = shifted(col, 0, 1)
        row = shifted(row, 1, 0)
        final = call(last_kernel, shape(3, 4, 4, WIDTH), inputs=4)(final, row, col, corner)
        return middle.reshape(displacement.shape), final

    return jax.shard_map(
        per_device,
        mesh=mesh,
        in_specs=(
            P(None, "colat", "depth", None),
            P(None, "colat", "depth", None),
            P("colat", "depth"),
            P("colat", "depth"),
            P(None, "colat", None, "depth", None),
            P(None, "colat", None, "depth", None),
            P("colat", None, "depth", None),
            P("colat", None, "depth", None, None),
            P("colat", None, "depth", None, None),
        ),
        out_specs=(P(None, "colat", "depth", None), P(None, "colat", "depth", None)),
        check_vma=False,
    )
```

```python
import functools
import math

import jax
import jax.numpy as jnp
import ml_dtypes
import numpy as np
from jax import lax
from jax.experimental import pallas as pl
from jax.experimental.pallas import tpu as pltpu
from jax.sharding import PartitionSpec as P

BF16 = jnp.bfloat16
F32 = jnp.float32
WIDTH = 2048
LANES = 128
RADIX = 16
OWN = 48
NODES = 80
STRAINS = 152
VMEM_LIMIT = 40 * 1024 * 1024


def gll_derivative():
    points = np.array([-1.0, -math.sqrt(3.0 / 7.0), 0.0, math.sqrt(3.0 / 7.0), 1.0])
    weights = np.ones(5)
    for row in range(5):
        for col in range(5):
            if row != col:
                weights[row] /= points[row] - points[col]
    matrix = np.zeros((5, 5))
    for row in range(5):
        for col in range(5):
            if row != col:
                matrix[row, col] = weights[col] / weights[row] / (points[row] - points[col])
        matrix[row, row] = -np.sum(matrix[row])
    return matrix


def node_row(comp, i, j):
    if i == 4:
        return OWN + (12 + comp if j == 4 else 4 * comp + j)
    if j == 4:
        return OWN + 16 + 4 * comp + i
    return 16 * comp + 4 * i + j


def strain_row(strain, node):
    return 24 * strain + node if node < 24 else 144 + strain


def strain_terms():
    deriv = gll_derivative()
    parts = np.zeros((5, STRAINS, 2 * NODES))
    place_of = np.zeros((2, STRAINS, 5))
    half = math.sqrt(0.5)
    for i in range(5):
        for j in range(5):
            node = 5 * i + j

            def grad(strain, along_z, comp, scale):
                row = strain_row(strain, node)
                for other in range(5):
                    xi, eta = (2, 3) if along_z else (0, 1)
                    parts[xi, row, node_row(comp, other, j)] += scale * deriv[i, other]
                    parts[eta, row, node_row(comp, i, other)] += scale * deriv[j, other]

            def radial(strain, comp, azimuthal, scale):
                row = strain_row(strain, node)
                parts[4, row, NODES * azimuthal + node_row(comp, i, j)] += scale / 1024.0

            grad(0, False, 0, 1.0)
            grad(1, True, 2, 1.0)
            radial(2, 1, 1, 1.0)
            radial(2, 0, 0, 1.0)
            grad(3, True, 0, half)
            grad(3, False, 2, half)
            radial(4, 0, 1, half)
            radial(4, 1, 0, -half)
            grad(4, False, 1, half)
            radial(5, 2, 1, half)
            grad(5, True, 1, half)
            for strain in range(6):
                place_of[0, strain_row(strain, node), i] = 1.0
                place_of[1, strain_row(strain, node), j] = 1.0
    parts[:, 150] = parts[:, 144] + parts[:, 145] + parts[:, 146]
    place_of[:, 150, 4] = 1.0
    return parts.astype(np.float32), place_of.astype(np.float32)


def sample_tables():
    order = np.arange(LANES)[:, None]
    table = np.zeros((RADIX, 2 * LANES, LANES))
    for k0 in range(RADIX):
        angle = 2.0 * math.pi * (order * (16 * np.arange(LANES)[None, :] + k0) % WIDTH) / WIDTH
        table[k0, :LANES] = np.cos(angle)
        table[k0, LANES:] = -np.sin(angle)
    return (
        table.astype(ml_dtypes.bfloat16),
        np.ascontiguousarray(table.transpose(0, 2, 1)).astype(ml_dtypes.bfloat16),
    )


def lane_shuffle():
    shuffle = np.zeros((LANES, LANES))
    for t in range(8):
        for k0 in range(16):
            shuffle[16 * t + k0, 8 * k0 + t] = 1.0
    return shuffle.astype(ml_dtypes.bfloat16)


def face(fixed_i, fixed_j):
    return [(fixed_i, n) if fixed_j is None else (n, fixed_j) for n in range(5)]


def message_row(comp, n):
    return 12 + comp if n == 4 else 4 * comp + n


def pick(faces):
    select = np.zeros((16 * len(faces), NODES))
    for index, nodes in enumerate(faces):
        for comp in range(3):
            for n, (i, j) in enumerate(nodes):
                select[16 * index + message_row(comp, n), node_row(comp, i, j)] = 1.0
    return select


ROW_LOW, ROW_HIGH = face(0, None), face(4, None)
COL_LOW, COL_HIGH = face(None, 0), face(None, 4)


def outgoing_select():
    even = pick([ROW_HIGH, ROW_LOW, COL_HIGH, COL_LOW])
    odd = pick([ROW_LOW, ROW_HIGH, COL_HIGH, COL_LOW])
    return np.stack([even, odd]).astype(ml_dtypes.bfloat16)


def column_select():
    out = np.zeros((4, 32, 64))
    for par_c in range(2):
        faces = [ROW_HIGH, ROW_LOW] if par_c == 0 else [ROW_LOW, ROW_HIGH]
        arrive = pick(faces).T
        full = np.concatenate([pick([COL_HIGH]), pick([COL_LOW])], axis=0)
        whole = np.concatenate([np.eye(32), full @ arrive], axis=1)
        for par_d in range(2):
            out[2 * par_c + par_d] = whole if par_d == 0 else np.roll(whole, 16, axis=0)
    return out.astype(ml_dtypes.bfloat16)


def arrival_select():
    out = np.zeros((4, NODES, 64))
    for par_c in range(2):
        rows = [ROW_HIGH, ROW_LOW] if par_c == 0 else [ROW_LOW, ROW_HIGH]
        for par_d in range(2):
            cols = [COL_HIGH, COL_LOW] if par_d == 0 else [COL_LOW, COL_HIGH]
            out[2 * par_c + par_d] = pick(rows + cols).T
    return out.astype(ml_dtypes.bfloat16)


def turned(value, eighths, scale_sign):
    re, im = value
    eighths = (scale_sign * eighths) % 16
    if eighths == 0:
        return re, im
    if eighths == 4:
        return -im, re
    if eighths == 8:
        return -re, -im
    if eighths == 12:
        return im, -re
    root = math.sqrt(0.5)
    if eighths == 2:
        return (re - im) * root, (im + re) * root
    if eighths == 14:
        return (re + im) * root, (im - re) * root
    cosine = math.cos(2.0 * math.pi * eighths / 16)
    sine = math.sin(2.0 * math.pi * eighths / 16)
    return re * cosine - im * sine, im * cosine + re * sine


def add(left, right):
    return left[0] + right[0], left[1] + right[1]


def sub(left, right):
    return left[0] - right[0], left[1] - right[1]


def transform(values, sign):
    count = len(values)
    if count == 1:
        return values
    even = transform(values[0::2], sign)
    odd = transform(values[1::2], sign)
    odd = [turned(value, q * (16 // count), sign) for q, value in enumerate(odd)]
    return [add(a, b) for a, b in zip(even, odd)] + [sub(a, b) for a, b in zip(even, odd)]


def spread(blocks):
    even = transform(blocks, 1)
    odd = transform([turned(value, b, 1) for b, value in enumerate(blocks)], 1)
    return [value for pair in zip(even, odd) for value in pair]


def gathered(values):
    even = transform(values[0::2], -1)
    odd = transform(values[1::2], -1)
    return [add(a, turned(b, index, -1)) for index, (a, b) in enumerate(zip(even, odd))]


def block(index, part):
    return slice(2 * LANES * index + LANES * part, 2 * LANES * index + LANES * (part + 1))


def orders(index):
    lane = lax.broadcasted_iota(jnp.int32, (1, LANES), 1)
    return (lane + LANES * index).astype(F32)


def dot(left, right):
    return jnp.dot(left, right, preferred_element_type=F32)


def node_column(scalar, rows):
    row = lax.broadcasted_iota(jnp.int32, (len(rows), 1), 0)
    column = jnp.zeros((len(rows), 1), F32)
    for value in sorted(set(rows)):
        chosen = functools.reduce(jnp.logical_or, [row == at for at, held in enumerate(rows) if held == value])
        column = jnp.where(chosen, scalar(value), column)
    return column


def own_rows(ref, lanes):
    return jnp.concatenate([ref[c, i, :, lanes] for c in range(3) for i in range(4)], axis=0)


def first_kernel(blocks_hbm, mass_hbm, disp_hbm, row_out, col_out, corner_out, blocks_ref, mass_ref, disp_ref, sems):
    loads = [
        pltpu.make_async_copy(source, target, sems.at[n])
        for n, (source, target) in enumerate(
            ((blocks_hbm, blocks_ref), (mass_hbm, mass_ref), (disp_hbm, disp_ref))
        )
    ]
    for load in loads:
        load.start()
    for load in loads:
        load.wait()
    faces = (
        (row_out, [(0, n) for n in range(4)]),
        (col_out, [(n, 0) for n in range(4)]),
        (corner_out, [(0, 0)]),
    )
    for out, rows in faces:
        live = node_column(lambda at: blocks_ref[at[0], at[1]].astype(F32), rows)
        mass = node_column(lambda at: mass_ref[at[0], at[1]], rows)
        high = mass.astype(BF16).astype(F32)
        lane = lax.broadcasted_iota(jnp.int32, (len(rows), LANES), 1)
        info = jnp.where(lane == 0, high, jnp.where(lane == 1, mass - high, jnp.where(lane == 2, live, 0.0)))
        for c in range(3):
            for index in range(8):
                lanes = slice(256 * index, 256 * (index + 1))
                if out is row_out:
                    value = disp_ref[c, 0, :, lanes]
                elif out is col_out:
                    value = jnp.concatenate([disp_ref[c, n, 0:1, lanes] for n in range(4)], axis=0)
                else:
                    value = disp_ref[c, 0, 0:1, lanes]
                out[c, :, lanes] = jnp.where(live > index, value, 0.0).astype(BF16)
            out[c, :, WIDTH:] = info.astype(BF16)


def exact_dot(left, right):
    return jnp.dot(left, right, preferred_element_type=F32, precision=lax.Precision.HIGHEST)


def packed_constants():
    _, place_of = strain_terms()
    pieces = {"shuffle": lane_shuffle()[None], "place": place_of, "outgoing": outgoing_select()}
    pieces.update(column=column_select(), arrival=arrival_select())
    rows, starts = [], {}
    for name, piece in pieces.items():
        starts[name] = sum(map(len, rows))
        for matrix in np.asarray(piece, np.float32):
            padded = np.zeros((-(-matrix.shape[0] // 16) * 16, LANES), np.float32)
            padded[: matrix.shape[0], : matrix.shape[1]] = matrix
            rows.append(padded)
    return np.concatenate(rows).astype(ml_dtypes.bfloat16), starts


def prepare_kernel(
    starts, place, blocks_ref, mass_ref, disp_ref, prev_ref, diag_ref, off_ref, radius_ref, lambda_ref, mu_ref,
    parts_ref, packed_ref,
    operator_out, back_out, material_out, own_out, free_out, info_out, outgoing_out, column_out, arrival_out,
    shuffled,
):
    operator = jnp.zeros((STRAINS, 2 * NODES), F32)
    first = starts["place"]
    at_i = packed_ref[first : first + 160, :5].astype(F32)[:STRAINS]
    at_j = packed_ref[first + 160 : first + 320, :5].astype(F32)[:STRAINS]
    terms = ((diag_ref, 0), (off_ref, 0), (off_ref, 5), (diag_ref, 5), (radius_ref, 0))
    for term, (ref, row) in enumerate(terms):
        factor = jnp.concatenate([ref[row + i] for i in range(5)], axis=0)
        spread_i = exact_dot(at_i, factor) * at_j
        operator = operator + parts_ref[term] * exact_dot(spread_i, jnp.ones((5, 2 * NODES), F32))
    operator_out[...] = operator.astype(BF16)
    back_out[...] = operator.T.astype(BF16)

    nodes = [(i, j) for i in range(4) for j in range(4)]
    live = jnp.concatenate([node_column(lambda at: blocks_ref[at[0], at[1]].astype(F32), nodes)] * 3, axis=0)
    mass = jnp.concatenate([node_column(lambda at: mass_ref[at[0], at[1]], nodes)] * 3, axis=0)
    lane = lax.broadcasted_iota(jnp.int32, (OWN, LANES), 1)
    info_out[:OWN] = jnp.where(lane == 0, mass, jnp.where(lane == 1, live, 0.0))
    lane = lax.broadcasted_iota(jnp.int32, (8, LANES), 1)
    rests = jnp.where(lane == 0, place[2].astype(F32), jnp.where(lane == 1, place[3].astype(F32), 0.0))
    info_out[OWN:] = rests
    for index in range(8):
        lanes = slice(256 * index, 256 * (index + 1))
        value = jnp.where(live > index, own_rows(disp_ref, lanes), 0.0)
        own_out[:, lanes] = value
        free_out[:, lanes] = jnp.where(live > index, 2.0 * value - own_rows(prev_ref, lanes), 0.0)

    def packed(name, index, rows, columns):
        first = pl.multiple_of(starts[name] + index * rows, 16)
        return packed_ref[pl.ds(first, rows), :columns]

    outgoing_out[...] = packed("outgoing", place[0], 64, NODES)
    column_out[...] = packed("column", 2 * place[0] + place[1], 32, 64)
    arrival_out[...] = packed("arrival", 2 * place[0] + place[1], NODES, 64)
    shuffle = packed_ref[starts["shuffle"] : starts["shuffle"] + LANES]

    for which, (ref, factor) in enumerate(((lambda_ref, 1.0), (mu_ref, 2.0))):
        value = ref[...] * factor
        high = value.astype(BF16)
        low = (value - high.astype(F32)).astype(BF16)
        shuffled[which] = dot(high, shuffle) + dot(low, shuffle)
    group = lax.broadcasted_iota(jnp.int32, (8, LANES), 1) // 8
    row = lax.broadcasted_iota(jnp.int32, (8, LANES), 0)
    for rows in range(7):
        held = []
        for s in range(16):
            if rows < 6:
                value = shuffled[rows // 3, pl.ds(128 * (rows % 3) + s, 8, stride=16), :]
            else:
                at = slice(384 + s, 385 + s)
                value = jnp.where(row < 6, shuffled[1, at], jnp.where(row == 6, shuffled[0, at], 0.0))
            held.append(value if s == 0 else pltpu.roll(value, 8 * s, 1))
        held = [held[(16 - index) % 16] for index in range(16)]
        for bit in range(4):
            chosen = (group >> bit) % 2 == 1
            held = [jnp.where(chosen, held[(index - (1 << bit)) % 16], held[index]) for index in range(16)]
        for index in range(16):
            value = held[index] if index == 0 else pltpu.roll(held[index], LANES - 8 * index, 1)
            material_out[index, 8 * rows : 8 * rows + 8] = value


def forces(nodes, operator_ref, back_ref, table_ref, tback_ref, material_ref, both, strain, spectrum, emit):
    for index in range(8):
        order = orders(index)
        re = nodes(block(index, 0))
        im = nodes(block(index, 1))
        both[:NODES, block(index, 0)] = re.astype(BF16)
        both[:NODES, block(index, 1)] = im.astype(BF16)
        both[NODES:, block(index, 0)] = (im * (-order)).astype(BF16)
        both[NODES:, block(index, 1)] = (re * order).astype(BF16)
        lanes = slice(256 * index, 256 * (index + 1))
        strain[:, lanes] = dot(operator_ref[...], both[:, lanes])

    for group in range(STRAINS // 8):
        rows = slice(8 * group, 8 * group + 8)
        values = [(strain[rows, block(b, 0)], strain[rows, block(b, 1)]) for b in range(8)]
        for k0, (re, im) in enumerate(spread(values)):
            spectrum[k0, rows, :LANES] = re
            spectrum[k0, rows, LANES:] = im

    for k0 in range(RADIX):
        sample = dot(spectrum[k0].astype(BF16), table_ref[k0])
        lam, mu, last = material_ref[k0, :24], material_ref[k0, 24:48], material_ref[k0, 48:]
        parts = [sample[24 * s : 24 * s + 24] for s in range(6)]
        volume = lam * (parts[0] + parts[1] + parts[2])
        stress = [volume + mu * part for part in parts[:3]] + [mu * part for part in parts[3:]]
        stress.append(last * sample[144:])
        stress = jnp.concatenate(stress, axis=0).astype(BF16)
        spectrum[k0] = dot(stress, tback_ref[k0])

    for group in range(STRAINS // 8):
        rows = slice(8 * group, 8 * group + 8)
        values = [(spectrum[k0, rows, :LANES], spectrum[k0, rows, LANES:]) for k0 in range(RADIX)]
        for b, (re, im) in enumerate(gathered(values)):
            strain[rows, block(b, 0)] = re
            strain[rows, block(b, 1)] = im

    for index in range(8):
        lanes = slice(256 * index, 256 * (index + 1))
        order = orders(index)
        pulled = dot(back_ref[...], strain[:, lanes].astype(BF16))
        re = pulled[:NODES, :LANES] + order * pulled[NODES:, LANES:]
        im = pulled[:NODES, LANES:] - order * pulled[NODES:, :LANES]
        emit(index, re, im)


def step_one_kernel(
    own_ref, free_ref, info_ref, col_ref, corner_ref, row_ref,
    operator_ref, back_ref, table_ref, tback_ref, material_ref, select_ref,
    sum_ref, pair_ref, side_ref, faces_ref,
    tiles, both, strain, spectrum,
):
    rest_c, rest_d = info_ref[OWN : OWN + 1, 0:1], info_ref[OWN : OWN + 1, 1:2]
    for lanes in [slice(256 * n, 256 * (n + 1)) for n in range(8)] + [slice(WIDTH, WIDTH + LANES)]:
        rows = [row_ref[c, :, lanes].astype(F32) * rest_c for c in range(3)]
        corner = [corner_ref[c, :, lanes].astype(F32) * (rest_c * rest_d) for c in range(3)]
        cols = [col_ref[c, :, lanes].astype(F32) * rest_d for c in range(3)]
        width = lanes.stop - lanes.start
        pieces = rows + corner + [jnp.zeros((1, width), F32)] + cols + [jnp.zeros((4, width), F32)]
        tiles[:, lanes] = jnp.concatenate(pieces, axis=0)
    info = tiles[:, WIDTH:]
    lane = lax.broadcasted_iota(jnp.int32, (32, LANES), 1)
    sum_ref[:OWN, WIDTH:] = info_ref[:OWN]
    sum_ref[OWN:, WIDTH:] = jnp.where(
        lane == 0, info[:, 0:1] + info[:, 1:2], jnp.where(lane == 1, info[:, 2:3], 0.0)
    )
    mass = sum_ref[:, WIDTH : WIDTH + 1] * (-1.0 / WIDTH)

    def nodes(lanes):
        return jnp.concatenate([own_ref[:, lanes], tiles[:, lanes]], axis=0)

    def emit(index, re, im):
        for part, value in ((0, re), (1, im)):
            lanes = block(index, part)
            value = mass * value
            sum_ref[:OWN, lanes] = free_ref[:, lanes] + value[:OWN]
            sum_ref[OWN:, lanes] = value[OWN:]
        lanes = slice(256 * index, 256 * (index + 1))
        sent = dot(select_ref[...], sum_ref[:, lanes].astype(BF16)).astype(BF16)
        pair_ref[:, lanes] = sent[:16]
        side_ref[:, lanes] = sent[16:32]
        faces_ref[:, lanes] = sent[32:]

    forces(nodes, operator_ref, back_ref, table_ref, tback_ref, material_ref, both, strain, spectrum, emit)


def column_kernel(faces_ref, side_ref, pair_ref, select_ref, side_out, pair_out):
    for index in range(8):
        lanes = slice(256 * index, 256 * (index + 1))
        stacked = jnp.concatenate([faces_ref[:, lanes], pair_ref[:, lanes], side_ref[:, lanes]], axis=0)
        sent = dot(select_ref[...], stacked).astype(BF16)
        pair_out[:, lanes] = sent[:16]
        side_out[:, lanes] = sent[16:]


def step_two_kernel(
    own_ref, sum_ref, cside_ref, cpair_ref, dside_ref, dpair_ref,
    operator_ref, back_ref, table_ref, tback_ref, material_ref, select_ref,
    mid_ref, sum_out, row_out, col_out, corner_out,
    current, both, strain, spectrum,
):
    live = sum_ref[:, WIDTH + 1 : WIDTH + 2]
    for index in range(8):
        lanes = slice(256 * index, 256 * (index + 1))
        arrived = jnp.concatenate([ref[:, lanes] for ref in (cpair_ref, cside_ref, dpair_ref, dside_ref)], axis=0)
        value = jnp.where(live > index, sum_ref[:, lanes] + dot(select_ref[...], arrived), 0.0)
        current[:, lanes] = value
        mid_ref[:, lanes] = value[:OWN]
    mass = sum_ref[:, WIDTH : WIDTH + 1] * (-1.0 / WIDTH)

    def emit(index, re, im):
        masked = jnp.where(live > index, mass, 0.0)
        for part, value in ((0, re), (1, im)):
            lanes = block(index, part)
            value = masked * value
            total = 2.0 * current[:OWN, lanes] - own_ref[:, lanes] + value[:OWN]
            value = value.astype(BF16)
            for c in range(3):
                for i in range(4):
                    at = 16 * c + 4 * i
                    sum_out[c, i, :, lanes] = total[at : at + 4]
                at = OWN + 4 * c
                row_out[c, :, lanes] = value[at : at + 4]
                corner_out[c, :, lanes] = value[OWN + 12 + c : OWN + 13 + c]
                col_out[c, :, lanes] = value[at + 16 : at + 20]

    forces(
        lambda lanes: current[:, lanes],
        operator_ref, back_ref, table_ref, tback_ref, material_ref, both, strain, spectrum, emit,
    )


def last_kernel(sum_ref, col_ref, corner_ref, row_ref, out_ref):
    first = lax.broadcasted_iota(jnp.int32, (4, 1), 0) == 0
    for c in range(3):
        for i in range(4):
            arrived = col_ref[c, i : i + 1].astype(F32)
            if i == 0:
                arrived = arrived + corner_ref[c].astype(F32)
            value = sum_ref[c, i] + jnp.where(first, arrived, 0.0)
            if i == 0:
                value = value + row_ref[c].astype(F32)
            out_ref[c, i] = value


def call(kernel, outs, scratch=(), scalars=0, inputs=0, flops=0, far=0, vmem=VMEM_LIMIT):
    near = pl.BlockSpec(memory_space=pltpu.VMEM)
    return pl.pallas_call(
        kernel,
        out_shape=outs,
        in_specs=[pl.BlockSpec(memory_space=pltpu.HBM)] * far
        + [pl.BlockSpec(memory_space=pltpu.SMEM)] * scalars
        + [near] * inputs,
        out_specs=jax.tree.map(lambda _: near, outs),
        scratch_shapes=list(scratch),
        compiler_params=pltpu.CompilerParams(vmem_limit_bytes=vmem),
        cost_estimate=pl.CostEstimate(flops=flops, bytes_accessed=1 << 20, transcendentals=0),
    )


def shape(*dims, dtype=F32):
    return jax.ShapeDtypeStruct(dims, dtype)


def solution(mesh):
    bands, layers = mesh.shape["colat"], mesh.shape["depth"]
    parts, _ = strain_terms()
    packed, starts = packed_constants()
    table, tback = sample_tables()

    def target(c, d, by_c, by_d):
        past = not 0 <= d + by_d < layers
        return (c + by_c + past * (bands // 2)) % bands * layers + (d + by_d) % layers

    def shifted(array, by_c, by_d):
        pairs = [(c * layers + d, target(c, d, by_c, by_d)) for c in range(bands) for d in range(layers)]
        return lax.ppermute(array, ("colat", "depth"), pairs)

    def swapped(array, axis, odd):
        along_c = axis == "colat"
        pairs = []
        for c in range(bands):
            for d in range(layers):
                step = 1 if (c if along_c else d) % 2 == odd else -1
                pairs.append((c * layers + d, target(c, d, step * along_c, step * (not along_c))))
        return lax.ppermute(array, ("colat", "depth"), pairs)

    def per_device(displacement, previous, node_blocks, inverse_mass, jac_diag, jac_off, inv_radius, lame_l, lame_m):
        at_c, at_d = lax.axis_index("colat"), lax.axis_index("depth")
        place = jnp.stack([at_c % 2, at_d % 2, at_c < bands - 1, at_d < layers - 1]).astype(jnp.int32)
        row_face = shape(3, 4, WIDTH + LANES, dtype=BF16)
        point = shape(3, 1, WIDTH + LANES, dtype=BF16)
        row, col, corner = call(
            first_kernel,
            (row_face, row_face, point),
            [
                pltpu.SMEM((4, 4), jnp.int32),
                pltpu.SMEM((4, 4), F32),
                pltpu.VMEM((3, 4, 4, WIDTH), F32),
                pltpu.SemaphoreType.DMA((3,)),
            ],
            far=3, flops=2 * 10**11, vmem=62 * 1024 * 1024,
        )(node_blocks, inverse_mass, displacement)
        col = shifted(col, 0, -1)
        corner = shifted(corner, -1, -1)
        row = shifted(row, -1, 0)

        operator, back, material, own, free, info, outgoing, column, arrival = call(
            functools.partial(prepare_kernel, starts),
            (
                shape(STRAINS, 2 * NODES, dtype=BF16),
                shape(2 * NODES, STRAINS, dtype=BF16),
                shape(RADIX, 56, LANES),
                shape(OWN, WIDTH),
                shape(OWN, WIDTH),
                shape(OWN + 8, LANES),
                shape(64, NODES, dtype=BF16),
                shape(32, 64, dtype=BF16),
                shape(NODES, 64, dtype=BF16),
            ),
            [pltpu.VMEM((2, 400, LANES), F32)],
            scalars=3, inputs=9, flops=10**9,
        )(
            place, node_blocks, inverse_mass, displacement, previous,
            jac_diag.reshape(10, 1, 5), jac_off.reshape(10, 1, 5), inv_radius.reshape(5, 1, 5),
            lame_l.reshape(400, LANES), lame_m.reshape(400, LANES), jnp.asarray(parts), jnp.asarray(packed),
        )

        work = [
            pltpu.VMEM((2 * NODES, WIDTH), BF16),
            pltpu.VMEM((STRAINS, WIDTH), F32),
            pltpu.VMEM((RADIX, STRAINS, 2 * LANES), F32),
        ]
        tile = shape(16, WIDTH, dtype=BF16)
        shared = (operator, back, jnp.asarray(table), jnp.asarray(tback), material)
        total, pair, side, faces = call(
            step_one_kernel,
            (shape(NODES, WIDTH + LANES), tile, tile, shape(32, WIDTH, dtype=BF16)),
            [pltpu.VMEM((32, WIDTH + LANES), F32)] + work,
            inputs=12, flops=10**9,
        )(own, free, info, col, corner, row, *shared, outgoing)
        cside = swapped(side, "colat", 1)
        cpair = swapped(pair, "colat", 0)
        side, pair = call(column_kernel, (tile, tile), inputs=4)(faces, cside, cpair, column)
        dside = swapped(side, "depth", 1)
        dpair = swapped(pair, "depth", 0)
        row_face = shape(3, 4, WIDTH, dtype=BF16)
        middle, final, row, col, corner = call(
            step_two_kernel,
            (
                shape(OWN, WIDTH), shape(3, 4, 4, WIDTH), row_face, row_face,
                shape(3, 1, WIDTH, dtype=BF16),
            ),
            [pltpu.VMEM((NODES, WIDTH), F32)] + work,
            inputs=12, flops=10**9,
        )(own, total, cside, cpair, dside, dpair, *shared, arrival)
        col = shifted(col, 0, 1)
        corner = shifted(corner, 1, 1)
        row = shifted(row, 1, 0)
        final = call(last_kernel, shape(3, 4, 4, WIDTH), inputs=4)(final, col, corner, row)
        return middle.reshape(displacement.shape), final

    return jax.shard_map(
        per_device,
        mesh=mesh,
        in_specs=(
            P(None, "colat", "depth", None),
            P(None, "colat", "depth", None),
            P("colat", "depth"),
            P("colat", "depth"),
            P(None, "colat", None, "depth", None),
            P(None, "colat", None, "depth", None),
            P("colat", None, "depth", None),
            P("colat", None, "depth", None, None),
            P("colat", None, "depth", None, None),
        ),
        out_specs=(P(None, "colat", "depth", None), P(None, "colat", "depth", None)),
        check_vma=False,
    )
```

```python
import functools
import math

import jax
import jax.numpy as jnp
import ml_dtypes
import numpy as np
from jax import lax
from jax.experimental import pallas as pl
from jax.experimental.pallas import tpu as pltpu
from jax.sharding import PartitionSpec as P

BF16 = jnp.bfloat16
F32 = jnp.float32
WIDTH = 2048
LANES = 128
RADIX = 16
OWN = 48
NODES = 80
STRAINS = 152
VMEM_LIMIT = 40 * 1024 * 1024


def gll_derivative():
    points = np.array([-1.0, -math.sqrt(3.0 / 7.0), 0.0, math.sqrt(3.0 / 7.0), 1.0])
    weights = np.ones(5)
    for row in range(5):
        for col in range(5):
            if row != col:
                weights[row] /= points[row] - points[col]
    matrix = np.zeros((5, 5))
    for row in range(5):
        for col in range(5):
            if row != col:
                matrix[row, col] = weights[col] / weights[row] / (points[row] - points[col])
        matrix[row, row] = -np.sum(matrix[row])
    return matrix


def node_row(comp, i, j):
    if i == 4:
        return OWN + (12 + comp if j == 4 else 4 * comp + j)
    if j == 4:
        return OWN + 16 + 4 * comp + i
    return 16 * comp + 4 * i + j


def strain_row(strain, node):
    return 24 * strain + node if node < 24 else 144 + strain


def strain_terms():
    deriv = gll_derivative()
    parts = np.zeros((5, STRAINS, 2 * NODES))
    place_of = np.zeros((2, STRAINS, 5))
    half = math.sqrt(0.5)
    for i in range(5):
        for j in range(5):
            node = 5 * i + j

            def grad(strain, along_z, comp, scale):
                row = strain_row(strain, node)
                for other in range(5):
                    xi, eta = (2, 3) if along_z else (0, 1)
                    parts[xi, row, node_row(comp, other, j)] += scale * deriv[i, other]
                    parts[eta, row, node_row(comp, i, other)] += scale * deriv[j, other]

            def radial(strain, comp, azimuthal, scale):
                row = strain_row(strain, node)
                parts[4, row, NODES * azimuthal + node_row(comp, i, j)] += scale / 1024.0

            grad(0, False, 0, 1.0)
            grad(1, True, 2, 1.0)
            radial(2, 1, 1, 1.0)
            radial(2, 0, 0, 1.0)
            grad(3, True, 0, half)
            grad(3, False, 2, half)
            radial(4, 0, 1, half)
            radial(4, 1, 0, -half)
            grad(4, False, 1, half)
            radial(5, 2, 1, half)
            grad(5, True, 1, half)
            for strain in range(6):
                place_of[0, strain_row(strain, node), i] = 1.0
                place_of[1, strain_row(strain, node), j] = 1.0
    parts[:, 150] = parts[:, 144] + parts[:, 145] + parts[:, 146]
    place_of[:, 150, 4] = 1.0
    return parts.astype(np.float32), place_of.astype(np.float32)


def sample_tables():
    order = np.arange(LANES)[:, None]
    table = np.zeros((RADIX, 2 * LANES, LANES))
    for k0 in range(RADIX):
        angle = 2.0 * math.pi * (order * (16 * np.arange(LANES)[None, :] + k0) % WIDTH) / WIDTH
        table[k0, :LANES] = np.cos(angle)
        table[k0, LANES:] = -np.sin(angle)
    return (
        table.astype(ml_dtypes.bfloat16),
        np.ascontiguousarray(table.transpose(0, 2, 1)).astype(ml_dtypes.bfloat16),
    )


def lane_shuffle():
    shuffle = np.zeros((LANES, LANES))
    for t in range(8):
        for k0 in range(16):
            shuffle[16 * t + k0, 8 * k0 + t] = 1.0
    return shuffle.astype(ml_dtypes.bfloat16)


def face(fixed_i, fixed_j):
    return [(fixed_i, n) if fixed_j is None else (n, fixed_j) for n in range(5)]


def message_row(comp, n):
    return 12 + comp if n == 4 else 4 * comp + n


def pick(faces):
    select = np.zeros((16 * len(faces), NODES))
    for index, nodes in enumerate(faces):
        for comp in range(3):
            for n, (i, j) in enumerate(nodes):
                select[16 * index + message_row(comp, n), node_row(comp, i, j)] = 1.0
    return select


ROW_LOW, ROW_HIGH = face(0, None), face(4, None)
COL_LOW, COL_HIGH = face(None, 0), face(None, 4)


def outgoing_select():
    even = pick([ROW_HIGH, ROW_LOW, COL_HIGH, COL_LOW])
    odd = pick([ROW_LOW, ROW_HIGH, COL_HIGH, COL_LOW])
    return np.stack([even, odd]).astype(ml_dtypes.bfloat16)


def column_select():
    out = np.zeros((4, 32, 64))
    for par_c in range(2):
        faces = [ROW_HIGH, ROW_LOW] if par_c == 0 else [ROW_LOW, ROW_HIGH]
        arrive = pick(faces).T
        full = np.concatenate([pick([COL_HIGH]), pick([COL_LOW])], axis=0)
        whole = np.concatenate([np.eye(32), full @ arrive], axis=1)
        for par_d in range(2):
            out[2 * par_c + par_d] = whole if par_d == 0 else np.roll(whole, 16, axis=0)
    return out.astype(ml_dtypes.bfloat16)


def arrival_select():
    out = np.zeros((4, NODES, 64))
    for par_c in range(2):
        rows = [ROW_HIGH, ROW_LOW] if par_c == 0 else [ROW_LOW, ROW_HIGH]
        for par_d in range(2):
            cols = [COL_HIGH, COL_LOW] if par_d == 0 else [COL_LOW, COL_HIGH]
            out[2 * par_c + par_d] = pick(rows + cols).T
    return out.astype(ml_dtypes.bfloat16)


def turned(value, eighths, scale_sign):
    re, im = value
    eighths = (scale_sign * eighths) % 16
    if eighths == 0:
        return re, im
    if eighths == 4:
        return -im, re
    if eighths == 8:
        return -re, -im
    if eighths == 12:
        return im, -re
    root = math.sqrt(0.5)
    if eighths == 2:
        return (re - im) * root, (im + re) * root
    if eighths == 14:
        return (re + im) * root, (im - re) * root
    cosine = math.cos(2.0 * math.pi * eighths / 16)
    sine = math.sin(2.0 * math.pi * eighths / 16)
    return re * cosine - im * sine, im * cosine + re * sine


def add(left, right):
    return left[0] + right[0], left[1] + right[1]


def sub(left, right):
    return left[0] - right[0], left[1] - right[1]


def transform(values, sign):
    count = len(values)
    if count == 1:
        return values
    even = transform(values[0::2], sign)
    odd = transform(values[1::2], sign)
    odd = [turned(value, q * (16 // count), sign) for q, value in enumerate(odd)]
    return [add(a, b) for a, b in zip(even, odd)] + [sub(a, b) for a, b in zip(even, odd)]


def spread(blocks):
    even = transform(blocks, 1)
    odd = transform([turned(value, b, 1) for b, value in enumerate(blocks)], 1)
    return [value for pair in zip(even, odd) for value in pair]


def gathered(values):
    even = transform(values[0::2], -1)
    odd = transform(values[1::2], -1)
    return [add(a, turned(b, index, -1)) for index, (a, b) in enumerate(zip(even, odd))]


def block(index, part):
    return slice(2 * LANES * index + LANES * part, 2 * LANES * index + LANES * (part + 1))


def orders(index):
    lane = lax.broadcasted_iota(jnp.int32, (1, LANES), 1)
    return (lane + LANES * index).astype(F32)


def dot(left, right):
    return jnp.dot(left, right, preferred_element_type=F32)


def node_column(scalar, rows):
    row = lax.broadcasted_iota(jnp.int32, (len(rows), 1), 0)
    column = jnp.zeros((len(rows), 1), F32)
    for value in sorted(set(rows)):
        chosen = functools.reduce(jnp.logical_or, [row == at for at, held in enumerate(rows) if held == value])
        column = jnp.where(chosen, scalar(value), column)
    return column


def own_rows(ref, lanes):
    return jnp.concatenate([ref[c, i, :, lanes] for c in range(3) for i in range(4)], axis=0)


def first_kernel(blocks_hbm, mass_hbm, disp_hbm, row_out, col_out, corner_out, blocks_ref, mass_ref, disp_ref, sems):
    loads = [
        pltpu.make_async_copy(source, target, sems.at[n])
        for n, (source, target) in enumerate(
            ((blocks_hbm, blocks_ref), (mass_hbm, mass_ref), (disp_hbm, disp_ref))
        )
    ]
    for load in loads:
        load.start()
    for load in loads:
        load.wait()
    faces = (
        (row_out, [(0, n) for n in range(4)]),
        (col_out, [(n, 0) for n in range(4)]),
        (corner_out, [(0, 0)]),
    )
    for out, rows in faces:
        live = node_column(lambda at: blocks_ref[at[0], at[1]].astype(F32), rows)
        mass = node_column(lambda at: mass_ref[at[0], at[1]], rows)
        high = mass.astype(BF16).astype(F32)
        lane = lax.broadcasted_iota(jnp.int32, (len(rows), LANES), 1)
        info = jnp.where(lane == 0, high, jnp.where(lane == 1, mass - high, jnp.where(lane == 2, live, 0.0)))
        for c in range(3):
            for index in range(8):
                lanes = slice(256 * index, 256 * (index + 1))
                if out is row_out:
                    value = disp_ref[c, 0, :, lanes]
                elif out is col_out:
                    value = jnp.concatenate([disp_ref[c, n, 0:1, lanes] for n in range(4)], axis=0)
                else:
                    value = disp_ref[c, 0, 0:1, lanes]
                out[c, :, lanes] = jnp.where(live > index, value, 0.0).astype(BF16)
            out[c, :, WIDTH:] = info.astype(BF16)


def exact_dot(left, right):
    return jnp.dot(left, right, preferred_element_type=F32, precision=lax.Precision.HIGHEST)


def packed_constants():
    parts, place_of = strain_terms()
    upper = np.zeros((3, STRAINS, 2 * LANES), np.float32)
    for term in range(4):
        upper[term // 2, :, NODES * (term % 2) : NODES * (term % 2 + 1)] = parts[term, :, :NODES]
    upper[2, :, : 2 * NODES] = parts[4]
    columns = (
        {"arrival": arrival_select(), "outgoing": outgoing_select()},
        {"shuffle": lane_shuffle()[None], "place": place_of, "column": column_select()},
    )
    lower, starts = np.zeros((3 * STRAINS + 560, 2 * LANES), np.float32), {}
    lower[: 3 * STRAINS] = upper.reshape(-1, 2 * LANES)
    for side, pieces in enumerate(columns):
        first = 3 * STRAINS
        for name, piece in pieces.items():
            starts[name] = (first, LANES * side)
            for matrix in np.asarray(piece, np.float32):
                rows, width = matrix.shape
                lower[first : first + rows, LANES * side : LANES * side + width] = matrix
                first += rows
    return lower, starts


def prepare_kernel(
    starts, place_ref, blocks_ref, mass_ref, disp_ref, prev_ref, diag_ref, off_ref, radius_ref, lambda_ref, mu_ref,
    packed_ref,
    operator_out, back_out, material_out, own_out, free_out, info_out, outgoing_out, column_out, arrival_out,
    shuffled,
):
    def constant(name, rows, columns, index=0):
        first, lane = starts[name]
        return packed_ref[first + rows * index : first + rows * (index + 1), lane : lane + columns]

    at_i, at_j = constant("place", STRAINS, 5), constant("place", STRAINS, 5, 1)
    factors = []
    for ref, row in ((diag_ref, 0), (off_ref, 0), (off_ref, 5), (diag_ref, 5), (radius_ref, 0)):
        factor = jnp.concatenate([ref[row + i] for i in range(5)], axis=0)
        spread_i = exact_dot(at_i, factor) * at_j
        factors.append(jnp.sum(spread_i, axis=1, keepdims=True))
    parts = [packed_ref[STRAINS * n : STRAINS * (n + 1)] for n in range(3)]
    operator = parts[2][:, : 2 * NODES] * factors[4]
    plain = sum(parts[t // 2][:, NODES * (t % 2) : NODES * (t % 2 + 1)] * factors[t] for t in range(4))
    operator = operator + jnp.concatenate([plain, jnp.zeros_like(plain)], axis=1)
    operator_out[...] = operator.astype(BF16)
    back_out[...] = operator.T.astype(BF16)

    def column(ref):
        shape = (4, 4)
        diagonal = lax.broadcasted_iota(jnp.int32, shape, 0) == lax.broadcasted_iota(jnp.int32, shape, 1)
        value = ref[...].astype(F32)
        pieces = [jnp.sum(jnp.where(diagonal, value[i : i + 1], 0.0), axis=1, keepdims=True) for i in range(4)]
        return jnp.concatenate(pieces * 3, axis=0)

    live, mass = column(blocks_ref), column(mass_ref)
    lane = lax.broadcasted_iota(jnp.int32, (OWN, LANES), 1)
    info_out[:OWN] = jnp.where(lane == 0, mass, jnp.where(lane == 1, live, 0.0))
    info_out[OWN:] = place_ref[...]
    for index in range(8):
        lanes = slice(256 * index, 256 * (index + 1))
        value = jnp.where(live > index, own_rows(disp_ref, lanes), 0.0)
        own_out[:, lanes] = value
        free_out[:, lanes] = jnp.where(live > index, 2.0 * value - own_rows(prev_ref, lanes), 0.0)

    def packed(name, rows, columns, *bits):
        pieces = [constant(name, rows, columns, index) for index in range(2 ** len(bits))]
        for bit in reversed(bits):
            pieces = [jnp.where(bit > 0.5, one, zero) for zero, one in zip(pieces[0::2], pieces[1::2])]
        return pieces[0]

    def kept(matrix, first, flag):
        column = lax.broadcasted_iota(jnp.int32, matrix.shape, 1)
        dropped = jnp.logical_and(jnp.logical_and(column >= first, column < first + 16), flag < 0.5)
        return jnp.where(dropped, 0.0, matrix)

    odd_c, odd_d, side_c, side_d = (place_ref[0:1, n : n + 1] for n in range(2, 6))
    outgoing_out[...] = packed("outgoing", 64, NODES, odd_c).astype(BF16)
    column_out[...] = kept(packed("column", 32, 64, odd_c, odd_d), 48, side_c).astype(BF16)
    arrived = kept(packed("arrival", NODES, 64, odd_c, odd_d), 16, side_c)
    arrival_out[...] = kept(arrived, 48, side_d).astype(BF16)
    shuffle = constant("shuffle", LANES, LANES).astype(BF16)

    for which, (ref, factor) in enumerate(((lambda_ref, 1.0), (mu_ref, 2.0))):
        value = ref[...] * factor
        high = value.astype(BF16)
        low = (value - high.astype(F32)).astype(BF16)
        shuffled[which] = dot(high, shuffle) + dot(low, shuffle)
    group = lax.broadcasted_iota(jnp.int32, (8, LANES), 1) // 8
    row = lax.broadcasted_iota(jnp.int32, (8, LANES), 0)
    for rows in range(7):
        held = []
        for s in range(16):
            if rows < 6:
                value = shuffled[rows // 3, pl.ds(128 * (rows % 3) + s, 8, stride=16), :]
            else:
                at = slice(384 + s, 385 + s)
                value = jnp.where(row < 6, shuffled[1, at], jnp.where(row == 6, shuffled[0, at], 0.0))
            held.append(value if s == 0 else pltpu.roll(value, 8 * s, 1))
        held = [held[(16 - index) % 16] for index in range(16)]
        for bit in range(4):
            chosen = (group >> bit) % 2 == 1
            held = [jnp.where(chosen, held[(index - (1 << bit)) % 16], held[index]) for index in range(16)]
        for index in range(16):
            value = held[index] if index == 0 else pltpu.roll(held[index], LANES - 8 * index, 1)
            material_out[index, 8 * rows : 8 * rows + 8] = value


def forces(nodes, operator_ref, back_ref, table_ref, tback_ref, material_ref, both, strain, spectrum, emit):
    for index in range(8):
        order = orders(index)
        re = nodes(block(index, 0))
        im = nodes(block(index, 1))
        both[:NODES, block(index, 0)] = re.astype(BF16)
        both[:NODES, block(index, 1)] = im.astype(BF16)
        both[NODES:, block(index, 0)] = (im * (-order)).astype(BF16)
        both[NODES:, block(index, 1)] = (re * order).astype(BF16)
        lanes = slice(256 * index, 256 * (index + 1))
        strain[:, lanes] = dot(operator_ref[...], both[:, lanes])

    for group in range(STRAINS // 8):
        rows = slice(8 * group, 8 * group + 8)
        values = [(strain[rows, block(b, 0)], strain[rows, block(b, 1)]) for b in range(8)]
        for k0, (re, im) in enumerate(spread(values)):
            spectrum[k0, rows, :LANES] = re
            spectrum[k0, rows, LANES:] = im

    for k0 in range(RADIX):
        sample = dot(spectrum[k0].astype(BF16), table_ref[k0])
        lam, mu, last = material_ref[k0, :24], material_ref[k0, 24:48], material_ref[k0, 48:]
        parts = [sample[24 * s : 24 * s + 24] for s in range(6)]
        volume = lam * (parts[0] + parts[1] + parts[2])
        stress = [volume + mu * part for part in parts[:3]] + [mu * part for part in parts[3:]]
        stress.append(last * sample[144:])
        stress = jnp.concatenate(stress, axis=0).astype(BF16)
        spectrum[k0] = dot(stress, tback_ref[k0])

    for group in range(STRAINS // 8):
        rows = slice(8 * group, 8 * group + 8)
        values = [(spectrum[k0, rows, :LANES], spectrum[k0, rows, LANES:]) for k0 in range(RADIX)]
        for b, (re, im) in enumerate(gathered(values)):
            strain[rows, block(b, 0)] = re
            strain[rows, block(b, 1)] = im

    for index in range(8):
        lanes = slice(256 * index, 256 * (index + 1))
        order = orders(index)
        pulled = dot(back_ref[...], strain[:, lanes].astype(BF16))
        re = pulled[:NODES, :LANES] + order * pulled[NODES:, LANES:]
        im = pulled[:NODES, LANES:] - order * pulled[NODES:, :LANES]
        emit(index, re, im)


def step_one_kernel(
    own_ref, free_ref, info_ref, col_ref, corner_ref, row_ref,
    operator_ref, back_ref, table_ref, tback_ref, material_ref, select_ref,
    sum_ref, pair_ref, side_ref, faces_ref,
    tiles, both, strain, spectrum,
):
    rest_c, rest_d = info_ref[OWN : OWN + 1, 0:1], info_ref[OWN : OWN + 1, 1:2]
    for lanes in [slice(256 * n, 256 * (n + 1)) for n in range(8)] + [slice(WIDTH, WIDTH + LANES)]:
        rows = [row_ref[c, :, lanes].astype(F32) * rest_c for c in range(3)]
        corner = [corner_ref[c, :, lanes].astype(F32) * (rest_c * rest_d) for c in range(3)]
        cols = [col_ref[c, :, lanes].astype(F32) * rest_d for c in range(3)]
        width = lanes.stop - lanes.start
        pieces = rows + corner + [jnp.zeros((1, width), F32)] + cols + [jnp.zeros((4, width), F32)]
        tiles[:, lanes] = jnp.concatenate(pieces, axis=0)
    info = tiles[:, WIDTH:]
    lane = lax.broadcasted_iota(jnp.int32, (32, LANES), 1)
    sum_ref[:OWN, WIDTH:] = info_ref[:OWN]
    sum_ref[OWN:, WIDTH:] = jnp.where(
        lane == 0, info[:, 0:1] + info[:, 1:2], jnp.where(lane == 1, info[:, 2:3], 0.0)
    )
    mass = sum_ref[:, WIDTH : WIDTH + 1] * (-1.0 / WIDTH)

    def nodes(lanes):
        return jnp.concatenate([own_ref[:, lanes], tiles[:, lanes]], axis=0)

    def emit(index, re, im):
        for part, value in ((0, re), (1, im)):
            lanes = block(index, part)
            value = mass * value
            sum_ref[:OWN, lanes] = free_ref[:, lanes] + value[:OWN]
            sum_ref[OWN:, lanes] = value[OWN:]
        lanes = slice(256 * index, 256 * (index + 1))
        sent = dot(select_ref[...], sum_ref[:, lanes].astype(BF16)).astype(BF16)
        pair_ref[:, lanes] = sent[:16]
        side_ref[:, lanes] = sent[16:32]
        faces_ref[:, lanes] = sent[32:]

    forces(nodes, operator_ref, back_ref, table_ref, tback_ref, material_ref, both, strain, spectrum, emit)


def column_kernel(faces_ref, side_ref, pair_ref, select_ref, side_out, pair_out):
    for index in range(8):
        lanes = slice(256 * index, 256 * (index + 1))
        stacked = jnp.concatenate([faces_ref[:, lanes], pair_ref[:, lanes], side_ref[:, lanes]], axis=0)
        sent = dot(select_ref[...], stacked).astype(BF16)
        pair_out[:, lanes] = sent[:16]
        side_out[:, lanes] = sent[16:]


def step_two_kernel(
    own_ref, sum_ref, cside_ref, cpair_ref, dside_ref, dpair_ref,
    operator_ref, back_ref, table_ref, tback_ref, material_ref, select_ref,
    mid_ref, sum_out, row_out, col_out, corner_out,
    current, both, strain, spectrum,
):
    live = sum_ref[:, WIDTH + 1 : WIDTH + 2]
    for index in range(8):
        lanes = slice(256 * index, 256 * (index + 1))
        arrived = jnp.concatenate([ref[:, lanes] for ref in (cpair_ref, cside_ref, dpair_ref, dside_ref)], axis=0)
        value = jnp.where(live > index, sum_ref[:, lanes] + dot(select_ref[...], arrived), 0.0)
        current[:, lanes] = value
        mid_ref[:, lanes] = value[:OWN]
    mass = sum_ref[:, WIDTH : WIDTH + 1] * (-1.0 / WIDTH)

    def emit(index, re, im):
        masked = jnp.where(live > index, mass, 0.0)
        for part, value in ((0, re), (1, im)):
            lanes = block(index, part)
            value = masked * value
            total = 2.0 * current[:OWN, lanes] - own_ref[:, lanes] + value[:OWN]
            value = value.astype(BF16)
            for c in range(3):
                for i in range(4):
                    at = 16 * c + 4 * i
                    sum_out[c, i, :, lanes] = total[at : at + 4]
                at = OWN + 4 * c
                row_out[c, :, lanes] = value[at : at + 4]
                corner_out[c, :, lanes] = value[OWN + 12 + c : OWN + 13 + c]
                col_out[c, :, lanes] = value[at + 16 : at + 20]

    forces(
        lambda lanes: current[:, lanes],
        operator_ref, back_ref, table_ref, tback_ref, material_ref, both, strain, spectrum, emit,
    )


def middle_kernel(rows_ref, out_ref):
    for c in range(3):
        for i in range(4):
            at = 16 * c + 4 * i
            out_ref[c, i] = rows_ref[at : at + 4]


def last_kernel(sum_ref, col_ref, corner_ref, row_ref, out_ref):
    first = lax.broadcasted_iota(jnp.int32, (4, 1), 0) == 0
    for c in range(3):
        for i in range(4):
            arrived = col_ref[c, i : i + 1].astype(F32)
            if i == 0:
                arrived = arrived + corner_ref[c].astype(F32)
            value = sum_ref[c, i] + jnp.where(first, arrived, 0.0)
            if i == 0:
                value = value + row_ref[c].astype(F32)
            out_ref[c, i] = value


def call(kernel, outs, scratch=(), scalars=0, inputs=0, flops=0, far=0, vmem=VMEM_LIMIT):
    near = pl.BlockSpec(memory_space=pltpu.VMEM)
    return pl.pallas_call(
        kernel,
        out_shape=outs,
        in_specs=[pl.BlockSpec(memory_space=pltpu.HBM)] * far
        + [pl.BlockSpec(memory_space=pltpu.SMEM)] * scalars
        + [near] * inputs,
        out_specs=jax.tree.map(lambda _: near, outs),
        scratch_shapes=list(scratch),
        compiler_params=pltpu.CompilerParams(vmem_limit_bytes=vmem),
        cost_estimate=pl.CostEstimate(flops=flops, bytes_accessed=1 << 20, transcendentals=0),
    )


def shape(*dims, dtype=F32):
    return jax.ShapeDtypeStruct(dims, dtype)


def solution(mesh):
    bands, layers = mesh.shape["colat"], mesh.shape["depth"]
    packed, starts = packed_constants()
    table, tback = sample_tables()

    def target(c, d, by_c, by_d):
        past = not 0 <= d + by_d < layers
        return (c + by_c + past * (bands // 2)) % bands * layers + (d + by_d) % layers

    def shifted(array, by_c, by_d):
        pairs = [(c * layers + d, target(c, d, by_c, by_d)) for c in range(bands) for d in range(layers)]
        return lax.ppermute(array, ("colat", "depth"), pairs)

    def swapped(array, axis, odd):
        along_c = axis == "colat"
        pairs = []
        for c in range(bands):
            for d in range(layers):
                step = 1 if (c if along_c else d) % 2 == odd else -1
                to_c, to_d = c + step * along_c, d + step * (not along_c)
                if not 0 <= to_c < bands:
                    to_c, to_d = c, d ^ 1
                if not 0 <= to_d < layers:
                    to_c, to_d = c ^ 1, d
                pairs.append((c * layers + d, to_c * layers + to_d))
        return lax.ppermute(array, ("colat", "depth"), pairs)

    def per_device(displacement, previous, node_blocks, inverse_mass, jac_diag, jac_off, inv_radius, lame_l, lame_m):
        at_c, at_d = lax.axis_index("colat"), lax.axis_index("depth")
        lane = lax.broadcasted_iota(jnp.int32, (8, LANES), 1)
        place = jnp.zeros((8, LANES), F32)
        has_side_c = jnp.where(at_c % 2 == 1, at_c < bands - 1, at_c > 0)
        has_side_d = jnp.where(at_d % 2 == 1, at_d < layers - 1, at_d > 0)
        flags = (at_c < bands - 1, at_d < layers - 1, at_c % 2, at_d % 2, has_side_c, has_side_d)
        for at, value in enumerate(flags):
            place = jnp.where(lane == at, value.astype(F32), place)
        row_face = shape(3, 4, WIDTH + LANES, dtype=BF16)
        point = shape(3, 1, WIDTH + LANES, dtype=BF16)
        row, col, corner = call(
            first_kernel,
            (row_face, row_face, point),
            [
                pltpu.SMEM((4, 4), jnp.int32),
                pltpu.SMEM((4, 4), F32),
                pltpu.VMEM((3, 4, 4, WIDTH), F32),
                pltpu.SemaphoreType.DMA((3,)),
            ],
            far=3, flops=2 * 10**10, vmem=62 * 1024 * 1024,
        )(node_blocks, inverse_mass, displacement)
        col = shifted(col, 0, -1)
        corner = shifted(corner, -1, -1)
        row = shifted(row, -1, 0)

        operator, back, material, own, free, info, outgoing, column, arrival = call(
            functools.partial(prepare_kernel, starts),
            (
                shape(STRAINS, 2 * NODES, dtype=BF16),
                shape(2 * NODES, STRAINS, dtype=BF16),
                shape(RADIX, 56, LANES),
                shape(OWN, WIDTH),
                shape(OWN, WIDTH),
                shape(OWN + 8, LANES),
                shape(64, NODES, dtype=BF16),
                shape(32, 64, dtype=BF16),
                shape(NODES, 64, dtype=BF16),
            ),
            [pltpu.VMEM((2, 400, LANES), F32)],
            inputs=11, flops=10**9,
        )(
            place, node_blocks, inverse_mass, displacement, previous,
            jac_diag.reshape(10, 1, 5), jac_off.reshape(10, 1, 5), inv_radius.reshape(5, 1, 5),
            lame_l.reshape(400, LANES), lame_m.reshape(400, LANES), jnp.asarray(packed),
        )

        work = [
            pltpu.VMEM((2 * NODES, WIDTH), BF16),
            pltpu.VMEM((STRAINS, WIDTH), F32),
            pltpu.VMEM((RADIX, STRAINS, 2 * LANES), F32),
        ]
        tile = shape(16, WIDTH, dtype=BF16)
        shared = (operator, back, jnp.asarray(table), jnp.asarray(tback), material)
        total, pair, side, faces = call(
            step_one_kernel,
            (shape(NODES, WIDTH + LANES), tile, tile, shape(32, WIDTH, dtype=BF16)),
            [pltpu.VMEM((32, WIDTH + LANES), F32)] + work,
            inputs=12, flops=10**9,
        )(own, free, info, col, corner, row, *shared, outgoing)
        cside = swapped(side, "colat", 1)
        cpair = swapped(pair, "colat", 0)
        side, pair = call(column_kernel, (tile, tile), inputs=4)(faces, cside, cpair, column)
        dside = swapped(side, "depth", 1)
        dpair = swapped(pair, "depth", 0)
        row_face = shape(3, 4, WIDTH, dtype=BF16)
        middle, final, row, col, corner = call(
            step_two_kernel,
            (
                shape(OWN, WIDTH), shape(3, 4, 4, WIDTH), row_face, row_face,
                shape(3, 1, WIDTH, dtype=BF16),
            ),
            [pltpu.VMEM((NODES, WIDTH), F32)] + work,
            inputs=12, flops=10**9,
        )(own, total, cside, cpair, dside, dpair, *shared, arrival)
        col = shifted(col, 0, 1)
        corner = shifted(corner, 1, 1)
        row = shifted(row, 1, 0)
        middle = call(middle_kernel, shape(3, 4, 4, WIDTH), inputs=1, flops=2 * 10**10, vmem=4 * 1024 * 1024)(middle)
        final = call(last_kernel, shape(3, 4, 4, WIDTH), inputs=4)(final, col, corner, row)
        return middle, final

    return jax.shard_map(
        per_device,
        mesh=mesh,
        in_specs=(
            P(None, "colat", "depth", None),
            P(None, "colat", "depth", None),
            P("colat", "depth"),
            P("colat", "depth"),
            P(None, "colat", None, "depth", None),
            P(None, "colat", None, "depth", None),
            P("colat", None, "depth", None),
            P("colat", None, "depth", None, None),
            P("colat", None, "depth", None, None),
        ),
        out_specs=(P(None, "colat", "depth", None), P(None, "colat", "depth", None)),
        check_vma=False,
    )
```

```python
import functools
import math

import jax
import jax.numpy as jnp
import ml_dtypes
import numpy as np
from jax import lax
from jax.experimental import pallas as pl
from jax.experimental.pallas import tpu as pltpu
from jax.sharding import PartitionSpec as P

BF16 = jnp.bfloat16
F32 = jnp.float32
WIDTH = 2048
LANES = 128
RADIX = 16
OWN = 48
NODES = 80
STRAINS = 152
VMEM_LIMIT = 40 * 1024 * 1024


def gll_derivative():
    points = np.array([-1.0, -math.sqrt(3.0 / 7.0), 0.0, math.sqrt(3.0 / 7.0), 1.0])
    weights = np.ones(5)
    for row in range(5):
        for col in range(5):
            if row != col:
                weights[row] /= points[row] - points[col]
    matrix = np.zeros((5, 5))
    for row in range(5):
        for col in range(5):
            if row != col:
                matrix[row, col] = weights[col] / weights[row] / (points[row] - points[col])
        matrix[row, row] = -np.sum(matrix[row])
    return matrix


def node_row(comp, i, j):
    if i == 4:
        return OWN + (12 + comp if j == 4 else 4 * comp + j)
    if j == 4:
        return OWN + 16 + 4 * comp + i
    return 16 * comp + 4 * i + j


def strain_row(strain, node):
    return 24 * strain + node if node < 24 else 144 + strain


def strain_terms():
    deriv = gll_derivative()
    parts = np.zeros((5, STRAINS, 2 * NODES))
    place_of = np.zeros((2, STRAINS, 5))
    half = math.sqrt(0.5)
    for i in range(5):
        for j in range(5):
            node = 5 * i + j

            def grad(strain, along_z, comp, scale):
                row = strain_row(strain, node)
                for other in range(5):
                    xi, eta = (2, 3) if along_z else (0, 1)
                    parts[xi, row, node_row(comp, other, j)] += scale * deriv[i, other]
                    parts[eta, row, node_row(comp, i, other)] += scale * deriv[j, other]

            def radial(strain, comp, azimuthal, scale):
                row = strain_row(strain, node)
                parts[4, row, NODES * azimuthal + node_row(comp, i, j)] += scale / 1024.0

            grad(0, False, 0, 1.0)
            grad(1, True, 2, 1.0)
            radial(2, 1, 1, 1.0)
            radial(2, 0, 0, 1.0)
            grad(3, True, 0, half)
            grad(3, False, 2, half)
            radial(4, 0, 1, half)
            radial(4, 1, 0, -half)
            grad(4, False, 1, half)
            radial(5, 2, 1, half)
            grad(5, True, 1, half)
            for strain in range(6):
                place_of[0, strain_row(strain, node), i] = 1.0
                place_of[1, strain_row(strain, node), j] = 1.0
    parts[:, 150] = parts[:, 144] + parts[:, 145] + parts[:, 146]
    place_of[:, 150, 4] = 1.0
    return parts.astype(np.float32), place_of.astype(np.float32)


def sample_tables():
    order = np.arange(LANES)[:, None]
    table = np.zeros((RADIX, 2 * LANES, LANES))
    for k0 in range(RADIX):
        angle = 2.0 * math.pi * (order * (16 * np.arange(LANES)[None, :] + k0) % WIDTH) / WIDTH
        table[k0, :LANES] = np.cos(angle)
        table[k0, LANES:] = -np.sin(angle)
    return (
        table.astype(ml_dtypes.bfloat16),
        np.ascontiguousarray(table.transpose(0, 2, 1)).astype(ml_dtypes.bfloat16),
    )


def lane_shuffle():
    shuffle = np.zeros((LANES, LANES))
    for t in range(8):
        for k0 in range(16):
            shuffle[16 * t + k0, 8 * k0 + t] = 1.0
    return shuffle.astype(ml_dtypes.bfloat16)


def face(fixed_i, fixed_j):
    return [(fixed_i, n) if fixed_j is None else (n, fixed_j) for n in range(5)]


def message_row(comp, n):
    return 12 + comp if n == 4 else 4 * comp + n


def pick(faces):
    select = np.zeros((16 * len(faces), NODES))
    for index, nodes in enumerate(faces):
        for comp in range(3):
            for n, (i, j) in enumerate(nodes):
                select[16 * index + message_row(comp, n), node_row(comp, i, j)] = 1.0
    return select


ROW_LOW, ROW_HIGH = face(0, None), face(4, None)
COL_LOW, COL_HIGH = face(None, 0), face(None, 4)


def outgoing_select():
    even = pick([ROW_HIGH, ROW_LOW, COL_HIGH, COL_LOW])
    odd = pick([ROW_LOW, ROW_HIGH, COL_HIGH, COL_LOW])
    return np.stack([even, odd]).astype(ml_dtypes.bfloat16)


def column_select():
    out = np.zeros((4, 32, 64))
    for par_c in range(2):
        faces = [ROW_HIGH, ROW_LOW] if par_c == 0 else [ROW_LOW, ROW_HIGH]
        arrive = pick(faces).T
        full = np.concatenate([pick([COL_HIGH]), pick([COL_LOW])], axis=0)
        whole = np.concatenate([np.eye(32), full @ arrive], axis=1)
        for par_d in range(2):
            out[2 * par_c + par_d] = whole if par_d == 0 else np.roll(whole, 16, axis=0)
    return out.astype(ml_dtypes.bfloat16)


def arrival_select():
    out = np.zeros((4, NODES, 64))
    for par_c in range(2):
        rows = [ROW_HIGH, ROW_LOW] if par_c == 0 else [ROW_LOW, ROW_HIGH]
        for par_d in range(2):
            cols = [COL_HIGH, COL_LOW] if par_d == 0 else [COL_LOW, COL_HIGH]
            out[2 * par_c + par_d] = pick(rows + cols).T
    return out.astype(ml_dtypes.bfloat16)


def turned(value, eighths, scale_sign):
    re, im = value
    eighths = (scale_sign * eighths) % 16
    if eighths == 0:
        return re, im
    if eighths == 4:
        return -im, re
    if eighths == 8:
        return -re, -im
    if eighths == 12:
        return im, -re
    root = math.sqrt(0.5)
    if eighths == 2:
        return (re - im) * root, (im + re) * root
    if eighths == 14:
        return (re + im) * root, (im - re) * root
    cosine = math.cos(2.0 * math.pi * eighths / 16)
    sine = math.sin(2.0 * math.pi * eighths / 16)
    return re * cosine - im * sine, im * cosine + re * sine


def add(left, right):
    return left[0] + right[0], left[1] + right[1]


def sub(left, right):
    return left[0] - right[0], left[1] - right[1]


def transform(values, sign):
    count = len(values)
    if count == 1:
        return values
    even = transform(values[0::2], sign)
    odd = transform(values[1::2], sign)
    odd = [turned(value, q * (16 // count), sign) for q, value in enumerate(odd)]
    return [add(a, b) for a, b in zip(even, odd)] + [sub(a, b) for a, b in zip(even, odd)]


def spread(blocks):
    even = transform(blocks, 1)
    odd = transform([turned(value, b, 1) for b, value in enumerate(blocks)], 1)
    return [value for pair in zip(even, odd) for value in pair]


def gathered(values):
    even = transform(values[0::2], -1)
    odd = transform(values[1::2], -1)
    return [add(a, turned(b, index, -1)) for index, (a, b) in enumerate(zip(even, odd))]


def block(index, part):
    return slice(2 * LANES * index + LANES * part, 2 * LANES * index + LANES * (part + 1))


def orders(index):
    lane = lax.broadcasted_iota(jnp.int32, (1, LANES), 1)
    return (lane + LANES * index).astype(F32)


def dot(left, right):
    return jnp.dot(left, right, preferred_element_type=F32)


def node_column(scalar, rows):
    row = lax.broadcasted_iota(jnp.int32, (len(rows), 1), 0)
    column = jnp.zeros((len(rows), 1), F32)
    for value in sorted(set(rows)):
        chosen = functools.reduce(jnp.logical_or, [row == at for at, held in enumerate(rows) if held == value])
        column = jnp.where(chosen, scalar(value), column)
    return column


def own_rows(ref, lanes):
    return jnp.concatenate([ref[c, i, :, lanes] for c in range(3) for i in range(4)], axis=0)


def first_kernel(blocks_hbm, mass_hbm, disp_hbm, row_out, col_out, corner_out, blocks_ref, mass_ref, disp_ref, sems):
    loads = [
        pltpu.make_async_copy(source, target, sems.at[n])
        for n, (source, target) in enumerate(
            ((blocks_hbm, blocks_ref), (mass_hbm, mass_ref), (disp_hbm, disp_ref))
        )
    ]
    for load in loads:
        load.start()
    faces = (
        (row_out, [(0, n) for n in range(4)]),
        (col_out, [(n, 0) for n in range(4)]),
        (corner_out, [(0, 0)]),
    )
    loads[0].wait()
    loads[1].wait()
    columns = []
    for out, rows in faces:
        live = node_column(lambda at: blocks_ref[at[0], at[1]].astype(F32), rows)
        mass = node_column(lambda at: mass_ref[at[0], at[1]], rows)
        high = mass.astype(BF16).astype(F32)
        lane = lax.broadcasted_iota(jnp.int32, (len(rows), LANES), 1)
        info = jnp.where(lane == 0, high, jnp.where(lane == 1, mass - high, jnp.where(lane == 2, live, 0.0)))
        for c in range(3):
            out[c, :, WIDTH:] = info.astype(BF16)
        columns.append(live)
    loads[2].wait()
    for (out, rows), live in zip(faces, columns):
        for index in range(8):
            lanes = slice(256 * index, 256 * (index + 1))
            kept = live > index
            for c in range(3):
                if out is row_out:
                    value = disp_ref[c, 0, :, lanes]
                elif out is col_out:
                    value = jnp.concatenate([disp_ref[c, n, 0:1, lanes] for n in range(4)], axis=0)
                else:
                    value = disp_ref[c, 0, 0:1, lanes]
                out[c, :, lanes] = jnp.where(kept, value, 0.0).astype(BF16)


def own_kernel(place_ref, blocks_ref, mass_ref, disp_ref, prev_ref, own_out, free_out, info_out):
    def column(ref):
        shape = (4, 4)
        diagonal = lax.broadcasted_iota(jnp.int32, shape, 0) == lax.broadcasted_iota(jnp.int32, shape, 1)
        value = ref[...].astype(F32)
        pieces = [jnp.sum(jnp.where(diagonal, value[i : i + 1], 0.0), axis=1, keepdims=True) for i in range(4)]
        return jnp.concatenate(pieces * 3, axis=0)

    live, mass = column(blocks_ref), column(mass_ref)
    lane = lax.broadcasted_iota(jnp.int32, (OWN, LANES), 1)
    info_out[:OWN] = jnp.where(lane == 0, mass, jnp.where(lane == 1, live, 0.0))
    info_out[OWN:] = place_ref[...]
    for index in range(8):
        lanes = slice(256 * index, 256 * (index + 1))
        value = jnp.where(live > index, own_rows(disp_ref, lanes), 0.0)
        own_out[:, lanes] = value
        free_out[:, lanes] = jnp.where(live > index, 2.0 * value - own_rows(prev_ref, lanes), 0.0)


def exact_dot(left, right):
    return jnp.dot(left, right, preferred_element_type=F32, precision=lax.Precision.HIGHEST)


def packed_constants():
    parts, place_of = strain_terms()
    upper = np.zeros((3, STRAINS, 2 * LANES), np.float32)
    for term in range(4):
        upper[term // 2, :, NODES * (term % 2) : NODES * (term % 2 + 1)] = parts[term, :, :NODES]
    upper[2, :, : 2 * NODES] = parts[4]
    columns = (
        {"arrival": arrival_select(), "outgoing": outgoing_select()},
        {"shuffle": lane_shuffle()[None], "place": place_of, "column": column_select()},
    )
    lower, starts = np.zeros((3 * STRAINS + 560, 2 * LANES), np.float32), {}
    lower[: 3 * STRAINS] = upper.reshape(-1, 2 * LANES)
    for side, pieces in enumerate(columns):
        first = 3 * STRAINS
        for name, piece in pieces.items():
            starts[name] = (first, LANES * side)
            for matrix in np.asarray(piece, np.float32):
                rows, width = matrix.shape
                lower[first : first + rows, LANES * side : LANES * side + width] = matrix
                first += rows
    return lower, starts


def prepare_kernel(
    starts, place_ref, diag_ref, off_ref, radius_ref, lambda_ref, mu_ref, packed_ref,
    operator_out, back_out, material_out, outgoing_out, column_out, arrival_out,
    shuffled,
):
    def constant(name, rows, columns, index=0):
        first, lane = starts[name]
        return packed_ref[first + rows * index : first + rows * (index + 1), lane : lane + columns]

    at_i, at_j = constant("place", STRAINS, 5), constant("place", STRAINS, 5, 1)
    factors = []
    for ref, row in ((diag_ref, 0), (off_ref, 0), (off_ref, 5), (diag_ref, 5), (radius_ref, 0)):
        factor = jnp.concatenate([ref[row + i] for i in range(5)], axis=0)
        spread_i = exact_dot(at_i, factor) * at_j
        factors.append(jnp.sum(spread_i, axis=1, keepdims=True))
    parts = [packed_ref[STRAINS * n : STRAINS * (n + 1)] for n in range(3)]
    operator = parts[2][:, : 2 * NODES] * factors[4]
    plain = sum(parts[t // 2][:, NODES * (t % 2) : NODES * (t % 2 + 1)] * factors[t] for t in range(4))
    operator = operator + jnp.concatenate([plain, jnp.zeros_like(plain)], axis=1)
    operator_out[...] = operator.astype(BF16)
    back_out[...] = operator.T.astype(BF16)

    def packed(name, rows, columns, *bits):
        pieces = [constant(name, rows, columns, index) for index in range(2 ** len(bits))]
        for bit in reversed(bits):
            pieces = [jnp.where(bit > 0.5, one, zero) for zero, one in zip(pieces[0::2], pieces[1::2])]
        return pieces[0]

    def kept(matrix, first, flag):
        column = lax.broadcasted_iota(jnp.int32, matrix.shape, 1)
        dropped = jnp.logical_and(jnp.logical_and(column >= first, column < first + 16), flag < 0.5)
        return jnp.where(dropped, 0.0, matrix)

    odd_c, odd_d, side_c, side_d = (place_ref[0:1, n : n + 1] for n in range(2, 6))
    outgoing_out[...] = packed("outgoing", 64, NODES, odd_c).astype(BF16)
    column_out[...] = kept(packed("column", 32, 64, odd_c, odd_d), 48, side_c).astype(BF16)
    arrived = kept(packed("arrival", NODES, 64, odd_c, odd_d), 16, side_c)
    arrival_out[...] = kept(arrived, 48, side_d).astype(BF16)
    shuffle = constant("shuffle", LANES, LANES).astype(BF16)

    for which, (ref, factor) in enumerate(((lambda_ref, 1.0), (mu_ref, 2.0))):
        value = ref[...] * factor
        high = value.astype(BF16)
        low = (value - high.astype(F32)).astype(BF16)
        shuffled[which] = dot(high, shuffle) + dot(low, shuffle)
    group = lax.broadcasted_iota(jnp.int32, (8, LANES), 1) // 8
    row = lax.broadcasted_iota(jnp.int32, (8, LANES), 0)
    for rows in range(7):
        held = []
        for s in range(16):
            if rows < 6:
                value = shuffled[rows // 3, pl.ds(128 * (rows % 3) + s, 8, stride=16), :]
            else:
                at = slice(384 + s, 385 + s)
                value = jnp.where(row < 6, shuffled[1, at], jnp.where(row == 6, shuffled[0, at], 0.0))
            held.append(value if s == 0 else pltpu.roll(value, 8 * s, 1))
        held = [held[(16 - index) % 16] for index in range(16)]
        for bit in range(4):
            chosen = (group >> bit) % 2 == 1
            held = [jnp.where(chosen, held[(index - (1 << bit)) % 16], held[index]) for index in range(16)]
        for index in range(16):
            value = held[index] if index == 0 else pltpu.roll(held[index], LANES - 8 * index, 1)
            material_out[index, 8 * rows : 8 * rows + 8] = value


def forces(nodes, operator_ref, back_ref, table_ref, tback_ref, material_ref, both, strain, spectrum, emit):
    for index in range(8):
        order = orders(index)
        re = nodes(block(index, 0))
        im = nodes(block(index, 1))
        both[:NODES, block(index, 0)] = re.astype(BF16)
        both[:NODES, block(index, 1)] = im.astype(BF16)
        both[NODES:, block(index, 0)] = (im * (-order)).astype(BF16)
        both[NODES:, block(index, 1)] = (re * order).astype(BF16)
        lanes = slice(256 * index, 256 * (index + 1))
        strain[:, lanes] = dot(operator_ref[...], both[:, lanes])

    for group in range(STRAINS // 8):
        rows = slice(8 * group, 8 * group + 8)
        values = [(strain[rows, block(b, 0)], strain[rows, block(b, 1)]) for b in range(8)]
        for k0, (re, im) in enumerate(spread(values)):
            spectrum[k0, rows, :LANES] = re
            spectrum[k0, rows, LANES:] = im

    for k0 in range(RADIX):
        sample = dot(spectrum[k0].astype(BF16), table_ref[k0])
        lam, mu, last = material_ref[k0, :24], material_ref[k0, 24:48], material_ref[k0, 48:]
        parts = [sample[24 * s : 24 * s + 24] for s in range(6)]
        volume = lam * (parts[0] + parts[1] + parts[2])
        stress = [volume + mu * part for part in parts[:3]] + [mu * part for part in parts[3:]]
        stress.append(last * sample[144:])
        stress = jnp.concatenate(stress, axis=0).astype(BF16)
        spectrum[k0] = dot(stress, tback_ref[k0])

    for group in range(STRAINS // 8):
        rows = slice(8 * group, 8 * group + 8)
        values = [(spectrum[k0, rows, :LANES], spectrum[k0, rows, LANES:]) for k0 in range(RADIX)]
        for b, (re, im) in enumerate(gathered(values)):
            strain[rows, block(b, 0)] = re
            strain[rows, block(b, 1)] = im

    for index in range(8):
        lanes = slice(256 * index, 256 * (index + 1))
        order = orders(index)
        pulled = dot(back_ref[...], strain[:, lanes].astype(BF16))
        re = pulled[:NODES, :LANES] + order * pulled[NODES:, LANES:]
        im = pulled[:NODES, LANES:] - order * pulled[NODES:, :LANES]
        emit(index, re, im)


def step_one_kernel(
    own_ref, free_ref, info_ref, col_ref, corner_ref, row_ref,
    operator_ref, back_ref, table_ref, tback_ref, material_ref, select_ref,
    sum_ref, pair_ref, side_ref, faces_ref,
    tiles, both, strain, spectrum,
):
    rest_c, rest_d = info_ref[OWN : OWN + 1, 0:1], info_ref[OWN : OWN + 1, 1:2]
    for lanes in [slice(256 * n, 256 * (n + 1)) for n in range(8)] + [slice(WIDTH, WIDTH + LANES)]:
        rows = [row_ref[c, :, lanes].astype(F32) * rest_c for c in range(3)]
        corner = [corner_ref[c, :, lanes].astype(F32) * (rest_c * rest_d) for c in range(3)]
        cols = [col_ref[c, :, lanes].astype(F32) * rest_d for c in range(3)]
        width = lanes.stop - lanes.start
        pieces = rows + corner + [jnp.zeros((1, width), F32)] + cols + [jnp.zeros((4, width), F32)]
        tiles[:, lanes] = jnp.concatenate(pieces, axis=0)
    info = tiles[:, WIDTH:]
    lane = lax.broadcasted_iota(jnp.int32, (32, LANES), 1)
    sum_ref[:OWN, WIDTH:] = info_ref[:OWN]
    sum_ref[OWN:, WIDTH:] = jnp.where(
        lane == 0, info[:, 0:1] + info[:, 1:2], jnp.where(lane == 1, info[:, 2:3], 0.0)
    )
    mass = sum_ref[:, WIDTH : WIDTH + 1] * (-1.0 / WIDTH)

    def nodes(lanes):
        return jnp.concatenate([own_ref[:, lanes], tiles[:, lanes]], axis=0)

    def emit(index, re, im):
        for part, value in ((0, re), (1, im)):
            lanes = block(index, part)
            value = mass * value
            sum_ref[:OWN, lanes] = free_ref[:, lanes] + value[:OWN]
            sum_ref[OWN:, lanes] = value[OWN:]

    forces(nodes, operator_ref, back_ref, table_ref, tback_ref, material_ref, both, strain, spectrum, emit)

    for index in range(8):
        lanes = slice(256 * index, 256 * (index + 1))
        sent = dot(select_ref[...], sum_ref[:, lanes].astype(BF16)).astype(BF16)
        pair_ref[:, lanes] = sent[:16]
        side_ref[:, lanes] = sent[16:32]
        faces_ref[:, lanes] = sent[32:]


def column_kernel(faces_ref, side_ref, pair_ref, select_ref, side_out, pair_out):
    for index in range(8):
        lanes = slice(256 * index, 256 * (index + 1))
        stacked = jnp.concatenate([faces_ref[:, lanes], pair_ref[:, lanes], side_ref[:, lanes]], axis=0)
        sent = dot(select_ref[...], stacked).astype(BF16)
        pair_out[:, lanes] = sent[:16]
        side_out[:, lanes] = sent[16:]


def step_two_kernel(
    own_ref, sum_ref, cside_ref, cpair_ref, dside_ref, dpair_ref,
    operator_ref, back_ref, table_ref, tback_ref, material_ref, select_ref,
    mid_ref, sum_out, row_out, col_out, corner_out,
    current, both, strain, spectrum,
):
    live = sum_ref[:, WIDTH + 1 : WIDTH + 2]
    for index in range(8):
        lanes = slice(256 * index, 256 * (index + 1))
        arrived = jnp.concatenate([ref[:, lanes] for ref in (cpair_ref, cside_ref, dpair_ref, dside_ref)], axis=0)
        value = jnp.where(live > index, sum_ref[:, lanes] + dot(select_ref[...], arrived), 0.0)
        current[:, lanes] = value
        mid_ref[:, lanes] = value[:OWN]
    mass = sum_ref[:, WIDTH : WIDTH + 1] * (-1.0 / WIDTH)

    def emit(index, re, im):
        masked = jnp.where(live > index, mass, 0.0)
        for part, value in ((0, re), (1, im)):
            lanes = block(index, part)
            value = masked * value
            total = 2.0 * current[:OWN, lanes] - own_ref[:, lanes] + value[:OWN]
            value = value.astype(BF16)
            for c in range(3):
                for i in range(4):
                    at = 16 * c + 4 * i
                    sum_out[c, i, :, lanes] = total[at : at + 4]
                at = OWN + 4 * c
                row_out[c, :, lanes] = value[at : at + 4]
                corner_out[c, :, lanes] = value[OWN + 12 + c : OWN + 13 + c]
                col_out[c, :, lanes] = value[at + 16 : at + 20]

    forces(
        lambda lanes: current[:, lanes],
        operator_ref, back_ref, table_ref, tback_ref, material_ref, both, strain, spectrum, emit,
    )


def middle_kernel(rows_ref, out_ref):
    for c in range(3):
        for i in range(4):
            at = 16 * c + 4 * i
            out_ref[c, i] = rows_ref[at : at + 4]


def last_kernel(sum_ref, col_ref, corner_ref, row_ref, out_ref):
    first = lax.broadcasted_iota(jnp.int32, (4, 1), 0) == 0
    for c in range(3):
        for i in range(4):
            arrived = col_ref[c, i : i + 1].astype(F32)
            if i == 0:
                arrived = arrived + corner_ref[c].astype(F32)
            value = sum_ref[c, i] + jnp.where(first, arrived, 0.0)
            if i == 0:
                value = value + row_ref[c].astype(F32)
            out_ref[c, i] = value


def call(kernel, outs, scratch=(), scalars=0, inputs=0, flops=0, far=0, vmem=VMEM_LIMIT):
    near = pl.BlockSpec(memory_space=pltpu.VMEM)
    return pl.pallas_call(
        kernel,
        out_shape=outs,
        in_specs=[pl.BlockSpec(memory_space=pltpu.HBM)] * far
        + [pl.BlockSpec(memory_space=pltpu.SMEM)] * scalars
        + [near] * inputs,
        out_specs=jax.tree.map(lambda _: near, outs),
        scratch_shapes=list(scratch),
        compiler_params=pltpu.CompilerParams(vmem_limit_bytes=vmem),
        cost_estimate=pl.CostEstimate(flops=flops, bytes_accessed=1 << 20, transcendentals=0),
    )


def shape(*dims, dtype=F32):
    return jax.ShapeDtypeStruct(dims, dtype)


def solution(mesh):
    bands, layers = mesh.shape["colat"], mesh.shape["depth"]
    packed, starts = packed_constants()
    table, tback = sample_tables()

    def target(c, d, by_c, by_d):
        past = not 0 <= d + by_d < layers
        return (c + by_c + past * (bands // 2)) % bands * layers + (d + by_d) % layers

    def shifted(array, by_c, by_d):
        pairs = [(c * layers + d, target(c, d, by_c, by_d)) for c in range(bands) for d in range(layers)]
        return lax.ppermute(array, ("colat", "depth"), pairs)

    def swapped(array, axis, odd):
        along_c = axis == "colat"
        pairs = []
        for c in range(bands):
            for d in range(layers):
                step = 1 if (c if along_c else d) % 2 == odd else -1
                to_c, to_d = c + step * along_c, d + step * (not along_c)
                if not 0 <= to_c < bands:
                    to_c, to_d = c, d ^ 1
                if not 0 <= to_d < layers:
                    to_c, to_d = c ^ 1, d
                pairs.append((c * layers + d, to_c * layers + to_d))
        return lax.ppermute(array, ("colat", "depth"), pairs)

    def per_device(displacement, previous, node_blocks, inverse_mass, jac_diag, jac_off, inv_radius, lame_l, lame_m):
        at_c, at_d = lax.axis_index("colat"), lax.axis_index("depth")
        lane = lax.broadcasted_iota(jnp.int32, (8, LANES), 1)
        place = jnp.zeros((8, LANES), F32)
        has_side_c = jnp.where(at_c % 2 == 1, at_c < bands - 1, at_c > 0)
        has_side_d = jnp.where(at_d % 2 == 1, at_d < layers - 1, at_d > 0)
        flags = (at_c < bands - 1, at_d < layers - 1, at_c % 2, at_d % 2, has_side_c, has_side_d)
        for at, value in enumerate(flags):
            place = jnp.where(lane == at, value.astype(F32), place)
        row_face = shape(3, 4, WIDTH + LANES, dtype=BF16)
        point = shape(3, 1, WIDTH + LANES, dtype=BF16)
        row, col, corner = call(
            first_kernel,
            (row_face, row_face, point),
            [
                pltpu.SMEM((4, 4), jnp.int32),
                pltpu.SMEM((4, 4), F32),
                pltpu.VMEM((3, 4, 4, WIDTH), F32),
                pltpu.SemaphoreType.DMA((3,)),
            ],
            far=3, flops=2 * 10**10, vmem=62 * 1024 * 1024,
        )(node_blocks, inverse_mass, displacement)
        col = shifted(col, 0, -1)
        corner = shifted(corner, -1, -1)
        row = shifted(row, -1, 0)

        own, free, info = call(
            own_kernel,
            (shape(OWN, WIDTH), shape(OWN, WIDTH), shape(OWN + 8, LANES)),
            inputs=5, flops=2 * 10**10, vmem=8 * 1024 * 1024,
        )(place, node_blocks, inverse_mass, displacement, previous)
        operator, back, material, outgoing, column, arrival = call(
            functools.partial(prepare_kernel, starts),
            (
                shape(STRAINS, 2 * NODES, dtype=BF16),
                shape(2 * NODES, STRAINS, dtype=BF16),
                shape(RADIX, 56, LANES),
                shape(64, NODES, dtype=BF16),
                shape(32, 64, dtype=BF16),
                shape(NODES, 64, dtype=BF16),
            ),
            [pltpu.VMEM((2, 400, LANES), F32)],
            inputs=7, flops=10**9, vmem=8 * 1024 * 1024,
        )(
            place,
            jac_diag.reshape(10, 1, 5), jac_off.reshape(10, 1, 5), inv_radius.reshape(5, 1, 5),
            lame_l.reshape(400, LANES), lame_m.reshape(400, LANES), jnp.asarray(packed),
        )

        work = [
            pltpu.VMEM((2 * NODES, WIDTH), BF16),
            pltpu.VMEM((STRAINS, WIDTH), F32),
            pltpu.VMEM((RADIX, STRAINS, 2 * LANES), F32),
        ]
        tile = shape(16, WIDTH, dtype=BF16)
        shared = (operator, back, jnp.asarray(table), jnp.asarray(tback), material)
        total, pair, side, faces = call(
            step_one_kernel,
            (shape(NODES, WIDTH + LANES), tile, tile, shape(32, WIDTH, dtype=BF16)),
            [pltpu.VMEM((32, WIDTH + LANES), F32)] + work,
            inputs=12, flops=10**9,
        )(own, free, info, col, corner, row, *shared, outgoing)
        cside = swapped(side, "colat", 1)
        cpair = swapped(pair, "colat", 0)
        side, pair = call(column_kernel, (tile, tile), inputs=4)(faces, cside, cpair, column)
        dside = swapped(side, "depth", 1)
        dpair = swapped(pair, "depth", 0)
        row_face = shape(3, 4, WIDTH, dtype=BF16)
        middle, final, row, col, corner = call(
            step_two_kernel,
            (
                shape(OWN, WIDTH), shape(3, 4, 4, WIDTH), row_face, row_face,
                shape(3, 1, WIDTH, dtype=BF16),
            ),
            [pltpu.VMEM((NODES, WIDTH), F32)] + work,
            inputs=12, flops=10**9,
        )(own, total, cside, cpair, dside, dpair, *shared, arrival)
        col = shifted(col, 0, 1)
        corner = shifted(corner, 1, 1)
        row = shifted(row, 1, 0)
        middle = call(middle_kernel, shape(3, 4, 4, WIDTH), inputs=1, flops=2 * 10**10, vmem=4 * 1024 * 1024)(middle)
        final = call(last_kernel, shape(3, 4, 4, WIDTH), inputs=4)(final, col, corner, row)
        return middle, final

    return jax.shard_map(
        per_device,
        mesh=mesh,
        in_specs=(
            P(None, "colat", "depth", None),
            P(None, "colat", "depth", None),
            P("colat", "depth"),
            P("colat", "depth"),
            P(None, "colat", None, "depth", None),
            P(None, "colat", None, "depth", None),
            P("colat", None, "depth", None),
            P("colat", None, "depth", None, None),
            P("colat", None, "depth", None, None),
        ),
        out_specs=(P(None, "colat", "depth", None), P(None, "colat", "depth", None)),
        check_vma=False,
    )
```

```python
import functools
import math

import jax
import jax.numpy as jnp
import ml_dtypes
import numpy as np
from jax import lax
from jax.experimental import pallas as pl
from jax.experimental.pallas import tpu as pltpu
from jax.sharding import PartitionSpec as P

BF16 = jnp.bfloat16
F32 = jnp.float32
WIDTH = 2048
LANES = 128
RADIX = 16
OWN = 48
NODES = 80
STRAINS = 152
VMEM_LIMIT = 40 * 1024 * 1024


def gll_derivative():
    points = np.array([-1.0, -math.sqrt(3.0 / 7.0), 0.0, math.sqrt(3.0 / 7.0), 1.0])
    weights = np.ones(5)
    for row in range(5):
        for col in range(5):
            if row != col:
                weights[row] /= points[row] - points[col]
    matrix = np.zeros((5, 5))
    for row in range(5):
        for col in range(5):
            if row != col:
                matrix[row, col] = weights[col] / weights[row] / (points[row] - points[col])
        matrix[row, row] = -np.sum(matrix[row])
    return matrix


def node_row(comp, i, j):
    if i == 4:
        return OWN + (12 + comp if j == 4 else 4 * comp + j)
    if j == 4:
        return OWN + 16 + 4 * comp + i
    return 16 * comp + 4 * i + j


def strain_row(strain, node):
    return 24 * strain + node if node < 24 else 144 + strain


def strain_terms():
    deriv = gll_derivative()
    parts = np.zeros((5, STRAINS, 2 * NODES))
    place_of = np.zeros((2, STRAINS, 5))
    half = math.sqrt(0.5)
    for i in range(5):
        for j in range(5):
            node = 5 * i + j

            def grad(strain, along_z, comp, scale):
                row = strain_row(strain, node)
                for other in range(5):
                    xi, eta = (2, 3) if along_z else (0, 1)
                    parts[xi, row, node_row(comp, other, j)] += scale * deriv[i, other]
                    parts[eta, row, node_row(comp, i, other)] += scale * deriv[j, other]

            def radial(strain, comp, azimuthal, scale):
                row = strain_row(strain, node)
                parts[4, row, NODES * azimuthal + node_row(comp, i, j)] += scale / 1024.0

            grad(0, False, 0, 1.0)
            grad(1, True, 2, 1.0)
            radial(2, 1, 1, 1.0)
            radial(2, 0, 0, 1.0)
            grad(3, True, 0, half)
            grad(3, False, 2, half)
            radial(4, 0, 1, half)
            radial(4, 1, 0, -half)
            grad(4, False, 1, half)
            radial(5, 2, 1, half)
            grad(5, True, 1, half)
            for strain in range(6):
                place_of[0, strain_row(strain, node), i] = 1.0
                place_of[1, strain_row(strain, node), j] = 1.0
    parts[:, 150] = parts[:, 144] + parts[:, 145] + parts[:, 146]
    place_of[:, 150, 4] = 1.0
    return parts.astype(np.float32), place_of.astype(np.float32)


def sample_tables():
    order = np.arange(LANES)[:, None]
    table = np.zeros((RADIX, 2 * LANES, LANES))
    for k0 in range(RADIX):
        angle = 2.0 * math.pi * (order * (16 * np.arange(LANES)[None, :] + k0) % WIDTH) / WIDTH
        table[k0, :LANES] = np.cos(angle)
        table[k0, LANES:] = -np.sin(angle)
    return (
        table.astype(ml_dtypes.bfloat16),
        np.ascontiguousarray(table.transpose(0, 2, 1)).astype(ml_dtypes.bfloat16),
    )


def lane_shuffle():
    shuffle = np.zeros((LANES, LANES))
    for t in range(8):
        for k0 in range(16):
            shuffle[16 * t + k0, 8 * k0 + t] = 1.0
    return shuffle.astype(ml_dtypes.bfloat16)


def face(fixed_i, fixed_j):
    return [(fixed_i, n) if fixed_j is None else (n, fixed_j) for n in range(5)]


def message_row(comp, n):
    return 12 + comp if n == 4 else 4 * comp + n


def pick(faces):
    select = np.zeros((16 * len(faces), NODES))
    for index, nodes in enumerate(faces):
        for comp in range(3):
            for n, (i, j) in enumerate(nodes):
                select[16 * index + message_row(comp, n), node_row(comp, i, j)] = 1.0
    return select


ROW_LOW, ROW_HIGH = face(0, None), face(4, None)
COL_LOW, COL_HIGH = face(None, 0), face(None, 4)


def outgoing_select():
    even = pick([ROW_HIGH, ROW_LOW, COL_HIGH, COL_LOW])
    odd = pick([ROW_LOW, ROW_HIGH, COL_HIGH, COL_LOW])
    return np.stack([even, odd]).astype(ml_dtypes.bfloat16)


def column_select():
    out = np.zeros((4, 32, 64))
    for par_c in range(2):
        faces = [ROW_HIGH, ROW_LOW] if par_c == 0 else [ROW_LOW, ROW_HIGH]
        arrive = pick(faces).T
        full = np.concatenate([pick([COL_HIGH]), pick([COL_LOW])], axis=0)
        whole = np.concatenate([np.eye(32), full @ arrive], axis=1)
        for par_d in range(2):
            out[2 * par_c + par_d] = whole if par_d == 0 else np.roll(whole, 16, axis=0)
    return out.astype(ml_dtypes.bfloat16)


def arrival_select():
    out = np.zeros((4, NODES, 64))
    for par_c in range(2):
        rows = [ROW_HIGH, ROW_LOW] if par_c == 0 else [ROW_LOW, ROW_HIGH]
        for par_d in range(2):
            cols = [COL_HIGH, COL_LOW] if par_d == 0 else [COL_LOW, COL_HIGH]
            out[2 * par_c + par_d] = pick(rows + cols).T
    return out.astype(ml_dtypes.bfloat16)


def turned(value, eighths, scale_sign):
    re, im = value
    eighths = (scale_sign * eighths) % 16
    if eighths == 0:
        return re, im
    if eighths == 4:
        return -im, re
    if eighths == 8:
        return -re, -im
    if eighths == 12:
        return im, -re
    root = math.sqrt(0.5)
    if eighths == 2:
        return (re - im) * root, (im + re) * root
    if eighths == 14:
        return (re + im) * root, (im - re) * root
    cosine = math.cos(2.0 * math.pi * eighths / 16)
    sine = math.sin(2.0 * math.pi * eighths / 16)
    return re * cosine - im * sine, im * cosine + re * sine


def add(left, right):
    return left[0] + right[0], left[1] + right[1]


def sub(left, right):
    return left[0] - right[0], left[1] - right[1]


def transform(values, sign):
    count = len(values)
    if count == 1:
        return values
    even = transform(values[0::2], sign)
    odd = transform(values[1::2], sign)
    odd = [turned(value, q * (16 // count), sign) for q, value in enumerate(odd)]
    return [add(a, b) for a, b in zip(even, odd)] + [sub(a, b) for a, b in zip(even, odd)]


def spread(blocks):
    even = transform(blocks, 1)
    odd = transform([turned(value, b, 1) for b, value in enumerate(blocks)], 1)
    return [value for pair in zip(even, odd) for value in pair]


def gathered(values):
    even = transform(values[0::2], -1)
    odd = transform(values[1::2], -1)
    return [add(a, turned(b, index, -1)) for index, (a, b) in enumerate(zip(even, odd))]


def block(index, part):
    return slice(2 * LANES * index + LANES * part, 2 * LANES * index + LANES * (part + 1))


def orders(index):
    lane = lax.broadcasted_iota(jnp.int32, (1, LANES), 1)
    return (lane + LANES * index).astype(F32)


def dot(left, right):
    return jnp.dot(left, right, preferred_element_type=F32)


def node_column(scalar, rows):
    row = lax.broadcasted_iota(jnp.int32, (len(rows), 1), 0)
    column = jnp.zeros((len(rows), 1), F32)
    for value in sorted(set(rows)):
        chosen = functools.reduce(jnp.logical_or, [row == at for at, held in enumerate(rows) if held == value])
        column = jnp.where(chosen, scalar(value), column)
    return column


def own_rows(ref, lanes):
    return jnp.concatenate([ref[c, i, :, lanes] for c in range(3) for i in range(4)], axis=0)


def first_kernel(blocks_hbm, mass_hbm, disp_hbm, row_out, col_out, corner_out, blocks_ref, mass_ref, disp_ref, sems):
    loads = [
        pltpu.make_async_copy(source, target, sems.at[n])
        for n, (source, target) in enumerate(
            ((blocks_hbm, blocks_ref), (mass_hbm, mass_ref), (disp_hbm, disp_ref))
        )
    ]
    for load in loads:
        load.start()
    faces = (
        (row_out, [(0, n) for n in range(4)]),
        (col_out, [(n, 0) for n in range(4)]),
        (corner_out, [(0, 0)]),
    )
    loads[0].wait()
    loads[1].wait()
    columns = []
    for out, rows in faces:
        live = node_column(lambda at: blocks_ref[at[0], at[1]].astype(F32), rows)
        mass = node_column(lambda at: mass_ref[at[0], at[1]], rows)
        high = mass.astype(BF16).astype(F32)
        lane = lax.broadcasted_iota(jnp.int32, (len(rows), LANES), 1)
        info = jnp.where(lane == 0, high, jnp.where(lane == 1, mass - high, jnp.where(lane == 2, live, 0.0)))
        for c in range(3):
            out[c, :, WIDTH:] = info.astype(BF16)
        columns.append(live)
    loads[2].wait()
    for (out, rows), live in zip(faces, columns):
        for index in range(8):
            lanes = slice(256 * index, 256 * (index + 1))
            kept = live > index
            for c in range(3):
                if out is row_out:
                    value = disp_ref[c, 0, :, lanes]
                elif out is col_out:
                    value = jnp.concatenate([disp_ref[c, n, 0:1, lanes] for n in range(4)], axis=0)
                else:
                    value = disp_ref[c, 0, 0:1, lanes]
                out[c, :, lanes] = jnp.where(kept, value, 0.0).astype(BF16)


def own_kernel(place_ref, blocks_ref, mass_ref, disp_ref, prev_ref, own_out, free_out, info_out):
    def column(ref):
        shape = (4, 4)
        diagonal = lax.broadcasted_iota(jnp.int32, shape, 0) == lax.broadcasted_iota(jnp.int32, shape, 1)
        value = ref[...].astype(F32)
        pieces = [jnp.sum(jnp.where(diagonal, value[i : i + 1], 0.0), axis=1, keepdims=True) for i in range(4)]
        return jnp.concatenate(pieces * 3, axis=0)

    live, mass = column(blocks_ref), column(mass_ref)
    lane = lax.broadcasted_iota(jnp.int32, (OWN, LANES), 1)
    info_out[:OWN] = jnp.where(lane == 0, mass, jnp.where(lane == 1, live, 0.0))
    info_out[OWN:] = place_ref[...]
    for index in range(8):
        lanes = slice(256 * index, 256 * (index + 1))
        value = jnp.where(live > index, own_rows(disp_ref, lanes), 0.0)
        own_out[:, lanes] = value
        free_out[:, lanes] = jnp.where(live > index, 2.0 * value - own_rows(prev_ref, lanes), 0.0)


def exact_dot(left, right):
    return jnp.dot(left, right, preferred_element_type=F32, precision=lax.Precision.HIGHEST)


def packed_constants():
    parts, place_of = strain_terms()
    upper = np.zeros((3, STRAINS, 2 * LANES), np.float32)
    for term in range(4):
        upper[term // 2, :, NODES * (term % 2) : NODES * (term % 2 + 1)] = parts[term, :, :NODES]
    upper[2, :, : 2 * NODES] = parts[4]
    columns = (
        {"arrival": arrival_select(), "outgoing": outgoing_select()},
        {"shuffle": lane_shuffle()[None], "place": place_of, "column": column_select()},
    )
    lower, starts = np.zeros((3 * STRAINS + 560, 2 * LANES), np.float32), {}
    lower[: 3 * STRAINS] = upper.reshape(-1, 2 * LANES)
    for side, pieces in enumerate(columns):
        first = 3 * STRAINS
        for name, piece in pieces.items():
            starts[name] = (first, LANES * side)
            for matrix in np.asarray(piece, np.float32):
                rows, width = matrix.shape
                lower[first : first + rows, LANES * side : LANES * side + width] = matrix
                first += rows
    return lower, starts


def prepare_kernel(
    starts, place_ref, diag_ref, off_ref, radius_ref, lambda_ref, mu_ref, packed_ref,
    operator_out, back_out, material_out, outgoing_out, column_out, arrival_out,
    shuffled,
):
    def constant(name, rows, columns, index=0):
        first, lane = starts[name]
        return packed_ref[first + rows * index : first + rows * (index + 1), lane : lane + columns]

    at_i, at_j = constant("place", STRAINS, 5), constant("place", STRAINS, 5, 1)
    factors = []
    for ref, row in ((diag_ref, 0), (off_ref, 0), (off_ref, 5), (diag_ref, 5), (radius_ref, 0)):
        factor = jnp.concatenate([ref[row + i] for i in range(5)], axis=0)
        spread_i = exact_dot(at_i, factor) * at_j
        factors.append(jnp.sum(spread_i, axis=1, keepdims=True))
    parts = [packed_ref[STRAINS * n : STRAINS * (n + 1)] for n in range(3)]
    operator = parts[2][:, : 2 * NODES] * factors[4]
    plain = sum(parts[t // 2][:, NODES * (t % 2) : NODES * (t % 2 + 1)] * factors[t] for t in range(4))
    operator = operator + jnp.concatenate([plain, jnp.zeros_like(plain)], axis=1)
    operator_out[...] = operator.astype(BF16)
    back_out[...] = operator.T.astype(BF16)

    def packed(name, rows, columns, *bits):
        pieces = [constant(name, rows, columns, index) for index in range(2 ** len(bits))]
        for bit in reversed(bits):
            pieces = [jnp.where(bit > 0.5, one, zero) for zero, one in zip(pieces[0::2], pieces[1::2])]
        return pieces[0]

    def kept(matrix, first, flag):
        column = lax.broadcasted_iota(jnp.int32, matrix.shape, 1)
        dropped = jnp.logical_and(jnp.logical_and(column >= first, column < first + 16), flag < 0.5)
        return jnp.where(dropped, 0.0, matrix)

    odd_c, odd_d, side_c, side_d = (place_ref[0:1, n : n + 1] for n in range(2, 6))
    outgoing_out[...] = packed("outgoing", 64, NODES, odd_c).astype(BF16)
    column_out[...] = kept(packed("column", 32, 64, odd_c, odd_d), 48, side_c).astype(BF16)
    arrived = kept(packed("arrival", NODES, 64, odd_c, odd_d), 16, side_c)
    arrival_out[...] = kept(arrived, 48, side_d).astype(BF16)
    shuffle = constant("shuffle", LANES, LANES).astype(BF16)

    for which, (ref, factor) in enumerate(((lambda_ref, 1.0), (mu_ref, 2.0))):
        value = ref[...] * factor
        high = value.astype(BF16)
        low = (value - high.astype(F32)).astype(BF16)
        shuffled[which] = dot(high, shuffle) + dot(low, shuffle)
    group = lax.broadcasted_iota(jnp.int32, (8, LANES), 1) // 8
    row = lax.broadcasted_iota(jnp.int32, (8, LANES), 0)
    for rows in range(7):
        held = []
        for s in range(16):
            if rows < 6:
                value = shuffled[rows // 3, pl.ds(128 * (rows % 3) + s, 8, stride=16), :]
            else:
                at = slice(384 + s, 385 + s)
                value = jnp.where(row < 6, shuffled[1, at], jnp.where(row == 6, shuffled[0, at], 0.0))
            held.append(value if s == 0 else pltpu.roll(value, 8 * s, 1))
        held = [held[(16 - index) % 16] for index in range(16)]
        for bit in range(4):
            chosen = (group >> bit) % 2 == 1
            held = [jnp.where(chosen, held[(index - (1 << bit)) % 16], held[index]) for index in range(16)]
        for index in range(16):
            value = held[index] if index == 0 else pltpu.roll(held[index], LANES - 8 * index, 1)
            material_out[index, 8 * rows : 8 * rows + 8] = value


def forces(nodes, operator_ref, back_ref, table_ref, tback_ref, material_ref, both, strain, spectrum, emit):
    for index in range(8):
        order = orders(index)
        re = nodes(block(index, 0))
        im = nodes(block(index, 1))
        both[:NODES, block(index, 0)] = re.astype(BF16)
        both[:NODES, block(index, 1)] = im.astype(BF16)
        both[NODES:, block(index, 0)] = (im * (-order)).astype(BF16)
        both[NODES:, block(index, 1)] = (re * order).astype(BF16)
        lanes = slice(256 * index, 256 * (index + 1))
        strain[:, lanes] = dot(operator_ref[...], both[:, lanes])

    for group in range(STRAINS // 8):
        rows = slice(8 * group, 8 * group + 8)
        values = [(strain[rows, block(b, 0)], strain[rows, block(b, 1)]) for b in range(8)]
        for k0, (re, im) in enumerate(spread(values)):
            spectrum[k0, rows, :LANES] = re
            spectrum[k0, rows, LANES:] = im

    for k0 in range(RADIX):
        sample = dot(spectrum[k0].astype(BF16), table_ref[k0])
        lam, mu, last = material_ref[k0, :24], material_ref[k0, 24:48], material_ref[k0, 48:]
        parts = [sample[24 * s : 24 * s + 24] for s in range(6)]
        volume = lam * (parts[0] + parts[1] + parts[2])
        stress = [volume + mu * part for part in parts[:3]] + [mu * part for part in parts[3:]]
        stress.append(last * sample[144:])
        stress = jnp.concatenate(stress, axis=0).astype(BF16)
        spectrum[k0] = dot(stress, tback_ref[k0])

    for group in range(STRAINS // 8):
        rows = slice(8 * group, 8 * group + 8)
        values = [(spectrum[k0, rows, :LANES], spectrum[k0, rows, LANES:]) for k0 in range(RADIX)]
        for b, (re, im) in enumerate(gathered(values)):
            strain[rows, block(b, 0)] = re
            strain[rows, block(b, 1)] = im

    for index in range(8):
        lanes = slice(256 * index, 256 * (index + 1))
        order = orders(index)
        pulled = dot(back_ref[...], strain[:, lanes].astype(BF16))
        re = pulled[:NODES, :LANES] + order * pulled[NODES:, LANES:]
        im = pulled[:NODES, LANES:] - order * pulled[NODES:, :LANES]
        emit(index, re, im)


def step_one_kernel(
    own_ref, free_ref, info_ref, col_ref, corner_ref, row_ref,
    operator_ref, back_ref, table_ref, tback_ref, material_ref, select_ref,
    sum_ref, pair_ref, side_ref, faces_ref,
    tiles, both, strain, spectrum,
):
    rest_c, rest_d = info_ref[OWN : OWN + 1, 0:1], info_ref[OWN : OWN + 1, 1:2]
    for lanes in [slice(256 * n, 256 * (n + 1)) for n in range(8)] + [slice(WIDTH, WIDTH + LANES)]:
        rows = [row_ref[c, :, lanes].astype(F32) * rest_c for c in range(3)]
        corner = [corner_ref[c, :, lanes].astype(F32) * (rest_c * rest_d) for c in range(3)]
        cols = [col_ref[c, :, lanes].astype(F32) * rest_d for c in range(3)]
        width = lanes.stop - lanes.start
        pieces = rows + corner + [jnp.zeros((1, width), F32)] + cols + [jnp.zeros((4, width), F32)]
        tiles[:, lanes] = jnp.concatenate(pieces, axis=0)
    info = tiles[:, WIDTH:]
    lane = lax.broadcasted_iota(jnp.int32, (32, LANES), 1)
    sum_ref[:OWN, WIDTH:] = info_ref[:OWN]
    sum_ref[OWN:, WIDTH:] = jnp.where(
        lane == 0, info[:, 0:1] + info[:, 1:2], jnp.where(lane == 1, info[:, 2:3], 0.0)
    )
    mass = sum_ref[:, WIDTH : WIDTH + 1] * (-1.0 / WIDTH)

    def nodes(lanes):
        return jnp.concatenate([own_ref[:, lanes], tiles[:, lanes]], axis=0)

    def emit(index, re, im):
        for part, value in ((0, re), (1, im)):
            lanes = block(index, part)
            value = mass * value
            sum_ref[:OWN, lanes] = free_ref[:, lanes] + value[:OWN]
            sum_ref[OWN:, lanes] = value[OWN:]

    forces(nodes, operator_ref, back_ref, table_ref, tback_ref, material_ref, both, strain, spectrum, emit)

    for index in range(8):
        lanes = slice(256 * index, 256 * (index + 1))
        sent = dot(select_ref[...], sum_ref[:, lanes].astype(BF16)).astype(BF16)
        pair_ref[:, lanes] = sent[:16]
        side_ref[:, lanes] = sent[16:32]
        faces_ref[:, lanes] = sent[32:]


def column_kernel(faces_ref, side_ref, pair_ref, select_ref, side_out, pair_out):
    for index in range(8):
        lanes = slice(256 * index, 256 * (index + 1))
        stacked = jnp.concatenate([faces_ref[:, lanes], pair_ref[:, lanes], side_ref[:, lanes]], axis=0)
        sent = dot(select_ref[...], stacked).astype(BF16)
        pair_out[:, lanes] = sent[:16]
        side_out[:, lanes] = sent[16:]


def step_two_kernel(
    own_ref, sum_ref, cside_ref, cpair_ref, dside_ref, dpair_ref,
    operator_ref, back_ref, table_ref, tback_ref, material_ref, select_ref,
    mid_ref, sum_out, row_out, col_out, corner_out,
    current, both, strain, spectrum,
):
    live = sum_ref[:, WIDTH + 1 : WIDTH + 2]
    for index in range(8):
        lanes = slice(256 * index, 256 * (index + 1))
        arrived = jnp.concatenate([ref[:, lanes] for ref in (cpair_ref, cside_ref, dpair_ref, dside_ref)], axis=0)
        value = jnp.where(live > index, sum_ref[:, lanes] + dot(select_ref[...], arrived), 0.0)
        current[:, lanes] = value
        mid_ref[:, lanes] = value[:OWN]
    mass = sum_ref[:, WIDTH : WIDTH + 1] * (-1.0 / WIDTH)

    def emit(index, re, im):
        masked = jnp.where(live > index, mass, 0.0)
        for part, value in ((0, re), (1, im)):
            lanes = block(index, part)
            value = masked * value
            total = 2.0 * current[:OWN, lanes] - own_ref[:, lanes] + value[:OWN]
            value = value.astype(BF16)
            for c in range(3):
                for i in range(4):
                    at = 16 * c + 4 * i
                    sum_out[c, i, :, lanes] = total[at : at + 4]
                at = OWN + 4 * c
                row_out[c, :, lanes] = value[at : at + 4]
                corner_out[c, :, lanes] = value[OWN + 12 + c : OWN + 13 + c]
                col_out[c, :, lanes] = value[at + 16 : at + 20]

    forces(
        lambda lanes: current[:, lanes],
        operator_ref, back_ref, table_ref, tback_ref, material_ref, both, strain, spectrum, emit,
    )


def middle_kernel(rows_ref, out_ref):
    for c in range(3):
        for i in range(4):
            at = 16 * c + 4 * i
            out_ref[c, i] = rows_ref[at : at + 4]


def last_kernel(sum_ref, col_ref, corner_ref, row_ref, out_ref):
    first = lax.broadcasted_iota(jnp.int32, (4, 1), 0) == 0
    for c in range(3):
        for i in range(4):
            arrived = col_ref[c, i : i + 1].astype(F32)
            if i == 0:
                arrived = arrived + corner_ref[c].astype(F32)
            value = sum_ref[c, i] + jnp.where(first, arrived, 0.0)
            if i == 0:
                value = value + row_ref[c].astype(F32)
            out_ref[c, i] = value


def call(kernel, outs, scratch=(), scalars=0, inputs=0, flops=0, far=0, vmem=VMEM_LIMIT):
    near = pl.BlockSpec(memory_space=pltpu.VMEM)
    return pl.pallas_call(
        kernel,
        out_shape=outs,
        in_specs=[pl.BlockSpec(memory_space=pltpu.HBM)] * far
        + [pl.BlockSpec(memory_space=pltpu.SMEM)] * scalars
        + [near] * inputs,
        out_specs=jax.tree.map(lambda _: near, outs),
        scratch_shapes=list(scratch),
        compiler_params=pltpu.CompilerParams(vmem_limit_bytes=vmem),
        cost_estimate=pl.CostEstimate(flops=flops, bytes_accessed=1 << 20, transcendentals=0),
    )


def shape(*dims, dtype=F32):
    return jax.ShapeDtypeStruct(dims, dtype)


def solution(mesh):
    bands, layers = mesh.shape["colat"], mesh.shape["depth"]
    packed, starts = packed_constants()
    table, tback = sample_tables()

    def target(c, d, by_c, by_d):
        past = not 0 <= d + by_d < layers
        return (c + by_c + past * (bands // 2)) % bands * layers + (d + by_d) % layers

    def shifted(array, by_c, by_d):
        pairs = [(c * layers + d, target(c, d, by_c, by_d)) for c in range(bands) for d in range(layers)]
        return lax.ppermute(array, ("colat", "depth"), pairs)

    def swapped(array, axis, odd):
        along_c = axis == "colat"
        pairs = []
        for c in range(bands):
            for d in range(layers):
                step = 1 if (c if along_c else d) % 2 == odd else -1
                to_c, to_d = c + step * along_c, d + step * (not along_c)
                if not 0 <= to_c < bands:
                    to_c, to_d = c, d ^ 1
                if not 0 <= to_d < layers:
                    to_c, to_d = c ^ 1, d
                pairs.append((c * layers + d, to_c * layers + to_d))
        return lax.ppermute(array, ("colat", "depth"), pairs)

    def per_device(displacement, previous, node_blocks, inverse_mass, jac_diag, jac_off, inv_radius, lame_l, lame_m):
        at_c, at_d = lax.axis_index("colat"), lax.axis_index("depth")
        lane = lax.broadcasted_iota(jnp.int32, (8, LANES), 1)
        place = jnp.zeros((8, LANES), F32)
        has_side_c = jnp.where(at_c % 2 == 1, at_c < bands - 1, at_c > 0)
        has_side_d = jnp.where(at_d % 2 == 1, at_d < layers - 1, at_d > 0)
        flags = (at_c < bands - 1, at_d < layers - 1, at_c % 2, at_d % 2, has_side_c, has_side_d)
        for at, value in enumerate(flags):
            place = jnp.where(lane == at, value.astype(F32), place)
        row_face = shape(3, 4, WIDTH + LANES, dtype=BF16)
        point = shape(3, 1, WIDTH + LANES, dtype=BF16)
        row, col, corner = call(
            first_kernel,
            (row_face, row_face, point),
            [
                pltpu.SMEM((4, 4), jnp.int32),
                pltpu.SMEM((4, 4), F32),
                pltpu.VMEM((3, 4, 4, WIDTH), F32),
                pltpu.SemaphoreType.DMA((3,)),
            ],
            far=3, flops=2 * 10**10, vmem=62 * 1024 * 1024,
        )(node_blocks, inverse_mass, displacement)
        col = shifted(col, 0, -1)
        corner = shifted(corner, -1, -1)
        row = shifted(row, -1, 0)

        own, free, info = call(
            own_kernel,
            (shape(OWN, WIDTH), shape(OWN, WIDTH), shape(OWN + 8, LANES)),
            inputs=5, flops=10**8, vmem=8 * 1024 * 1024,
        )(place, node_blocks, inverse_mass, displacement, previous)
        operator, back, material, outgoing, column, arrival = call(
            functools.partial(prepare_kernel, starts),
            (
                shape(STRAINS, 2 * NODES, dtype=BF16),
                shape(2 * NODES, STRAINS, dtype=BF16),
                shape(RADIX, 56, LANES),
                shape(64, NODES, dtype=BF16),
                shape(32, 64, dtype=BF16),
                shape(NODES, 64, dtype=BF16),
            ),
            [pltpu.VMEM((2, 400, LANES), F32)],
            inputs=7, flops=10**9, vmem=8 * 1024 * 1024,
        )(
            place,
            jac_diag.reshape(10, 1, 5), jac_off.reshape(10, 1, 5), inv_radius.reshape(5, 1, 5),
            lame_l.reshape(400, LANES), lame_m.reshape(400, LANES), jnp.asarray(packed),
        )

        work = [
            pltpu.VMEM((2 * NODES, WIDTH), BF16),
            pltpu.VMEM((STRAINS, WIDTH), F32),
            pltpu.VMEM((RADIX, STRAINS, 2 * LANES), F32),
        ]
        tile = shape(16, WIDTH, dtype=BF16)
        shared = (operator, back, jnp.asarray(table), jnp.asarray(tback), material)
        total, pair, side, faces = call(
            step_one_kernel,
            (shape(NODES, WIDTH + LANES), tile, tile, shape(32, WIDTH, dtype=BF16)),
            [pltpu.VMEM((32, WIDTH + LANES), F32)] + work,
            inputs=12, flops=10**9,
        )(own, free, info, col, corner, row, *shared, outgoing)
        cside = swapped(side, "colat", 1)
        cpair = swapped(pair, "colat", 0)
        side, pair = call(column_kernel, (tile, tile), inputs=4)(faces, cside, cpair, column)
        dside = swapped(side, "depth", 1)
        dpair = swapped(pair, "depth", 0)
        row_face = shape(3, 4, WIDTH, dtype=BF16)
        middle, final, row, col, corner = call(
            step_two_kernel,
            (
                shape(OWN, WIDTH), shape(3, 4, 4, WIDTH), row_face, row_face,
                shape(3, 1, WIDTH, dtype=BF16),
            ),
            [pltpu.VMEM((NODES, WIDTH), F32)] + work,
            inputs=12, flops=10**9,
        )(own, total, cside, cpair, dside, dpair, *shared, arrival)
        col = shifted(col, 0, 1)
        corner = shifted(corner, 1, 1)
        row = shifted(row, 1, 0)
        middle = call(middle_kernel, shape(3, 4, 4, WIDTH), inputs=1, flops=2 * 10**10, vmem=4 * 1024 * 1024)(middle)
        final = call(last_kernel, shape(3, 4, 4, WIDTH), inputs=4)(final, col, corner, row)
        return middle, final

    return jax.shard_map(
        per_device,
        mesh=mesh,
        in_specs=(
            P(None, "colat", "depth", None),
            P(None, "colat", "depth", None),
            P("colat", "depth"),
            P("colat", "depth"),
            P(None, "colat", None, "depth", None),
            P(None, "colat", None, "depth", None),
            P("colat", None, "depth", None),
            P("colat", None, "depth", None, None),
            P("colat", None, "depth", None, None),
        ),
        out_specs=(P(None, "colat", "depth", None), P(None, "colat", "depth", None)),
        check_vma=False,
    )
```

```python
import functools
import math

import jax
import jax.numpy as jnp
import ml_dtypes
import numpy as np
from jax import lax
from jax.experimental import pallas as pl
from jax.experimental.pallas import tpu as pltpu
from jax.sharding import PartitionSpec as P

BF16 = jnp.bfloat16
F32 = jnp.float32
WIDTH = 2048
LANES = 128
RADIX = 16
OWN = 48
NODES = 80
STRAINS = 152
VMEM_LIMIT = 40 * 1024 * 1024


def gll_derivative():
    points = np.array([-1.0, -math.sqrt(3.0 / 7.0), 0.0, math.sqrt(3.0 / 7.0), 1.0])
    weights = np.ones(5)
    for row in range(5):
        for col in range(5):
            if row != col:
                weights[row] /= points[row] - points[col]
    matrix = np.zeros((5, 5))
    for row in range(5):
        for col in range(5):
            if row != col:
                matrix[row, col] = weights[col] / weights[row] / (points[row] - points[col])
        matrix[row, row] = -np.sum(matrix[row])
    return matrix


def node_row(comp, i, j):
    if i == 4:
        return OWN + (12 + comp if j == 4 else 4 * comp + j)
    if j == 4:
        return OWN + 16 + 4 * comp + i
    return 16 * comp + 4 * i + j


def strain_row(strain, node):
    return 24 * strain + node if node < 24 else 144 + strain


def strain_terms():
    deriv = gll_derivative()
    parts = np.zeros((5, STRAINS, 2 * NODES))
    place_of = np.zeros((2, STRAINS, 5))
    half = math.sqrt(0.5)
    for i in range(5):
        for j in range(5):
            node = 5 * i + j

            def grad(strain, along_z, comp, scale):
                row = strain_row(strain, node)
                for other in range(5):
                    xi, eta = (2, 3) if along_z else (0, 1)
                    parts[xi, row, node_row(comp, other, j)] += scale * deriv[i, other]
                    parts[eta, row, node_row(comp, i, other)] += scale * deriv[j, other]

            def radial(strain, comp, azimuthal, scale):
                row = strain_row(strain, node)
                parts[4, row, NODES * azimuthal + node_row(comp, i, j)] += scale / 1024.0

            grad(0, False, 0, 1.0)
            grad(1, True, 2, 1.0)
            radial(2, 1, 1, 1.0)
            radial(2, 0, 0, 1.0)
            grad(3, True, 0, half)
            grad(3, False, 2, half)
            radial(4, 0, 1, half)
            radial(4, 1, 0, -half)
            grad(4, False, 1, half)
            radial(5, 2, 1, half)
            grad(5, True, 1, half)
            for strain in range(6):
                place_of[0, strain_row(strain, node), i] = 1.0
                place_of[1, strain_row(strain, node), j] = 1.0
    parts[:, 150] = parts[:, 144] + parts[:, 145] + parts[:, 146]
    place_of[:, 150, 4] = 1.0
    return parts.astype(np.float32), place_of.astype(np.float32)


def sample_tables():
    order = np.arange(LANES)[:, None]
    table = np.zeros((RADIX, 2 * LANES, LANES))
    for k0 in range(RADIX):
        angle = 2.0 * math.pi * (order * (16 * np.arange(LANES)[None, :] + k0) % WIDTH) / WIDTH
        table[k0, :LANES] = np.cos(angle)
        table[k0, LANES:] = -np.sin(angle)
    return (
        table.astype(ml_dtypes.bfloat16),
        np.ascontiguousarray(table.transpose(0, 2, 1)).astype(ml_dtypes.bfloat16),
    )


def lane_shuffle():
    shuffle = np.zeros((LANES, LANES))
    for t in range(8):
        for k0 in range(16):
            shuffle[16 * t + k0, 8 * k0 + t] = 1.0
    return shuffle.astype(ml_dtypes.bfloat16)


def face(fixed_i, fixed_j):
    return [(fixed_i, n) if fixed_j is None else (n, fixed_j) for n in range(5)]


def message_row(comp, n):
    return 12 + comp if n == 4 else 4 * comp + n


def pick(faces):
    select = np.zeros((16 * len(faces), NODES))
    for index, nodes in enumerate(faces):
        for comp in range(3):
            for n, (i, j) in enumerate(nodes):
                select[16 * index + message_row(comp, n), node_row(comp, i, j)] = 1.0
    return select


ROW_LOW, ROW_HIGH = face(0, None), face(4, None)
COL_LOW, COL_HIGH = face(None, 0), face(None, 4)


def outgoing_select():
    even = pick([ROW_HIGH, ROW_LOW, COL_HIGH, COL_LOW])
    odd = pick([ROW_LOW, ROW_HIGH, COL_HIGH, COL_LOW])
    return np.stack([even, odd]).astype(ml_dtypes.bfloat16)


def column_select():
    out = np.zeros((4, 32, 64))
    for par_c in range(2):
        faces = [ROW_HIGH, ROW_LOW] if par_c == 0 else [ROW_LOW, ROW_HIGH]
        arrive = pick(faces).T
        full = np.concatenate([pick([COL_HIGH]), pick([COL_LOW])], axis=0)
        whole = np.concatenate([np.eye(32), full @ arrive], axis=1)
        for par_d in range(2):
            out[2 * par_c + par_d] = whole if par_d == 0 else np.roll(whole, 16, axis=0)
    return out.astype(ml_dtypes.bfloat16)


def arrival_select():
    out = np.zeros((4, NODES, 64))
    for par_c in range(2):
        rows = [ROW_HIGH, ROW_LOW] if par_c == 0 else [ROW_LOW, ROW_HIGH]
        for par_d in range(2):
            cols = [COL_HIGH, COL_LOW] if par_d == 0 else [COL_LOW, COL_HIGH]
            out[2 * par_c + par_d] = pick(rows + cols).T
    return out.astype(ml_dtypes.bfloat16)


def turned(value, eighths, scale_sign):
    re, im = value
    eighths = (scale_sign * eighths) % 16
    if eighths == 0:
        return re, im
    if eighths == 4:
        return -im, re
    if eighths == 8:
        return -re, -im
    if eighths == 12:
        return im, -re
    root = math.sqrt(0.5)
    if eighths == 2:
        return (re - im) * root, (im + re) * root
    if eighths == 14:
        return (re + im) * root, (im - re) * root
    cosine = math.cos(2.0 * math.pi * eighths / 16)
    sine = math.sin(2.0 * math.pi * eighths / 16)
    return re * cosine - im * sine, im * cosine + re * sine


def add(left, right):
    return left[0] + right[0], left[1] + right[1]


def sub(left, right):
    return left[0] - right[0], left[1] - right[1]


def transform(values, sign):
    count = len(values)
    if count == 1:
        return values
    even = transform(values[0::2], sign)
    odd = transform(values[1::2], sign)
    odd = [turned(value, q * (16 // count), sign) for q, value in enumerate(odd)]
    return [add(a, b) for a, b in zip(even, odd)] + [sub(a, b) for a, b in zip(even, odd)]


def spread(blocks):
    even = transform(blocks, 1)
    odd = transform([turned(value, b, 1) for b, value in enumerate(blocks)], 1)
    return [value for pair in zip(even, odd) for value in pair]


def gathered(values):
    even = transform(values[0::2], -1)
    odd = transform(values[1::2], -1)
    return [add(a, turned(b, index, -1)) for index, (a, b) in enumerate(zip(even, odd))]


def block(index, part):
    return slice(2 * LANES * index + LANES * part, 2 * LANES * index + LANES * (part + 1))


def orders(index):
    lane = lax.broadcasted_iota(jnp.int32, (1, LANES), 1)
    return (lane + LANES * index).astype(F32)


def dot(left, right):
    return jnp.dot(left, right, preferred_element_type=F32)


def node_column(scalar, rows):
    row = lax.broadcasted_iota(jnp.int32, (len(rows), 1), 0)
    column = jnp.zeros((len(rows), 1), F32)
    for value in sorted(set(rows)):
        chosen = functools.reduce(jnp.logical_or, [row == at for at, held in enumerate(rows) if held == value])
        column = jnp.where(chosen, scalar(value), column)
    return column


def own_rows(ref, lanes):
    return jnp.concatenate([ref[c, i, :, lanes] for c in range(3) for i in range(4)], axis=0)


def first_kernel(blocks_hbm, mass_hbm, disp_hbm, row_out, col_out, corner_out, blocks_ref, mass_ref, disp_ref, sems):
    loads = [
        pltpu.make_async_copy(source, target, sems.at[n])
        for n, (source, target) in enumerate(
            ((blocks_hbm, blocks_ref), (mass_hbm, mass_ref), (disp_hbm, disp_ref))
        )
    ]
    for load in loads:
        load.start()
    faces = (
        (row_out, [(0, n) for n in range(4)]),
        (col_out, [(n, 0) for n in range(4)]),
        (corner_out, [(0, 0)]),
    )
    loads[0].wait()
    loads[1].wait()
    columns = []
    for out, rows in faces:
        live = node_column(lambda at: blocks_ref[at[0], at[1]].astype(F32), rows)
        mass = node_column(lambda at: mass_ref[at[0], at[1]], rows)
        high = mass.astype(BF16).astype(F32)
        lane = lax.broadcasted_iota(jnp.int32, (len(rows), LANES), 1)
        info = jnp.where(lane == 0, high, jnp.where(lane == 1, mass - high, jnp.where(lane == 2, live, 0.0)))
        for c in range(3):
            out[c, :, WIDTH:] = info.astype(BF16)
        columns.append(live)
    loads[2].wait()
    for (out, rows), live in zip(faces, columns):
        for index in range(8):
            lanes = slice(256 * index, 256 * (index + 1))
            kept = live > index
            for c in range(3):
                if out is row_out:
                    value = disp_ref[c, 0, :, lanes]
                elif out is col_out:
                    value = jnp.concatenate([disp_ref[c, n, 0:1, lanes] for n in range(4)], axis=0)
                else:
                    value = disp_ref[c, 0, 0:1, lanes]
                out[c, :, lanes] = jnp.where(kept, value, 0.0).astype(BF16)


def own_kernel(place_ref, blocks_ref, mass_ref, disp_ref, prev_ref, own_out, free_out, info_out):
    def column(ref):
        shape = (4, 4)
        diagonal = lax.broadcasted_iota(jnp.int32, shape, 0) == lax.broadcasted_iota(jnp.int32, shape, 1)
        value = ref[...].astype(F32)
        pieces = [jnp.sum(jnp.where(diagonal, value[i : i + 1], 0.0), axis=1, keepdims=True) for i in range(4)]
        return jnp.concatenate(pieces * 3, axis=0)

    live, mass = column(blocks_ref), column(mass_ref)
    lane = lax.broadcasted_iota(jnp.int32, (OWN, LANES), 1)
    info_out[:OWN] = jnp.where(lane == 0, mass, jnp.where(lane == 1, live, 0.0))
    info_out[OWN:] = place_ref[...]
    for index in range(8):
        lanes = slice(256 * index, 256 * (index + 1))
        value = jnp.where(live > index, own_rows(disp_ref, lanes), 0.0)
        own_out[:, lanes] = value
        free_out[:, lanes] = jnp.where(live > index, 2.0 * value - own_rows(prev_ref, lanes), 0.0)


def exact_dot(left, right):
    return jnp.dot(left, right, preferred_element_type=F32, precision=lax.Precision.HIGHEST)


def packed_constants():
    parts, place_of = strain_terms()
    upper = np.zeros((3, STRAINS, 2 * LANES), np.float32)
    for term in range(4):
        upper[term // 2, :, NODES * (term % 2) : NODES * (term % 2 + 1)] = parts[term, :, :NODES]
    upper[2, :, : 2 * NODES] = parts[4]
    columns = (
        {"arrival": arrival_select(), "outgoing": outgoing_select()},
        {"shuffle": lane_shuffle()[None], "place": place_of, "column": column_select()},
    )
    lower, starts = np.zeros((3 * STRAINS + 560, 2 * LANES), np.float32), {}
    lower[: 3 * STRAINS] = upper.reshape(-1, 2 * LANES)
    for side, pieces in enumerate(columns):
        first = 3 * STRAINS
        for name, piece in pieces.items():
            starts[name] = (first, LANES * side)
            for matrix in np.asarray(piece, np.float32):
                rows, width = matrix.shape
                lower[first : first + rows, LANES * side : LANES * side + width] = matrix
                first += rows
    return lower, starts


def prepare_kernel(
    starts, place_ref, diag_ref, off_ref, radius_ref, lambda_ref, mu_ref, packed_ref,
    operator_out, back_out, material_out, outgoing_out, column_out, arrival_out,
    shuffled,
):
    def constant(name, rows, columns, index=0):
        first, lane = starts[name]
        return packed_ref[first + rows * index : first + rows * (index + 1), lane : lane + columns]

    at_i, at_j = constant("place", STRAINS, 5), constant("place", STRAINS, 5, 1)
    factors = []
    for ref, row in ((diag_ref, 0), (off_ref, 0), (off_ref, 5), (diag_ref, 5), (radius_ref, 0)):
        factor = jnp.concatenate([ref[row + i] for i in range(5)], axis=0)
        spread_i = exact_dot(at_i, factor) * at_j
        factors.append(jnp.sum(spread_i, axis=1, keepdims=True))
    parts = [packed_ref[STRAINS * n : STRAINS * (n + 1)] for n in range(3)]
    operator = parts[2][:, : 2 * NODES] * factors[4]
    plain = sum(parts[t // 2][:, NODES * (t % 2) : NODES * (t % 2 + 1)] * factors[t] for t in range(4))
    operator = operator + jnp.concatenate([plain, jnp.zeros_like(plain)], axis=1)
    operator_out[...] = operator.astype(BF16)
    back_out[...] = operator.T.astype(BF16)

    def packed(name, rows, columns, *bits):
        pieces = [constant(name, rows, columns, index) for index in range(2 ** len(bits))]
        for bit in reversed(bits):
            pieces = [jnp.where(bit > 0.5, one, zero) for zero, one in zip(pieces[0::2], pieces[1::2])]
        return pieces[0]

    def kept(matrix, first, flag):
        column = lax.broadcasted_iota(jnp.int32, matrix.shape, 1)
        dropped = jnp.logical_and(jnp.logical_and(column >= first, column < first + 16), flag < 0.5)
        return jnp.where(dropped, 0.0, matrix)

    odd_c, odd_d, side_c, side_d = (place_ref[0:1, n : n + 1] for n in range(2, 6))
    outgoing_out[...] = packed("outgoing", 64, NODES, odd_c).astype(BF16)
    column_out[...] = kept(packed("column", 32, 64, odd_c, odd_d), 48, side_c).astype(BF16)
    arrived = kept(packed("arrival", NODES, 64, odd_c, odd_d), 16, side_c)
    arrival_out[...] = kept(arrived, 48, side_d).astype(BF16)
    shuffle = constant("shuffle", LANES, LANES).astype(BF16)

    for which, (ref, factor) in enumerate(((lambda_ref, 1.0), (mu_ref, 2.0))):
        value = ref[...] * factor
        high = value.astype(BF16)
        low = (value - high.astype(F32)).astype(BF16)
        shuffled[which] = dot(high, shuffle) + dot(low, shuffle)
    group = lax.broadcasted_iota(jnp.int32, (8, LANES), 1) // 8
    row = lax.broadcasted_iota(jnp.int32, (8, LANES), 0)
    for rows in range(7):
        held = []
        for s in range(16):
            if rows < 6:
                value = shuffled[rows // 3, pl.ds(128 * (rows % 3) + s, 8, stride=16), :]
            else:
                at = slice(384 + s, 385 + s)
                value = jnp.where(row < 6, shuffled[1, at], jnp.where(row == 6, shuffled[0, at], 0.0))
            held.append(value if s == 0 else pltpu.roll(value, 8 * s, 1))
        held = [held[(16 - index) % 16] for index in range(16)]
        for bit in range(4):
            chosen = (group >> bit) % 2 == 1
            held = [jnp.where(chosen, held[(index - (1 << bit)) % 16], held[index]) for index in range(16)]
        for index in range(16):
            value = held[index] if index == 0 else pltpu.roll(held[index], LANES - 8 * index, 1)
            material_out[index, 8 * rows : 8 * rows + 8] = value


def forces(nodes, operator_ref, back_ref, table_ref, tback_ref, material_ref, both, strain, spectrum, emit):
    for index in range(8):
        order = orders(index)
        re = nodes(block(index, 0))
        im = nodes(block(index, 1))
        both[:NODES, block(index, 0)] = re.astype(BF16)
        both[:NODES, block(index, 1)] = im.astype(BF16)
        both[NODES:, block(index, 0)] = (im * (-order)).astype(BF16)
        both[NODES:, block(index, 1)] = (re * order).astype(BF16)
        lanes = slice(256 * index, 256 * (index + 1))
        strain[:, lanes] = dot(operator_ref[...], both[:, lanes])

    for group in range(STRAINS // 8):
        rows = slice(8 * group, 8 * group + 8)
        values = [(strain[rows, block(b, 0)], strain[rows, block(b, 1)]) for b in range(8)]
        for k0, (re, im) in enumerate(spread(values)):
            spectrum[k0, rows, :LANES] = re
            spectrum[k0, rows, LANES:] = im

    for k0 in range(RADIX):
        sample = dot(spectrum[k0].astype(BF16), table_ref[k0])
        lam, mu, last = material_ref[k0, :24], material_ref[k0, 24:48], material_ref[k0, 48:]
        parts = [sample[24 * s : 24 * s + 24] for s in range(6)]
        volume = lam * (parts[0] + parts[1] + parts[2])
        stress = [volume + mu * part for part in parts[:3]] + [mu * part for part in parts[3:]]
        stress.append(last * sample[144:])
        stress = jnp.concatenate(stress, axis=0).astype(BF16)
        spectrum[k0] = dot(stress, tback_ref[k0])

    for group in range(STRAINS // 8):
        rows = slice(8 * group, 8 * group + 8)
        values = [(spectrum[k0, rows, :LANES], spectrum[k0, rows, LANES:]) for k0 in range(RADIX)]
        for b, (re, im) in enumerate(gathered(values)):
            strain[rows, block(b, 0)] = re
            strain[rows, block(b, 1)] = im

    for index in range(8):
        lanes = slice(256 * index, 256 * (index + 1))
        order = orders(index)
        pulled = dot(back_ref[...], strain[:, lanes].astype(BF16))
        re = pulled[:NODES, :LANES] + order * pulled[NODES:, LANES:]
        im = pulled[:NODES, LANES:] - order * pulled[NODES:, :LANES]
        emit(index, re, im)


def step_one_kernel(
    own_ref, free_ref, info_ref, col_ref, corner_ref, row_ref,
    operator_ref, back_ref, table_ref, tback_ref, material_ref, select_ref,
    sum_ref, pair_ref, side_ref, faces_ref,
    tiles, both, strain, spectrum,
):
    rest_c, rest_d = info_ref[OWN : OWN + 1, 0:1], info_ref[OWN : OWN + 1, 1:2]
    for lanes in [slice(256 * n, 256 * (n + 1)) for n in range(8)] + [slice(WIDTH, WIDTH + LANES)]:
        rows = [row_ref[c, :, lanes].astype(F32) * rest_c for c in range(3)]
        corner = [corner_ref[c, :, lanes].astype(F32) * (rest_c * rest_d) for c in range(3)]
        cols = [col_ref[c, :, lanes].astype(F32) * rest_d for c in range(3)]
        width = lanes.stop - lanes.start
        pieces = rows + corner + [jnp.zeros((1, width), F32)] + cols + [jnp.zeros((4, width), F32)]
        tiles[:, lanes] = jnp.concatenate(pieces, axis=0)
    info = tiles[:, WIDTH:]
    lane = lax.broadcasted_iota(jnp.int32, (32, LANES), 1)
    sum_ref[:OWN, WIDTH:] = info_ref[:OWN]
    sum_ref[OWN:, WIDTH:] = jnp.where(
        lane == 0, info[:, 0:1] + info[:, 1:2], jnp.where(lane == 1, info[:, 2:3], 0.0)
    )
    mass = sum_ref[:, WIDTH : WIDTH + 1] * (-1.0 / WIDTH)

    def nodes(lanes):
        return jnp.concatenate([own_ref[:, lanes], tiles[:, lanes]], axis=0)

    def emit(index, re, im):
        for part, value in ((0, re), (1, im)):
            lanes = block(index, part)
            value = mass * value
            sum_ref[:OWN, lanes] = free_ref[:, lanes] + value[:OWN]
            sum_ref[OWN:, lanes] = value[OWN:]

    forces(nodes, operator_ref, back_ref, table_ref, tback_ref, material_ref, both, strain, spectrum, emit)

    for index in range(8):
        lanes = slice(256 * index, 256 * (index + 1))
        sent = dot(select_ref[...], sum_ref[:, lanes].astype(BF16)).astype(BF16)
        pair_ref[:, lanes] = sent[:16]
        side_ref[:, lanes] = sent[16:32]
        faces_ref[:, lanes] = sent[32:]


def column_kernel(faces_ref, side_ref, pair_ref, select_ref, side_out, pair_out):
    for index in range(8):
        lanes = slice(256 * index, 256 * (index + 1))
        stacked = jnp.concatenate([faces_ref[:, lanes], pair_ref[:, lanes], side_ref[:, lanes]], axis=0)
        sent = dot(select_ref[...], stacked).astype(BF16)
        pair_out[:, lanes] = sent[:16]
        side_out[:, lanes] = sent[16:]


def step_two_kernel(
    own_ref, sum_ref, cside_ref, cpair_ref, dside_ref, dpair_ref,
    operator_ref, back_ref, table_ref, tback_ref, material_ref, select_ref,
    mid_ref, sum_out, row_out, col_out, corner_out,
    current, both, strain, spectrum,
):
    live = sum_ref[:, WIDTH + 1 : WIDTH + 2]
    for index in range(8):
        lanes = slice(256 * index, 256 * (index + 1))
        arrived = jnp.concatenate([ref[:, lanes] for ref in (cpair_ref, cside_ref, dpair_ref, dside_ref)], axis=0)
        value = jnp.where(live > index, sum_ref[:, lanes] + dot(select_ref[...], arrived), 0.0)
        current[:, lanes] = value
        mid_ref[:, lanes] = value[:OWN]
    mass = sum_ref[:, WIDTH : WIDTH + 1] * (-1.0 / WIDTH)

    def emit(index, re, im):
        masked = jnp.where(live > index, mass, 0.0)
        for part, value in ((0, re), (1, im)):
            lanes = block(index, part)
            value = masked * value
            total = 2.0 * current[:OWN, lanes] - own_ref[:, lanes] + value[:OWN]
            value = value.astype(BF16)
            for c in range(3):
                for i in range(4):
                    at = 16 * c + 4 * i
                    sum_out[c, i, :, lanes] = total[at : at + 4]
                at = OWN + 4 * c
                row_out[c, :, lanes] = value[at : at + 4]
                corner_out[c, :, lanes] = value[OWN + 12 + c : OWN + 13 + c]
                col_out[c, :, lanes] = value[at + 16 : at + 20]

    forces(
        lambda lanes: current[:, lanes],
        operator_ref, back_ref, table_ref, tback_ref, material_ref, both, strain, spectrum, emit,
    )


def middle_kernel(rows_ref, out_ref):
    for c in range(3):
        for i in range(4):
            at = 16 * c + 4 * i
            out_ref[c, i] = rows_ref[at : at + 4]


def last_kernel(sum_ref, col_ref, corner_ref, row_ref, out_hbm, out_ref, sems):
    first = lax.broadcasted_iota(jnp.int32, (4, 1), 0) == 0
    stores = [pltpu.make_async_copy(out_ref.at[c], out_hbm.at[c], sems.at[c]) for c in range(3)]
    for c in range(3):
        for i in range(4):
            arrived = col_ref[c, i : i + 1].astype(F32)
            if i == 0:
                arrived = arrived + corner_ref[c].astype(F32)
            value = sum_ref[c, i] + jnp.where(first, arrived, 0.0)
            if i == 0:
                value = value + row_ref[c].astype(F32)
            out_ref[c, i] = value
        stores[c].start()
    for store in stores:
        store.wait()


def call(kernel, outs, scratch=(), scalars=0, inputs=0, flops=0, far=0, vmem=VMEM_LIMIT, outside=False):
    near = pl.BlockSpec(memory_space=pltpu.VMEM)
    return pl.pallas_call(
        kernel,
        out_shape=outs,
        in_specs=[pl.BlockSpec(memory_space=pltpu.HBM)] * far
        + [pl.BlockSpec(memory_space=pltpu.SMEM)] * scalars
        + [near] * inputs,
        out_specs=jax.tree.map(lambda _: pl.BlockSpec(memory_space=pltpu.HBM) if outside else near, outs),
        scratch_shapes=list(scratch),
        compiler_params=pltpu.CompilerParams(vmem_limit_bytes=vmem),
        cost_estimate=pl.CostEstimate(flops=flops, bytes_accessed=1 << 20, transcendentals=0),
    )


def shape(*dims, dtype=F32):
    return jax.ShapeDtypeStruct(dims, dtype)


def solution(mesh):
    bands, layers = mesh.shape["colat"], mesh.shape["depth"]
    packed, starts = packed_constants()
    table, tback = sample_tables()

    def target(c, d, by_c, by_d):
        past = not 0 <= d + by_d < layers
        return (c + by_c + past * (bands // 2)) % bands * layers + (d + by_d) % layers

    def shifted(array, by_c, by_d):
        pairs = [(c * layers + d, target(c, d, by_c, by_d)) for c in range(bands) for d in range(layers)]
        return lax.ppermute(array, ("colat", "depth"), pairs)

    def swapped(array, axis, odd):
        along_c = axis == "colat"
        pairs = []
        for c in range(bands):
            for d in range(layers):
                step = 1 if (c if along_c else d) % 2 == odd else -1
                to_c, to_d = c + step * along_c, d + step * (not along_c)
                if not 0 <= to_c < bands:
                    to_c, to_d = c, d ^ 1
                if not 0 <= to_d < layers:
                    to_c, to_d = c ^ 1, d
                pairs.append((c * layers + d, to_c * layers + to_d))
        return lax.ppermute(array, ("colat", "depth"), pairs)

    def per_device(displacement, previous, node_blocks, inverse_mass, jac_diag, jac_off, inv_radius, lame_l, lame_m):
        at_c, at_d = lax.axis_index("colat"), lax.axis_index("depth")
        lane = lax.broadcasted_iota(jnp.int32, (8, LANES), 1)
        place = jnp.zeros((8, LANES), F32)
        has_side_c = jnp.where(at_c % 2 == 1, at_c < bands - 1, at_c > 0)
        has_side_d = jnp.where(at_d % 2 == 1, at_d < layers - 1, at_d > 0)
        flags = (at_c < bands - 1, at_d < layers - 1, at_c % 2, at_d % 2, has_side_c, has_side_d)
        for at, value in enumerate(flags):
            place = jnp.where(lane == at, value.astype(F32), place)
        row_face = shape(3, 4, WIDTH + LANES, dtype=BF16)
        point = shape(3, 1, WIDTH + LANES, dtype=BF16)
        row, col, corner = call(
            first_kernel,
            (row_face, row_face, point),
            [
                pltpu.SMEM((4, 4), jnp.int32),
                pltpu.SMEM((4, 4), F32),
                pltpu.VMEM((3, 4, 4, WIDTH), F32),
                pltpu.SemaphoreType.DMA((3,)),
            ],
            far=3, flops=2 * 10**10, vmem=62 * 1024 * 1024,
        )(node_blocks, inverse_mass, displacement)
        col = shifted(col, 0, -1)
        corner = shifted(corner, -1, -1)
        row = shifted(row, -1, 0)

        own, free, info = call(
            own_kernel,
            (shape(OWN, WIDTH), shape(OWN, WIDTH), shape(OWN + 8, LANES)),
            inputs=5, flops=2 * 10**10, vmem=8 * 1024 * 1024,
        )(place, node_blocks, inverse_mass, displacement, previous)
        operator, back, material, outgoing, column, arrival = call(
            functools.partial(prepare_kernel, starts),
            (
                shape(STRAINS, 2 * NODES, dtype=BF16),
                shape(2 * NODES, STRAINS, dtype=BF16),
                shape(RADIX, 56, LANES),
                shape(64, NODES, dtype=BF16),
                shape(32, 64, dtype=BF16),
                shape(NODES, 64, dtype=BF16),
            ),
            [pltpu.VMEM((2, 400, LANES), F32)],
            inputs=7, flops=10**9, vmem=8 * 1024 * 1024,
        )(
            place,
            jac_diag.reshape(10, 1, 5), jac_off.reshape(10, 1, 5), inv_radius.reshape(5, 1, 5),
            lame_l.reshape(400, LANES), lame_m.reshape(400, LANES), jnp.asarray(packed),
        )

        work = [
            pltpu.VMEM((2 * NODES, WIDTH), BF16),
            pltpu.VMEM((STRAINS, WIDTH), F32),
            pltpu.VMEM((RADIX, STRAINS, 2 * LANES), F32),
        ]
        tile = shape(16, WIDTH, dtype=BF16)
        shared = (operator, back, jnp.asarray(table), jnp.asarray(tback), material)
        total, pair, side, faces = call(
            step_one_kernel,
            (shape(NODES, WIDTH + LANES), tile, tile, shape(32, WIDTH, dtype=BF16)),
            [pltpu.VMEM((32, WIDTH + LANES), F32)] + work,
            inputs=12, flops=10**9,
        )(own, free, info, col, corner, row, *shared, outgoing)
        cside = swapped(side, "colat", 1)
        cpair = swapped(pair, "colat", 0)
        side, pair = call(column_kernel, (tile, tile), inputs=4)(faces, cside, cpair, column)
        dside = swapped(side, "depth", 1)
        dpair = swapped(pair, "depth", 0)
        row_face = shape(3, 4, WIDTH, dtype=BF16)
        middle, final, row, col, corner = call(
            step_two_kernel,
            (
                shape(OWN, WIDTH), shape(3, 4, 4, WIDTH), row_face, row_face,
                shape(3, 1, WIDTH, dtype=BF16),
            ),
            [pltpu.VMEM((NODES, WIDTH), F32)] + work,
            inputs=12, flops=10**9,
        )(own, total, cside, cpair, dside, dpair, *shared, arrival)
        col = shifted(col, 0, 1)
        corner = shifted(corner, 1, 1)
        row = shifted(row, 1, 0)
        middle = call(middle_kernel, shape(3, 4, 4, WIDTH), inputs=1, flops=2 * 10**10, vmem=4 * 1024 * 1024)(middle)
        final = call(
            last_kernel,
            shape(3, 4, 4, WIDTH),
            [pltpu.VMEM((3, 4, 4, WIDTH), F32), pltpu.SemaphoreType.DMA((3,))],
            inputs=4, outside=True,
        )(final, col, corner, row)
        return middle, final

    return jax.shard_map(
        per_device,
        mesh=mesh,
        in_specs=(
            P(None, "colat", "depth", None),
            P(None, "colat", "depth", None),
            P("colat", "depth"),
            P("colat", "depth"),
            P(None, "colat", None, "depth", None),
            P(None, "colat", None, "depth", None),
            P("colat", None, "depth", None),
            P("colat", None, "depth", None, None),
            P("colat", None, "depth", None, None),
        ),
        out_specs=(P(None, "colat", "depth", None), P(None, "colat", "depth", None)),
        check_vma=False,
    )
```

```python
import functools
import math

import jax
import jax.numpy as jnp
import ml_dtypes
import numpy as np
from jax import lax
from jax.experimental import pallas as pl
from jax.experimental.pallas import tpu as pltpu
from jax.sharding import PartitionSpec as P

BF16 = jnp.bfloat16
F32 = jnp.float32
WIDTH = 2048
LANES = 128
RADIX = 16
OWN = 48
NODES = 80
STRAINS = 152
VMEM_LIMIT = 40 * 1024 * 1024


def gll_derivative():
    points = np.array([-1.0, -math.sqrt(3.0 / 7.0), 0.0, math.sqrt(3.0 / 7.0), 1.0])
    weights = np.ones(5)
    for row in range(5):
        for col in range(5):
            if row != col:
                weights[row] /= points[row] - points[col]
    matrix = np.zeros((5, 5))
    for row in range(5):
        for col in range(5):
            if row != col:
                matrix[row, col] = weights[col] / weights[row] / (points[row] - points[col])
        matrix[row, row] = -np.sum(matrix[row])
    return matrix


def node_row(comp, i, j):
    if i == 4:
        return OWN + (12 + comp if j == 4 else 4 * comp + j)
    if j == 4:
        return OWN + 16 + 4 * comp + i
    return 16 * comp + 4 * i + j


def strain_row(strain, node):
    return 24 * strain + node if node < 24 else 144 + strain


def strain_terms():
    deriv = gll_derivative()
    parts = np.zeros((5, STRAINS, 2 * NODES))
    place_of = np.zeros((2, STRAINS, 5))
    half = math.sqrt(0.5)
    for i in range(5):
        for j in range(5):
            node = 5 * i + j

            def grad(strain, along_z, comp, scale):
                row = strain_row(strain, node)
                for other in range(5):
                    xi, eta = (2, 3) if along_z else (0, 1)
                    parts[xi, row, node_row(comp, other, j)] += scale * deriv[i, other]
                    parts[eta, row, node_row(comp, i, other)] += scale * deriv[j, other]

            def radial(strain, comp, azimuthal, scale):
                row = strain_row(strain, node)
                parts[4, row, NODES * azimuthal + node_row(comp, i, j)] += scale / 1024.0

            grad(0, False, 0, 1.0)
            grad(1, True, 2, 1.0)
            radial(2, 1, 1, 1.0)
            radial(2, 0, 0, 1.0)
            grad(3, True, 0, half)
            grad(3, False, 2, half)
            radial(4, 0, 1, half)
            radial(4, 1, 0, -half)
            grad(4, False, 1, half)
            radial(5, 2, 1, half)
            grad(5, True, 1, half)
            for strain in range(6):
                place_of[0, strain_row(strain, node), i] = 1.0
                place_of[1, strain_row(strain, node), j] = 1.0
    parts[:, 150] = parts[:, 144] + parts[:, 145] + parts[:, 146]
    place_of[:, 150, 4] = 1.0
    return parts.astype(np.float32), place_of.astype(np.float32)


def sample_tables():
    order = np.arange(LANES)[:, None]
    table = np.zeros((RADIX, 2 * LANES, LANES))
    for k0 in range(RADIX):
        angle = 2.0 * math.pi * (order * (16 * np.arange(LANES)[None, :] + k0) % WIDTH) / WIDTH
        table[k0, :LANES] = np.cos(angle)
        table[k0, LANES:] = -np.sin(angle)
    return (
        table.astype(ml_dtypes.bfloat16),
        np.ascontiguousarray(table.transpose(0, 2, 1)).astype(ml_dtypes.bfloat16),
    )


def lane_shuffle():
    shuffle = np.zeros((LANES, LANES))
    for t in range(8):
        for k0 in range(16):
            shuffle[16 * t + k0, 8 * k0 + t] = 1.0
    return shuffle.astype(ml_dtypes.bfloat16)


def face(fixed_i, fixed_j):
    return [(fixed_i, n) if fixed_j is None else (n, fixed_j) for n in range(5)]


def message_row(comp, n):
    return 12 + comp if n == 4 else 4 * comp + n


def pick(faces):
    select = np.zeros((16 * len(faces), NODES))
    for index, nodes in enumerate(faces):
        for comp in range(3):
            for n, (i, j) in enumerate(nodes):
                select[16 * index + message_row(comp, n), node_row(comp, i, j)] = 1.0
    return select


ROW_LOW, ROW_HIGH = face(0, None), face(4, None)
COL_LOW, COL_HIGH = face(None, 0), face(None, 4)


def outgoing_select():
    even = pick([ROW_HIGH, ROW_LOW, COL_HIGH, COL_LOW])
    odd = pick([ROW_LOW, ROW_HIGH, COL_HIGH, COL_LOW])
    return np.stack([even, odd]).astype(ml_dtypes.bfloat16)


def column_select():
    out = np.zeros((4, 32, 64))
    for par_c in range(2):
        faces = [ROW_HIGH, ROW_LOW] if par_c == 0 else [ROW_LOW, ROW_HIGH]
        arrive = pick(faces).T
        full = np.concatenate([pick([COL_HIGH]), pick([COL_LOW])], axis=0)
        whole = np.concatenate([np.eye(32), full @ arrive], axis=1)
        for par_d in range(2):
            out[2 * par_c + par_d] = whole if par_d == 0 else np.roll(whole, 16, axis=0)
    return out.astype(ml_dtypes.bfloat16)


def arrival_select():
    out = np.zeros((4, NODES, 64))
    for par_c in range(2):
        rows = [ROW_HIGH, ROW_LOW] if par_c == 0 else [ROW_LOW, ROW_HIGH]
        for par_d in range(2):
            cols = [COL_HIGH, COL_LOW] if par_d == 0 else [COL_LOW, COL_HIGH]
            out[2 * par_c + par_d] = pick(rows + cols).T
    return out.astype(ml_dtypes.bfloat16)


def turned(value, eighths, scale_sign):
    re, im = value
    eighths = (scale_sign * eighths) % 16
    if eighths == 0:
        return re, im
    if eighths == 4:
        return -im, re
    if eighths == 8:
        return -re, -im
    if eighths == 12:
        return im, -re
    root = math.sqrt(0.5)
    if eighths == 2:
        return (re - im) * root, (im + re) * root
    if eighths == 14:
        return (re + im) * root, (im - re) * root
    cosine = math.cos(2.0 * math.pi * eighths / 16)
    sine = math.sin(2.0 * math.pi * eighths / 16)
    return re * cosine - im * sine, im * cosine + re * sine


def add(left, right):
    return left[0] + right[0], left[1] + right[1]


def sub(left, right):
    return left[0] - right[0], left[1] - right[1]


def transform(values, sign):
    count = len(values)
    if count == 1:
        return values
    even = transform(values[0::2], sign)
    odd = transform(values[1::2], sign)
    odd = [turned(value, q * (16 // count), sign) for q, value in enumerate(odd)]
    return [add(a, b) for a, b in zip(even, odd)] + [sub(a, b) for a, b in zip(even, odd)]


def spread(blocks):
    even = transform(blocks, 1)
    odd = transform([turned(value, b, 1) for b, value in enumerate(blocks)], 1)
    return [value for pair in zip(even, odd) for value in pair]


def gathered(values):
    even = transform(values[0::2], -1)
    odd = transform(values[1::2], -1)
    return [add(a, turned(b, index, -1)) for index, (a, b) in enumerate(zip(even, odd))]


def block(index, part):
    return slice(2 * LANES * index + LANES * part, 2 * LANES * index + LANES * (part + 1))


def orders(index):
    lane = lax.broadcasted_iota(jnp.int32, (1, LANES), 1)
    return (lane + LANES * index).astype(F32)


def dot(left, right):
    return jnp.dot(left, right, preferred_element_type=F32)


def node_column(scalar, rows):
    row = lax.broadcasted_iota(jnp.int32, (len(rows), 1), 0)
    column = jnp.zeros((len(rows), 1), F32)
    for value in sorted(set(rows)):
        chosen = functools.reduce(jnp.logical_or, [row == at for at, held in enumerate(rows) if held == value])
        column = jnp.where(chosen, scalar(value), column)
    return column


def own_rows(ref, lanes):
    return jnp.concatenate([ref[c, i, :, lanes] for c in range(3) for i in range(4)], axis=0)


def first_kernel(blocks_hbm, mass_hbm, disp_hbm, row_out, col_out, corner_out, blocks_ref, mass_ref, disp_ref, sems):
    loads = [
        pltpu.make_async_copy(source, target, sems.at[n])
        for n, (source, target) in enumerate(
            ((blocks_hbm, blocks_ref), (mass_hbm, mass_ref), (disp_hbm, disp_ref))
        )
    ]
    for load in loads:
        load.start()
    faces = (
        (row_out, [(0, n) for n in range(4)]),
        (col_out, [(n, 0) for n in range(4)]),
        (corner_out, [(0, 0)]),
    )
    loads[0].wait()
    loads[1].wait()
    columns = []
    for out, rows in faces:
        live = node_column(lambda at: blocks_ref[at[0], at[1]].astype(F32), rows)
        mass = node_column(lambda at: mass_ref[at[0], at[1]], rows)
        high = mass.astype(BF16).astype(F32)
        lane = lax.broadcasted_iota(jnp.int32, (len(rows), LANES), 1)
        info = jnp.where(lane == 0, high, jnp.where(lane == 1, mass - high, jnp.where(lane == 2, live, 0.0)))
        for c in range(3):
            out[c, :, WIDTH:] = info.astype(BF16)
        columns.append(live)
    loads[2].wait()
    for (out, rows), live in zip(faces, columns):
        for index in range(8):
            lanes = slice(256 * index, 256 * (index + 1))
            kept = live > index
            for c in range(3):
                if out is row_out:
                    value = disp_ref[c, 0, :, lanes]
                elif out is col_out:
                    value = jnp.concatenate([disp_ref[c, n, 0:1, lanes] for n in range(4)], axis=0)
                else:
                    value = disp_ref[c, 0, 0:1, lanes]
                out[c, :, lanes] = jnp.where(kept, value, 0.0).astype(BF16)


def own_kernel(place_ref, blocks_ref, mass_ref, disp_ref, prev_ref, own_out, free_out, info_out):
    def column(ref):
        shape = (4, 4)
        diagonal = lax.broadcasted_iota(jnp.int32, shape, 0) == lax.broadcasted_iota(jnp.int32, shape, 1)
        value = ref[...].astype(F32)
        pieces = [jnp.sum(jnp.where(diagonal, value[i : i + 1], 0.0), axis=1, keepdims=True) for i in range(4)]
        return jnp.concatenate(pieces * 3, axis=0)

    live, mass = column(blocks_ref), column(mass_ref)
    lane = lax.broadcasted_iota(jnp.int32, (OWN, LANES), 1)
    info_out[:OWN] = jnp.where(lane == 0, mass, jnp.where(lane == 1, live, 0.0))
    info_out[OWN:] = place_ref[...]
    for index in range(8):
        lanes = slice(256 * index, 256 * (index + 1))
        value = jnp.where(live > index, own_rows(disp_ref, lanes), 0.0)
        own_out[:, lanes] = value
        free_out[:, lanes] = jnp.where(live > index, 2.0 * value - own_rows(prev_ref, lanes), 0.0)


def exact_dot(left, right):
    return jnp.dot(left, right, preferred_element_type=F32, precision=lax.Precision.HIGHEST)


def packed_constants():
    parts, place_of = strain_terms()
    upper = np.zeros((3, STRAINS, 2 * LANES), np.float32)
    for term in range(4):
        upper[term // 2, :, NODES * (term % 2) : NODES * (term % 2 + 1)] = parts[term, :, :NODES]
    upper[2, :, : 2 * NODES] = parts[4]
    columns = (
        {"arrival": arrival_select(), "outgoing": outgoing_select()},
        {"shuffle": lane_shuffle()[None], "place": place_of, "column": column_select()},
    )
    lower, starts = np.zeros((3 * STRAINS + 560, 2 * LANES), np.float32), {}
    lower[: 3 * STRAINS] = upper.reshape(-1, 2 * LANES)
    for side, pieces in enumerate(columns):
        first = 3 * STRAINS
        for name, piece in pieces.items():
            starts[name] = (first, LANES * side)
            for matrix in np.asarray(piece, np.float32):
                rows, width = matrix.shape
                lower[first : first + rows, LANES * side : LANES * side + width] = matrix
                first += rows
    return lower, starts


def prepare_kernel(
    starts, place_ref, diag_ref, off_ref, radius_ref, lambda_ref, mu_ref, packed_ref,
    operator_out, back_out, material_out, outgoing_out, column_out, arrival_out,
    shuffled,
):
    def constant(name, rows, columns, index=0):
        first, lane = starts[name]
        return packed_ref[first + rows * index : first + rows * (index + 1), lane : lane + columns]

    at_i, at_j = constant("place", STRAINS, 5), constant("place", STRAINS, 5, 1)
    factors = []
    for ref, row in ((diag_ref, 0), (off_ref, 0), (off_ref, 5), (diag_ref, 5), (radius_ref, 0)):
        factor = jnp.concatenate([ref[row + i] for i in range(5)], axis=0)
        spread_i = exact_dot(at_i, factor) * at_j
        factors.append(jnp.sum(spread_i, axis=1, keepdims=True))
    parts = [packed_ref[STRAINS * n : STRAINS * (n + 1)] for n in range(3)]
    operator = parts[2][:, : 2 * NODES] * factors[4]
    plain = sum(parts[t // 2][:, NODES * (t % 2) : NODES * (t % 2 + 1)] * factors[t] for t in range(4))
    operator = operator + jnp.concatenate([plain, jnp.zeros_like(plain)], axis=1)
    operator_out[...] = operator.astype(BF16)
    back_out[...] = operator.T.astype(BF16)

    def packed(name, rows, columns, *bits):
        pieces = [constant(name, rows, columns, index) for index in range(2 ** len(bits))]
        for bit in reversed(bits):
            pieces = [jnp.where(bit > 0.5, one, zero) for zero, one in zip(pieces[0::2], pieces[1::2])]
        return pieces[0]

    def kept(matrix, first, flag):
        column = lax.broadcasted_iota(jnp.int32, matrix.shape, 1)
        dropped = jnp.logical_and(jnp.logical_and(column >= first, column < first + 16), flag < 0.5)
        return jnp.where(dropped, 0.0, matrix)

    odd_c, odd_d, side_c, side_d = (place_ref[0:1, n : n + 1] for n in range(2, 6))
    outgoing_out[...] = packed("outgoing", 64, NODES, odd_c).astype(BF16)
    column_out[...] = kept(packed("column", 32, 64, odd_c, odd_d), 48, side_c).astype(BF16)
    arrived = kept(packed("arrival", NODES, 64, odd_c, odd_d), 16, side_c)
    arrival_out[...] = kept(arrived, 48, side_d).astype(BF16)
    shuffle = constant("shuffle", LANES, LANES).astype(BF16)

    for which, (ref, factor) in enumerate(((lambda_ref, 1.0), (mu_ref, 2.0))):
        value = ref[...] * factor
        high = value.astype(BF16)
        low = (value - high.astype(F32)).astype(BF16)
        shuffled[which] = dot(high, shuffle) + dot(low, shuffle)
    group = lax.broadcasted_iota(jnp.int32, (8, LANES), 1) // 8
    row = lax.broadcasted_iota(jnp.int32, (8, LANES), 0)
    for rows in range(7):
        held = []
        for s in range(16):
            if rows < 6:
                value = shuffled[rows // 3, pl.ds(128 * (rows % 3) + s, 8, stride=16), :]
            else:
                at = slice(384 + s, 385 + s)
                value = jnp.where(row < 6, shuffled[1, at], jnp.where(row == 6, shuffled[0, at], 0.0))
            held.append(value if s == 0 else pltpu.roll(value, 8 * s, 1))
        held = [held[(16 - index) % 16] for index in range(16)]
        for bit in range(4):
            chosen = (group >> bit) % 2 == 1
            held = [jnp.where(chosen, held[(index - (1 << bit)) % 16], held[index]) for index in range(16)]
        for index in range(16):
            value = held[index] if index == 0 else pltpu.roll(held[index], LANES - 8 * index, 1)
            material_out[index, 8 * rows : 8 * rows + 8] = value


def forces(nodes, operator_ref, back_ref, table_ref, tback_ref, material_ref, both, strain, spectrum, emit):
    for index in range(8):
        order = orders(index)
        re = nodes(block(index, 0))
        im = nodes(block(index, 1))
        both[:NODES, block(index, 0)] = re.astype(BF16)
        both[:NODES, block(index, 1)] = im.astype(BF16)
        both[NODES:, block(index, 0)] = (im * (-order)).astype(BF16)
        both[NODES:, block(index, 1)] = (re * order).astype(BF16)
        lanes = slice(256 * index, 256 * (index + 1))
        strain[:, lanes] = dot(operator_ref[...], both[:, lanes])

    for group in range(STRAINS // 8):
        rows = slice(8 * group, 8 * group + 8)
        values = [(strain[rows, block(b, 0)], strain[rows, block(b, 1)]) for b in range(8)]
        for k0, (re, im) in enumerate(spread(values)):
            spectrum[k0, rows, :LANES] = re
            spectrum[k0, rows, LANES:] = im

    for k0 in range(RADIX):
        sample = dot(spectrum[k0].astype(BF16), table_ref[k0])
        lam, mu, last = material_ref[k0, :24], material_ref[k0, 24:48], material_ref[k0, 48:]
        parts = [sample[24 * s : 24 * s + 24] for s in range(6)]
        volume = lam * (parts[0] + parts[1] + parts[2])
        stress = [volume + mu * part for part in parts[:3]] + [mu * part for part in parts[3:]]
        stress.append(last * sample[144:])
        stress = jnp.concatenate(stress, axis=0).astype(BF16)
        spectrum[k0] = dot(stress, tback_ref[k0])

    for group in range(STRAINS // 8):
        rows = slice(8 * group, 8 * group + 8)
        values = [(spectrum[k0, rows, :LANES], spectrum[k0, rows, LANES:]) for k0 in range(RADIX)]
        for b, (re, im) in enumerate(gathered(values)):
            strain[rows, block(b, 0)] = re
            strain[rows, block(b, 1)] = im

    for index in range(8):
        lanes = slice(256 * index, 256 * (index + 1))
        order = orders(index)
        pulled = dot(back_ref[...], strain[:, lanes].astype(BF16))
        re = pulled[:NODES, :LANES] + order * pulled[NODES:, LANES:]
        im = pulled[:NODES, LANES:] - order * pulled[NODES:, :LANES]
        emit(index, re, im)


def step_one_kernel(
    own_ref, free_ref, info_ref, row_ref, col_ref, corner_ref,
    operator_ref, back_ref, table_ref, tback_ref, material_ref, select_ref,
    sum_ref, pair_ref, side_ref, faces_ref,
    tiles, both, strain, spectrum,
):
    rest_c, rest_d = info_ref[OWN : OWN + 1, 0:1], info_ref[OWN : OWN + 1, 1:2]
    for lanes in [slice(256 * n, 256 * (n + 1)) for n in range(8)] + [slice(WIDTH, WIDTH + LANES)]:
        rows = [row_ref[c, :, lanes].astype(F32) * rest_c for c in range(3)]
        corner = [corner_ref[c, :, lanes].astype(F32) * (rest_c * rest_d) for c in range(3)]
        cols = [col_ref[c, :, lanes].astype(F32) * rest_d for c in range(3)]
        width = lanes.stop - lanes.start
        pieces = rows + corner + [jnp.zeros((1, width), F32)] + cols + [jnp.zeros((4, width), F32)]
        tiles[:, lanes] = jnp.concatenate(pieces, axis=0)
    info = tiles[:, WIDTH:]
    lane = lax.broadcasted_iota(jnp.int32, (32, LANES), 1)
    sum_ref[:OWN, WIDTH:] = info_ref[:OWN]
    sum_ref[OWN:, WIDTH:] = jnp.where(
        lane == 0, info[:, 0:1] + info[:, 1:2], jnp.where(lane == 1, info[:, 2:3], 0.0)
    )
    mass = sum_ref[:, WIDTH : WIDTH + 1] * (-1.0 / WIDTH)

    def nodes(lanes):
        return jnp.concatenate([own_ref[:, lanes], tiles[:, lanes]], axis=0)

    def emit(index, re, im):
        for part, value in ((0, re), (1, im)):
            lanes = block(index, part)
            value = mass * value
            sum_ref[:OWN, lanes] = free_ref[:, lanes] + value[:OWN]
            sum_ref[OWN:, lanes] = value[OWN:]

    forces(nodes, operator_ref, back_ref, table_ref, tback_ref, material_ref, both, strain, spectrum, emit)

    for index in range(8):
        lanes = slice(256 * index, 256 * (index + 1))
        sent = dot(select_ref[...], sum_ref[:, lanes].astype(BF16)).astype(BF16)
        pair_ref[:, lanes] = sent[:16]
        side_ref[:, lanes] = sent[16:32]
        faces_ref[:, lanes] = sent[32:]


def column_kernel(faces_ref, side_ref, pair_ref, select_ref, side_out, pair_out):
    for index in range(8):
        lanes = slice(256 * index, 256 * (index + 1))
        stacked = jnp.concatenate([faces_ref[:, lanes], pair_ref[:, lanes], side_ref[:, lanes]], axis=0)
        sent = dot(select_ref[...], stacked).astype(BF16)
        pair_out[:, lanes] = sent[:16]
        side_out[:, lanes] = sent[16:]


def step_two_kernel(
    own_ref, sum_ref, cside_ref, cpair_ref, dside_ref, dpair_ref,
    operator_ref, back_ref, table_ref, tback_ref, material_ref, select_ref,
    mid_ref, sum_out, row_out, col_out, corner_out,
    current, both, strain, spectrum,
):
    live = sum_ref[:, WIDTH + 1 : WIDTH + 2]
    for index in range(8):
        lanes = slice(256 * index, 256 * (index + 1))
        arrived = jnp.concatenate([ref[:, lanes] for ref in (cpair_ref, cside_ref, dpair_ref, dside_ref)], axis=0)
        value = jnp.where(live > index, sum_ref[:, lanes] + dot(select_ref[...], arrived), 0.0)
        current[:, lanes] = value
        mid_ref[:, lanes] = value[:OWN]
    mass = sum_ref[:, WIDTH : WIDTH + 1] * (-1.0 / WIDTH)

    def emit(index, re, im):
        masked = jnp.where(live > index, mass, 0.0)
        for part, value in ((0, re), (1, im)):
            lanes = block(index, part)
            value = masked * value
            total = 2.0 * current[:OWN, lanes] - own_ref[:, lanes] + value[:OWN]
            value = value.astype(BF16)
            for c in range(3):
                for i in range(4):
                    at = 16 * c + 4 * i
                    sum_out[c, i, :, lanes] = total[at : at + 4]
                at = OWN + 4 * c
                row_out[c, :, lanes] = value[at : at + 4]
                corner_out[c, :, lanes] = value[OWN + 12 + c : OWN + 13 + c]
                col_out[c, :, lanes] = value[at + 16 : at + 20]

    forces(
        lambda lanes: current[:, lanes],
        operator_ref, back_ref, table_ref, tback_ref, material_ref, both, strain, spectrum, emit,
    )


def middle_kernel(rows_ref, out_ref):
    for c in range(3):
        for i in range(4):
            at = 16 * c + 4 * i
            out_ref[c, i] = rows_ref[at : at + 4]


def last_kernel(sum_ref, col_ref, corner_ref, row_ref, out_hbm, out_ref, sems):
    first = lax.broadcasted_iota(jnp.int32, (4, 1), 0) == 0
    stores = [pltpu.make_async_copy(out_ref.at[c], out_hbm.at[c], sems.at[c]) for c in range(3)]
    for c in range(3):
        for i in range(4):
            arrived = col_ref[c, i : i + 1].astype(F32)
            if i == 0:
                arrived = arrived + corner_ref[c].astype(F32)
            value = sum_ref[c, i] + jnp.where(first, arrived, 0.0)
            if i == 0:
                value = value + row_ref[c].astype(F32)
            out_ref[c, i] = value
        stores[c].start()
    for store in stores:
        store.wait()


def call(kernel, outs, scratch=(), scalars=0, inputs=0, flops=0, far=0, vmem=VMEM_LIMIT, outside=False):
    near = pl.BlockSpec(memory_space=pltpu.VMEM)
    return pl.pallas_call(
        kernel,
        out_shape=outs,
        in_specs=[pl.BlockSpec(memory_space=pltpu.HBM)] * far
        + [pl.BlockSpec(memory_space=pltpu.SMEM)] * scalars
        + [near] * inputs,
        out_specs=jax.tree.map(lambda _: pl.BlockSpec(memory_space=pltpu.HBM) if outside else near, outs),
        scratch_shapes=list(scratch),
        compiler_params=pltpu.CompilerParams(vmem_limit_bytes=vmem),
        cost_estimate=pl.CostEstimate(flops=flops, bytes_accessed=1 << 20, transcendentals=0),
    )


def shape(*dims, dtype=F32):
    return jax.ShapeDtypeStruct(dims, dtype)


def solution(mesh):
    bands, layers = mesh.shape["colat"], mesh.shape["depth"]
    packed, starts = packed_constants()
    table, tback = sample_tables()

    def target(c, d, by_c, by_d):
        past = not 0 <= d + by_d < layers
        return (c + by_c + past * (bands // 2)) % bands * layers + (d + by_d) % layers

    def shifted(array, by_c, by_d):
        pairs = [(c * layers + d, target(c, d, by_c, by_d)) for c in range(bands) for d in range(layers)]
        return lax.ppermute(array, ("colat", "depth"), pairs)

    def swapped(array, axis, odd):
        along_c = axis == "colat"
        pairs = []
        for c in range(bands):
            for d in range(layers):
                step = 1 if (c if along_c else d) % 2 == odd else -1
                to_c, to_d = c + step * along_c, d + step * (not along_c)
                if not 0 <= to_c < bands:
                    to_c, to_d = c, d ^ 1
                if not 0 <= to_d < layers:
                    to_c, to_d = c ^ 1, d
                pairs.append((c * layers + d, to_c * layers + to_d))
        return lax.ppermute(array, ("colat", "depth"), pairs)

    def per_device(displacement, previous, node_blocks, inverse_mass, jac_diag, jac_off, inv_radius, lame_l, lame_m):
        at_c, at_d = lax.axis_index("colat"), lax.axis_index("depth")
        lane = lax.broadcasted_iota(jnp.int32, (8, LANES), 1)
        place = jnp.zeros((8, LANES), F32)
        has_side_c = jnp.where(at_c % 2 == 1, at_c < bands - 1, at_c > 0)
        has_side_d = jnp.where(at_d % 2 == 1, at_d < layers - 1, at_d > 0)
        flags = (at_c < bands - 1, at_d < layers - 1, at_c % 2, at_d % 2, has_side_c, has_side_d)
        for at, value in enumerate(flags):
            place = jnp.where(lane == at, value.astype(F32), place)
        row_face = shape(3, 4, WIDTH + LANES, dtype=BF16)
        point = shape(3, 1, WIDTH + LANES, dtype=BF16)
        row, col, corner = call(
            first_kernel,
            (row_face, row_face, point),
            [
                pltpu.SMEM((4, 4), jnp.int32),
                pltpu.SMEM((4, 4), F32),
                pltpu.VMEM((3, 4, 4, WIDTH), F32),
                pltpu.SemaphoreType.DMA((3,)),
            ],
            far=3, flops=2 * 10**10, vmem=62 * 1024 * 1024,
        )(node_blocks, inverse_mass, displacement)
        col = shifted(col, 0, -1)
        corner = shifted(corner, -1, -1)
        row = shifted(row, -1, 0)

        own, free, info = call(
            own_kernel,
            (shape(OWN, WIDTH), shape(OWN, WIDTH), shape(OWN + 8, LANES)),
            inputs=5, flops=2 * 10**10, vmem=8 * 1024 * 1024,
        )(place, node_blocks, inverse_mass, displacement, previous)
        operator, back, material, outgoing, column, arrival = call(
            functools.partial(prepare_kernel, starts),
            (
                shape(STRAINS, 2 * NODES, dtype=BF16),
                shape(2 * NODES, STRAINS, dtype=BF16),
                shape(RADIX, 56, LANES),
                shape(64, NODES, dtype=BF16),
                shape(32, 64, dtype=BF16),
                shape(NODES, 64, dtype=BF16),
            ),
            [pltpu.VMEM((2, 400, LANES), F32)],
            inputs=7, flops=10**9, vmem=8 * 1024 * 1024,
        )(
            place,
            jac_diag.reshape(10, 1, 5), jac_off.reshape(10, 1, 5), inv_radius.reshape(5, 1, 5),
            lame_l.reshape(400, LANES), lame_m.reshape(400, LANES), jnp.asarray(packed),
        )

        work = [
            pltpu.VMEM((2 * NODES, WIDTH), BF16),
            pltpu.VMEM((STRAINS, WIDTH), F32),
            pltpu.VMEM((RADIX, STRAINS, 2 * LANES), F32),
        ]
        tile = shape(16, WIDTH, dtype=BF16)
        shared = (operator, back, jnp.asarray(table), jnp.asarray(tback), material)
        total, pair, side, faces = call(
            step_one_kernel,
            (shape(NODES, WIDTH + LANES), tile, tile, shape(32, WIDTH, dtype=BF16)),
            [pltpu.VMEM((32, WIDTH + LANES), F32)] + work,
            inputs=12, flops=10**9,
        )(own, free, info, row, col, corner, *shared, outgoing)
        cside = swapped(side, "colat", 1)
        cpair = swapped(pair, "colat", 0)
        side, pair = call(column_kernel, (tile, tile), inputs=4)(faces, cside, cpair, column)
        dside = swapped(side, "depth", 1)
        dpair = swapped(pair, "depth", 0)
        row_face = shape(3, 4, WIDTH, dtype=BF16)
        middle, final, row, col, corner = call(
            step_two_kernel,
            (
                shape(OWN, WIDTH), shape(3, 4, 4, WIDTH), row_face, row_face,
                shape(3, 1, WIDTH, dtype=BF16),
            ),
            [pltpu.VMEM((NODES, WIDTH), F32)] + work,
            inputs=12, flops=10**9,
        )(own, total, cside, cpair, dside, dpair, *shared, arrival)
        col = shifted(col, 0, 1)
        corner = shifted(corner, 1, 1)
        row = shifted(row, 1, 0)
        middle = call(middle_kernel, shape(3, 4, 4, WIDTH), inputs=1, flops=2 * 10**10, vmem=4 * 1024 * 1024)(middle)
        final = call(
            last_kernel,
            shape(3, 4, 4, WIDTH),
            [pltpu.VMEM((3, 4, 4, WIDTH), F32), pltpu.SemaphoreType.DMA((3,))],
            inputs=4, outside=True,
        )(final, col, corner, row)
        return middle, final

    return jax.shard_map(
        per_device,
        mesh=mesh,
        in_specs=(
            P(None, "colat", "depth", None),
            P(None, "colat", "depth", None),
            P("colat", "depth"),
            P("colat", "depth"),
            P(None, "colat", None, "depth", None),
            P(None, "colat", None, "depth", None),
            P("colat", None, "depth", None),
            P("colat", None, "depth", None, None),
            P("colat", None, "depth", None, None),
        ),
        out_specs=(P(None, "colat", "depth", None), P(None, "colat", "depth", None)),
        check_vma=False,
    )
```
